256 devices in a mesh: gx: 8 (over z), gy: 4 (over x), gz: 8 (over y, core).
Axes of the slice: x: 4, y: 4, z: 8, core: 2. Of those that a mesh axis runs over, the one named last changes fastest.
Arguments:
- source: float32 [128, 64, 1024], P('gz', 'gy', 'gx'), may hold values from -6 to 6
- fraction: float32 [128, 64, 1024], P('gz', 'gy', 'gx'), may hold values from 0.35 to 1
Outputs:
- pressure: float32 [128, 64, 1024], P('gz', 'gy', 'gx')
- residual: float32 [128, 64, 1024], P('gz', 'gy', 'gx')
The draws below stay inside these ranges and needn't reach their ends.
All inputs are finite; a program needn't handle non-finite values.
Results may differ from the reference program's by a relative error of at most 0.0003.
Values sent between devices are 32-bit elements; how exact they have to be, the bound alone decides.
No kernel may reach another device: no remote copies, remote signals or barrier semaphores. Data moves between devices by JAX's collectives and lax.ppermute only.
A program may use at most 128 MiB of HBM per device.

```python
import jax
import jax.numpy as jnp
from jax import lax

LEVELS = 5
NZ = 128
NY = 64
NX = 1024


def draw_source(key, part):
    key = jax.random.fold_in(key, 7)
    return jnp.clip(jax.random.normal(key, (NZ, NY, NX), jnp.float32), -6.0, 6.0)


def level_of(stream_key, dims, pieces, smallest, top_value):
    loudness, own = 1.0, jax.random.fold_in(stream_key, 6)
    for position, shards_of in pieces:
        draws = jnp.exp(jax.random.uniform(jax.random.fold_in(own, position), (shards_of,), jnp.float32, smallest / len(pieces), top_value / len(pieces)))
        loudness = loudness * jnp.repeat(draws, dims[position] // shards_of).reshape([-1 if axis == position else 1 for axis in range(len(dims))])
    return loudness


def setup_inputs(seed: int = 0) -> dict:
    seeds = jax.random.split(jax.random.key(seed), 3)
    return {
        "source": draw_source(jax.random.fold_in(seeds[2], 71), 0),
        "fraction": jnp.clip(0.35 + 0.65 * jax.random.uniform(seeds[1], (NZ, NY, NX), jnp.float32) ** level_of(seeds[1], (NZ, NY, NX), ((0, 8), (1, 4), (2, 8)), -0.2, 0.2), 0.35, 1.0),
    }


RELAXATION = 0.8

def coarsen(values):
    extent_z, extent_y, extent_x = values.shape
    return values.reshape(extent_z // 2, 2, extent_y // 2, 2, extent_x // 2, 2).mean(axis=(1, 3, 5))

def refine(values):
    return jnp.repeat(jnp.repeat(jnp.repeat(values, 2, axis=0), 2, axis=1), 2, axis=2)

def face_weights(padded, weight_scale):
    centre = padded[1:-1, 1:-1, 1:-1]
    below_z = weight_scale * 0.5 * (centre + padded[:-2, 1:-1, 1:-1])
    above_z = weight_scale * 0.5 * (centre + padded[2:, 1:-1, 1:-1])
    below_y = weight_scale * 0.5 * (centre + padded[1:-1, :-2, 1:-1])
    above_y = weight_scale * 0.5 * (centre + padded[1:-1, 2:, 1:-1])
    below_x = weight_scale * 0.5 * (centre + padded[1:-1, 1:-1, :-2])
    above_x = weight_scale * 0.5 * (centre + padded[1:-1, 1:-1, 2:])
    diagonal = below_z + above_z + below_y + above_y + below_x + above_x
    return (below_z, above_z, below_y, above_y, below_x, above_x, diagonal)

def operate(extended, weights):
    below_z, above_z, below_y, above_y, below_x, above_x, diagonal = weights
    neighbours = below_z * extended[:-2, 1:-1, 1:-1] + above_z * extended[2:, 1:-1, 1:-1]
    neighbours = neighbours + below_y * extended[1:-1, :-2, 1:-1] + above_y * extended[1:-1, 2:, 1:-1]
    neighbours = neighbours + below_x * extended[1:-1, 1:-1, :-2] + above_x * extended[1:-1, 1:-1, 2:]
    return diagonal * extended[1:-1, 1:-1, 1:-1] - neighbours

def apply_level(values, fraction_now, weight_scale):
    return operate(jnp.pad(values, 1), face_weights(jnp.pad(fraction_now, 1), weight_scale))

def sweep_once(values, source_now, fraction_now, weight_scale):
    diagonal = face_weights(jnp.pad(fraction_now, 1), weight_scale)[6]
    return values + RELAXATION * (source_now - apply_level(values, fraction_now, weight_scale)) / diagonal

def bottom_matrix(fraction_now, weight_scale, start, count):
    extent_z, extent_y, extent_x = fraction_now.shape
    order_size = extent_z * extent_y * extent_x
    plane_size = extent_y * extent_x
    flat_fraction = fraction_now.reshape(order_size)
    diagonal = face_weights(jnp.pad(fraction_now, 1), weight_scale)[6].reshape(order_size)
    row_index = jnp.arange(order_size, dtype=jnp.int32)[:, None]
    col_index = start + jnp.arange(count, dtype=jnp.int32)[None, :]
    apart = jnp.abs(row_index // plane_size - col_index // plane_size) + jnp.abs(row_index // extent_x % extent_y - col_index // extent_x % extent_y) + jnp.abs(row_index % extent_x - col_index % extent_x)
    col_fraction = lax.dynamic_slice_in_dim(flat_fraction, start, count)
    linked = -weight_scale * 0.5 * (flat_fraction[:, None] + col_fraction[None, :])
    return jnp.where(apart == 0, diagonal[:, None], jnp.where(apart == 1, linked, 0.0))

def reference(source, fraction):
    fractions = [fraction]
    for level_index in range(LEVELS):
        fractions.append(coarsen(fractions[-1]))
    sources = []
    pressures = []
    source_now = source
    for level_index in range(LEVELS):
        weight_scale = 0.25 ** level_index
        diagonal = face_weights(jnp.pad(fractions[level_index], 1), weight_scale)[6]
        pressure = RELAXATION * source_now / diagonal
        pressure = sweep_once(pressure, source_now, fractions[level_index], weight_scale)
        sources.append(source_now)
        pressures.append(pressure)
        source_now = coarsen(source_now - apply_level(pressure, fractions[level_index], weight_scale))
    bottom = fractions[LEVELS]
    matrix = bottom_matrix(bottom, 0.25 ** LEVELS, 0, bottom.size)
    factor = jnp.linalg.cholesky(matrix)
    pressure = jax.scipy.linalg.cho_solve((factor, True), source_now.reshape(bottom.size)).reshape(bottom.shape)
    for level_index in reversed(range(LEVELS)):
        weight_scale = 0.25 ** level_index
        pressure = pressures[level_index] + refine(pressure)
        pressure = sweep_once(pressure, sources[level_index], fractions[level_index], weight_scale)
        pressure = sweep_once(pressure, sources[level_index], fractions[level_index], weight_scale)
    return (pressure, source - apply_level(pressure, fraction, 1.0))
```

```python
import jax
import jax.numpy as jnp
from jax import lax
from jax.experimental import pallas as pl
from jax.experimental.pallas import tpu as pltpu
from jax.sharding import PartitionSpec as P

RELAXATION = 0.8
F32 = jnp.float32
VMEM_LIMIT = 56 * 1024 * 1024
CENTRE = (0, 0)
AROUND = tuple((oz, oy) for oz in (-1, 0, 1) for oy in (-1, 0, 1) if (oz, oy) != CENTRE)


def turn(v, shift, axis):
    size = v.shape[axis]
    shift = shift % size
    return v if shift == 0 else pltpu.roll(v, shift, axis)


def ahead(v, axis):
    return turn(v, -1, axis)


def behind(v, axis):
    return turn(v, 1, axis)


def index_of(shape, axis):
    return lax.broadcasted_iota(jnp.int32, shape, axis)


def matmul(a, b):
    return lax.dot_general(
        a, b, (((1,), (0,)), ((), ())), precision=lax.Precision.HIGHEST, preferred_element_type=F32
    )


def planes(lo, hi, body, unroll=2):
    trips = (hi - lo) // unroll
    if trips > 1:

        def step(i, carry):
            for k in range(unroll):
                body(lo + i * unroll + k)
            return carry

        lax.fori_loop(0, trips, step, 0)
    else:
        trips = 0
    for p in range(lo + trips * unroll, hi):
        body(p)


class Level:
    def __init__(self, refs):
        self.wx, self.wy, self.wz, self.diag, self.inv = refs

    def build(self, frac, scale, lo, hi, wraps, unroll=2):
        half = 0.5 * scale
        self.wz[lo - 1] = half * (frac[lo - 1] + frac[lo])

        def plane(p):
            c, up, down = frac[p], frac[p + 1], frac[p - 1]
            total = 6.0 * c + up + down
            for axis, keep in ((1, self.wx), (0, self.wy)):
                after, before = ahead(c, axis), behind(c, axis)
                weight = half * (c + after)
                if wraps[axis]:
                    at = index_of(c.shape, axis)
                    last = at == c.shape[axis] - 1
                    weight = jnp.where(last, 0.0, weight)
                    after = jnp.where(last, 0.0, after)
                    before = jnp.where(at == 0, 0.0, before)
                keep[p] = weight
                total = total + after + before
            self.wz[p] = half * (c + up)
            diag = half * total
            self.diag[p] = diag
            self.inv[p] = jnp.where(c > 0.0, RELAXATION / jnp.where(c > 0.0, diag, 1.0), 0.0)

        planes(lo, hi, plane, unroll)

    def apply(self, q, p):
        c, wx, wy = q[p], self.wx[p], self.wy[p]
        near = wx * ahead(c, 1) + behind(wx * c, 1) + wy * ahead(c, 0) + behind(wy * c, 0)
        near = near + self.wz[p] * q[p + 1] + self.wz[p - 1] * q[p - 1]
        return c, self.diag[p] * c - near

    def first(self, rhs, out, lo, hi, unroll=2):
        def plane(p):
            out[p] = self.inv[p] * rhs[p]

        planes(lo, hi, plane, unroll)

    def sweep(self, q, rhs, out, lo, hi, unroll=2):
        def plane(p):
            c, applied = self.apply(q, p)
            out[p] = c + self.inv[p] * (rhs[p] - applied)

        planes(lo, hi, plane, unroll)

    def halved_residual(self, q, rhs, out, lo, hi, unroll=1):
        def pair(j):
            _, one = self.apply(q, lo + 2 * j)
            _, two = self.apply(q, lo + 2 * j + 1)
            out[j] = (rhs[lo + 2 * j] - one) + (rhs[lo + 2 * j + 1] - two)

        planes(0, (hi - lo) // 2, pair, unroll)


def halved(values, out, lo, hi):
    def pair(j):
        out[j] = values[lo + 2 * j] + values[lo + 2 * j + 1]

    planes(0, (hi - lo) // 2, pair)


def rows_of(ref, count):
    _, rows, lanes = ref.shape
    return ref[0:count].reshape(count * rows, lanes)


def gather_pairs(lanes, out_lanes, first, place, count):
    at, to = index_of((lanes, out_lanes), 0), index_of((lanes, out_lanes), 1) - place
    pair = jnp.remainder(at - first, lanes)
    hit = (pair >= 2 * to) & (pair <= 2 * to + 1) & (to >= 0) & (to < count)
    return jnp.where(hit, 0.125, 0.0).astype(F32)


def spread_pairs(lanes, out_lanes, first, start, count):
    at, to = index_of((lanes, out_lanes), 0) - first, index_of((lanes, out_lanes), 1)
    pair = jnp.remainder(to - start, out_lanes)
    hit = (pair >= 2 * at) & (pair <= 2 * at + 1) & (at >= 0) & (at < count)
    return jnp.where(hit, 1.0, 0.0).astype(F32)


def pack_x_kernel(s, f, to_left, to_right):
    lane = index_of((16, 128), 1)
    for z in range(8):
        a, b, c, d = s[z], s[z + 8], f[z], f[z + 8]
        to_left[z] = jnp.where(
            lane < 32,
            a,
            jnp.where(lane < 64, turn(b, 32, 1), jnp.where(lane < 96, turn(c, 64, 1), turn(d, 96, 1))),
        )
        to_right[z] = jnp.where(
            lane >= 96,
            a,
            jnp.where(lane >= 64, turn(b, 96, 1), jnp.where(lane >= 32, turn(c, 64, 1), turn(d, 32, 1))),
        )


def z_range(oz, corner):
    depth = 5 if corner else 7
    return {-1: (16 - depth, 16), 0: (0, 16), 1: (0, depth)}[oz]


def y_range(oy):
    return {-1: (8, 16), 0: (0, 16), 1: (0, 8)}[oy]


def piece_shape(oz, oy):
    (za, zb), (ya, yb) = z_range(oz, oy != 0), y_range(oy)
    return (3, zb - za, yb - ya, 128)


def pack_yz_kernel(s, f, from_right, from_left, halo, *outs):
    ix = lax.axis_index("gx")
    left = jnp.where(ix > 0, 1.0, 0.0).astype(F32)
    right = jnp.where(ix < lax.axis_size("gx") - 1, 1.0, 0.0).astype(F32)
    lane = index_of((16, 128), 1)
    is_right = (lane < 32) | ((lane >= 64) & (lane < 96))
    for z in range(8):
        r, l = from_right[z] * right, from_left[z] * left
        halo[z] = jnp.where(is_right, r, l)
        halo[z + 8] = jnp.where(is_right, turn(r, 96, 1), turn(l, 32, 1))
    for (oz, oy), out in zip(AROUND, outs):
        (za, zb), (ya, yb) = z_range(oz, oy != 0), y_range(oy)
        for k, ref in enumerate((s, f, halo)):
            out[k] = ref[za:zb, ya:yb, :]


def down_kernel(s, f, halo, *refs):
    pieces, refs = refs[:8], refs[8:]
    S, D0, *w0 = refs[:7]
    own1, payload = refs[7:9]
    F, Q, T, U, V, f1, F1, q1, d1, *w1 = refs[9:]
    iz, iy = lax.axis_index("gz"), lax.axis_index("gy")
    nz, ny = lax.axis_size("gz"), lax.axis_size("gy")
    for p in (0, 1, 2, 29, 30, 31):
        S[p] = jnp.zeros((32, 256), F32)
        F[p] = jnp.zeros((32, 256), F32)

    def put(z0, y0, depth, height, inside, plane):
        edge = index_of((height, 128), 1)
        edge = (edge < 32) | (edge >= 96)

        def body(k):
            a, b, h = plane(k)
            if inside is not None:
                a, b, h = a * inside, b * inside, h * inside
            rows = pl.ds(y0, height)
            S[z0 + k, rows, 0:128] = a
            F[z0 + k, rows, 0:128] = b
            S[z0 + k, rows, 128:256] = jnp.where(edge, h, 0.0)
            F[z0 + k, rows, 128:256] = jnp.where(edge, turn(h, 64, 1), 0.0)

        planes(0, depth, body, 4)

    put(8, 8, 16, 16, None, lambda k: (s[k], f[k], halo[k]))
    for (oz, oy), piece in zip(AROUND, pieces):
        _, depth, height, _ = piece.shape
        okay = (iz + oz >= 0) & (iz + oz < nz) & (iy + oy >= 0) & (iy + oy < ny)
        z0 = {-1: 8 - depth, 0: 8, 1: 24}[oz]
        y0 = {-1: 0, 0: 8, 1: 24}[oy]
        inside = jnp.where(okay, 1.0, 0.0).astype(F32)
        put(z0, y0, depth, height, inside, lambda k, piece=piece: (piece[0, k], piece[1, k], piece[2, k]))

    level = Level(w0)
    level.build(F, 1.0, 2, 30, (False, False))
    level.first(S, Q, 2, 30)
    level.sweep(Q, S, D0, 3, 29)
    level.halved_residual(D0, S, T, 4, 28)
    C = gather_pairs(256, 128, 0, 0, 128)

    def coarse(count, out, start):
        U[0:count] = matmul(rows_of(T, count), C).reshape(count, 32, 128)
        for j in range(count):
            out[start + j] = U[j, pl.ds(0, 16, 2), :] + U[j, pl.ds(1, 16, 2), :]

    coarse(12, f1, 1)
    halved(F, T, 2, 30)
    coarse(14, F1, 0)
    for j in range(8):
        own1[0, j] = f1[3 + j, 4:12, :]
        own1[1, j] = F1[3 + j, 4:12, :]

    level = Level(w1)
    level.build(F1, 0.25, 1, 13, (False, False))
    level.first(f1, q1, 1, 13)
    level.sweep(q1, f1, d1, 2, 12)
    level.halved_residual(d1, f1, V, 3, 11)
    first = matmul(rows_of(V, 4), gather_pairs(128, 128, 112, 0, 48))
    halved(F1, V, 3, 11)
    both = first + matmul(rows_of(V, 4), gather_pairs(128, 128, 112, 64, 48))
    V[0:4] = both.reshape(4, 16, 128)
    for j in range(4):
        rows = V[j, pl.ds(4, 4, 2), :] + V[j, pl.ds(5, 4, 2), :]
        for d in range(32):
            payload[d, 4 * j : 4 * j + 4, :] = rows


def middle_kernel(got, own1, y_low, y_high, to_z, payload, f2, F2, d2, *refs):
    q2, T, U, *w2 = refs
    iy, ny = lax.axis_index("gy"), lax.axis_size("gy")
    low = jnp.where(iy > 0, 1.0, 0.0).astype(F32)
    high = jnp.where(iy < ny - 1, 1.0, 0.0).astype(F32)
    for k in range(2):
        for z in range(8):
            to_z[k, z, 0:8, :] = y_low[k, z] * low
            to_z[k, z, 8:16, :] = own1[k, z]
            to_z[k, z, 16:24, :] = y_high[k, z] * high
    keep = index_of((16, 128), 1) < 48
    zero = jnp.zeros((16, 128), F32)
    for ref in (f2, F2, q2, d2):
        ref[0] = zero
        ref[33] = zero
    for gy in range(4):
        for gz in range(8):
            block = got[gy * 8 + gz]
            rhs, frac = jnp.where(keep, block, 0.0), jnp.where(keep, turn(block, 64, 1), 0.0)
            for j in range(4):
                f2[1 + gz * 4 + j, 4 * gy : 4 * gy + 4, :] = rhs[4 * j : 4 * j + 4]
                F2[1 + gz * 4 + j, 4 * gy : 4 * gy + 4, :] = frac[4 * j : 4 * j + 4]
    level = Level(w2)
    level.build(F2, 0.25**2, 1, 33, (True, False), 4)
    level.first(f2, q2, 1, 33, 4)
    level.sweep(q2, f2, d2, 1, 33, 4)
    C = gather_pairs(128, 128, 8, 0, 16)
    for field in range(2):
        if field == 0:
            level.halved_residual(d2, f2, T, 1, 33, 2)
        else:
            halved(F2, T, 1, 33)
        U[...] = matmul(rows_of(T, 16), C).reshape(16, 16, 128)
        for zh in range(2):
            total = None
            for zl in range(8):
                z = zh * 8 + zl
                part = U[z, pl.ds(0, 8, 2), :] + U[z, pl.ds(1, 8, 2), :]
                part = turn(part, 16 * zl, 1)
                total = part if total is None else total + part
            for d in range(8):
                payload[d, 2 * field + zh] = total


def bottom(frac, rhs, half):
    shape = (8, 128)
    row, lane = index_of(shape, 0), index_of(shape, 1)
    used = lane < 32
    odd = jnp.remainder(row, 2) == 1
    y_near = jnp.where(odd, behind(frac, 0), ahead(frac, 0))
    z_up = jnp.where(row >= 6, 0.0, turn(frac, -2, 0))
    z_down = jnp.where(row < 2, 0.0, turn(frac, 2, 0))
    x_up = jnp.where(lane < 31, ahead(frac, 1), 0.0)
    x_down = jnp.where(lane > 0, behind(frac, 1), 0.0)
    diag = half * (6.0 * frac + y_near + z_up + z_down + x_up + x_down)
    after = jnp.where(lane < 31, -half * (frac + x_up), 0.0)
    before = jnp.where((lane > 0) & used, -half * (frac + x_down), 0.0)
    A, C, D, g = [], [], [], []
    for i in range(8):
        here = row == i
        z, y = i // 2, i % 2
        linked = (row == 2 * z + 1 - y) | (row == i - 2) | (row == i + 2)
        mine = jnp.broadcast_to(frac[i : i + 1], shape)
        block = jnp.where(here, diag, jnp.where(linked, -half * (mine + frac), 0.0))
        D.append(jnp.where(used, block, jnp.where(here, 1.0, 0.0)))
        A.append(jnp.where(here, before, 0.0))
        C.append(jnp.where(here, after, 0.0))
        g.append(jnp.broadcast_to(jnp.where(used[:1], rhs[i : i + 1], 0.0), shape))

    def pick(v, k):
        return jnp.broadcast_to(v[k : k + 1], shape)

    def divide(D, others):
        D, others = list(D), [list(o) for o in others]
        for k in range(8):
            inverse = 1.0 / pick(D[k], k)
            D[k] = D[k] * inverse
            for o in others:
                o[k] = o[k] * inverse
            for i in range(8):
                if i != k:
                    factor = pick(D[i], k)
                    D[i] = D[i] - factor * D[k]
                    for o in others:
                        o[i] = o[i] - factor * o[k]
        return others

    step = 1
    while step < 32:
        X, Y, h = divide(D, (A, C, g))
        Xl, Yl, hl = [[turn(v, step, 1) for v in o] for o in (X, Y, h)]
        Xr, Yr, hr = [[turn(v, -step, 1) for v in o] for o in (X, Y, h)]
        nA, nC, nD, ng = [], [], [], []
        for i in range(8):
            d, a, c, r = D[i], None, None, g[i]
            for k in range(8):
                pa, pc = pick(A[i], k), pick(C[i], k)
                d = d - (pa * Yl[k] + pc * Xr[k])
                r = r - (pa * hl[k] + pc * hr[k])
                a = -pa * Xl[k] if a is None else a - pa * Xl[k]
                c = -pc * Yr[k] if c is None else c - pc * Yr[k]
            nA.append(a)
            nC.append(c)
            nD.append(d)
            ng.append(r)
        A, C, D, g = nA, nC, nD, ng
        step *= 2
    (u,) = divide(D, (g,))
    out = jnp.zeros(shape, F32)
    for i in range(8):
        out = jnp.where((row == i) & used, u[i], out)
    return out


def up_kernel(got, to_z, z_low, z_high, f2, F2, d2, S, D0, wx0, wy0, wz0, g0, i0, pressure, residual, *refs):
    f3, F3, q3, d3, f4, F4, q4, d4 = refs[:8]
    w3, w4, w2, w1 = refs[8:13], refs[13:18], refs[18:23], refs[23:28]
    T3, g5, F5, qa2, qb2, T2, f1, F1, qa1, qb1, T1, U1, T0, U0, qa0, qb0 = refs[28:]
    iz, iy, ix = lax.axis_index("gz"), lax.axis_index("gy"), lax.axis_index("gx")
    nz = lax.axis_size("gz")
    lane = index_of((8, 128), 1)
    row = index_of((8, 128), 0)
    zero = jnp.zeros((8, 128), F32)

    for ref in (f3, F3, q3, d3):
        ref[0] = zero
        ref[17] = zero
    for ref in (f4, F4, q4, d4):
        ref[0] = zero
        ref[9] = zero
    for field, ref in enumerate((f3, F3)):
        for zh in range(2):
            blocks = [got[d, 2 * field + zh] for d in range(8)]
            for zl in range(8):
                total = turn(blocks[0], -16 * zl, 1)
                for d in range(1, 8):
                    total = jnp.where(lane >= 16 * d, turn(blocks[d], 16 * (d - zl), 1), total)
                ref[1 + zh * 8 + zl] = total

    three, four = Level(w3), Level(w4)
    three.build(F3, 0.25**3, 1, 17, (True, True), 16)
    three.first(f3, q3, 1, 17, 16)
    three.sweep(q3, f3, d3, 1, 17, 16)
    C = gather_pairs(128, 128, 0, 0, 64)
    for field in range(2):
        if field == 0:
            three.halved_residual(d3, f3, T3, 1, 17, 8)
        else:
            halved(F3, T3, 1, 17)
        T3[0:8] = matmul(rows_of(T3, 8), C).reshape(8, 8, 128)
        out = (f4, F4)[field]
        for j in range(8):
            out[1 + j] = zero
            out[1 + j, 0:4, :] = T3[j, pl.ds(0, 4, 2), :] + T3[j, pl.ds(1, 4, 2), :]
    four.build(F4, 0.25**4, 1, 9, (False, False), 8)
    four.first(f4, q4, 1, 9, 8)
    four.sweep(q4, f4, d4, 1, 9, 8)
    for field in range(2):
        if field == 0:
            four.halved_residual(d4, f4, T3, 1, 9, 4)
        else:
            halved(F4, T3, 1, 9)
        T3[0:4] = matmul(rows_of(T3, 4), C).reshape(4, 8, 128)
        out = (g5, F5)[field]
        for j in range(4):
            out[2 * j : 2 * j + 2, :] = T3[j, pl.ds(0, 2, 2), :] + T3[j, pl.ds(1, 2, 2), :]
    corr5 = bottom(F5[...], g5[...], 0.5 * 0.25**5)

    double = spread_pairs(128, 128, 0, 0, 64)
    wide = matmul(corr5, double)
    for z in range(4):
        plane = jnp.where(row < 2, wide[2 * z : 2 * z + 1], jnp.where(row < 4, wide[2 * z + 1 : 2 * z + 2], 0.0))
        for k in (0, 1):
            p = 1 + 2 * z + k
            q4[p] = d4[p] + jnp.where(F4[p] > 0.0, plane, 0.0)
    four.sweep(q4, f4, d4, 1, 9, 8)
    four.sweep(d4, f4, q4, 1, 9, 8)

    T3[0:8] = matmul(rows_of(q4.at[1:9], 8), double).reshape(8, 8, 128)
    for j in range(8):
        part = T3[j, 0:4, :]
        T3[8, pl.ds(0, 4, 2), :] = part
        T3[8, pl.ds(1, 4, 2), :] = part
        plane = T3[8]
        for k in (0, 1):
            p = 1 + 2 * j + k
            q3[p] = d3[p] + plane
    three.sweep(q3, f3, d3, 1, 17, 16)
    three.sweep(d3, f3, q3, 1, 17, 16)

    two = Level(w2)
    two.build(F2, 0.25**2, 1, 33, (True, False), 4)
    shift = jnp.remainder(4 - 16 * ix, 128)
    for j in range(16):
        T2[0, j] = pltpu.roll(q3[1 + j], shift, 1)
    T2[1] = matmul(T2[0].reshape(128, 128), spread_pairs(128, 128, 0, 0, 24)).reshape(16, 8, 128)
    zero2 = jnp.zeros((16, 128), F32)
    for ref in (qa2, qb2):
        ref[0] = zero2
        ref[33] = zero2
    for j in range(16):
        part = T2[1, j]
        qb2[1, pl.ds(0, 8, 2), :] = part
        qb2[1, pl.ds(1, 8, 2), :] = part
        plane = qb2[1]
        for k in (0, 1):
            p = 1 + 2 * j + k
            qa2[p] = d2[p] + jnp.where(F2[p] > 0.0, plane, 0.0)
    two.sweep(qa2, f2, qb2, 1, 33, 4)
    two.sweep(qb2, f2, qa2, 1, 33, 4)

    low = jnp.where(iz > 0, 1.0, 0.0).astype(F32)
    high = jnp.where(iz < nz - 1, 1.0, 0.0).astype(F32)
    for k, ref in enumerate((f1, F1)):
        for z in range(8):
            ref[z] = z_low[k, z] * low
            ref[8 + z] = to_z[k, z]
            ref[16 + z] = z_high[k, z] * high
    one = Level(w1)
    one.build(F1, 0.25, 3, 21, (False, False))
    one.first(f1, qa1, 3, 21)
    one.sweep(qa1, f1, qb1, 4, 20)
    shift = jnp.remainder(4 - 4 * iy, 16)
    for j in range(8):
        at = jnp.clip(4 * iz - 2 + j, 0, 31)
        U1[j] = pltpu.roll(qa2[1 + at], shift, 0)
    U1[...] = matmul(rows_of(U1, 8), spread_pairs(128, 128, 0, 112, 48)).reshape(8, 16, 128)
    for j in range(8):
        part = U1[j, 0:12, :]
        T1[pl.ds(0, 12, 2), :] = part
        T1[pl.ds(1, 12, 2), :] = part
        plane = T1[...]
        for k in (0, 1):
            p = 4 + 2 * j + k
            qa1[p] = qb1[p] + jnp.where(F1[p] > 0.0, plane, 0.0)
    one.sweep(qa1, f1, qb1, 5, 19)
    one.sweep(qb1, f1, qa1, 6, 18)

    zero_level = Level((wx0, wy0, wz0, g0, i0))
    T0[...] = matmul(qa1[6:18].reshape(288, 128), spread_pairs(128, 256, 0, 0, 128)).reshape(12, 24, 256)

    def refine(j):
        for half in (0, 1):
            part = T0[j, 4:20, 128 * half : 128 * half + 128]
            U0[half, pl.ds(0, 16, 2), :] = part
            U0[half, pl.ds(1, 16, 2), :] = part
        plane = jnp.concatenate([U0[0], U0[1]], axis=1)
        for k in (0, 1):
            p = 4 + 2 * j + k
            qa0[p] = D0[p] + jnp.where(i0[p] > 0.0, plane, 0.0)

    planes(0, 12, refine, 1)
    zero_level.sweep(qa0, S, qb0, 6, 26)
    zero_level.sweep(qb0, S, qa0, 7, 25)

    def finish(p):
        c, applied = zero_level.apply(qa0, p)
        pressure[p - 8] = c[8:24, 0:128]
        residual[p - 8] = (S[p] - applied)[8:24, 0:128]

    planes(8, 24, finish)


def call(kernel, name, out_shapes, scratch=()):
    spec = pl.BlockSpec(memory_space=pltpu.VMEM)

    def run(*args):
        return pl.pallas_call(
            kernel,
            out_shape=[jax.ShapeDtypeStruct(shape, F32) for shape in out_shapes],
            in_specs=[spec] * len(args),
            out_specs=[spec] * len(out_shapes),
            scratch_shapes=[pltpu.VMEM(shape, F32) for shape in scratch],
            compiler_params=pltpu.CompilerParams(vmem_limit_bytes=VMEM_LIMIT),
            name=name,
        )(*args)

    return run


def ring(axis, step):
    size = lax.axis_size(axis)
    return [(i, (i + step) % size) for i in range(size)]


def around(oz, oy):
    nz, ny = lax.axis_size("gz"), lax.axis_size("gy")
    return [
        (y * nz + z, (y - oy) % ny * nz + (z - oz) % nz) for y in range(ny) for z in range(nz)
    ]


BIG, MID, MID2 = (32, 32, 256), (14, 16, 128), (34, 16, 128)
WIDE1 = (24, 24, 128)


def local(source, fraction):
    block = (8, 16, 128)
    to_left, to_right = call(pack_x_kernel, "pack_x", [block, block])(source, fraction)
    from_right = lax.ppermute(to_left, "gx", ring("gx", -1))
    from_left = lax.ppermute(to_right, "gx", ring("gx", 1))
    halo, *sends = call(
        pack_yz_kernel, "pack_yz", [(16, 16, 128)] + [piece_shape(oz, oy) for oz, oy in AROUND]
    )(source, fraction, from_right, from_left)
    pieces = [
        lax.ppermute(piece, ("gy", "gz"), around(oz, oy)) for (oz, oy), piece in zip(AROUND, sends)
    ]
    *fine, own1, payload = call(
        down_kernel,
        "down",
        [BIG] * 7 + [(2, 8, 8, 128), (32, 16, 128)],
        [BIG, BIG, (14, 32, 256), (14, 32, 128), (4, 16, 128)] + [MID] * 9,
    )(source, fraction, halo, *pieces)
    y_low = lax.ppermute(own1, "gy", ring("gy", 1))
    y_high = lax.ppermute(own1, "gy", ring("gy", -1))
    got = lax.all_to_all(payload, ("gy", "gz"), 0, 0)
    to_z, payload, f2, F2, d2 = call(
        middle_kernel,
        "middle",
        [(2, 8, 24, 128), (8, 4, 8, 128), MID2, MID2, MID2],
        [MID2, (16, 16, 128), (16, 16, 128)] + [MID2] * 5,
    )(got, own1, y_low, y_high)
    z_low = lax.ppermute(to_z, "gz", ring("gz", 1))
    z_high = lax.ppermute(to_z, "gz", ring("gz", -1))
    got = lax.all_to_all(payload, "gx", 0, 0)
    three, four = (18, 8, 128), (10, 8, 128)
    pressure, residual = call(
        up_kernel,
        "up",
        [(16, 16, 128)] * 2,
        [three] * 4
        + [four] * 4
        + [three] * 5
        + [four] * 5
        + [MID2] * 5
        + [WIDE1] * 5
        + [(9, 8, 128), (8, 128), (8, 128), MID2, MID2, (2, 16, 8, 128)]
        + [WIDE1] * 4
        + [(24, 128), (8, 16, 128), (12, 24, 256), (2, 32, 128), BIG, BIG],
    )(got, to_z, z_low, z_high, f2, F2, d2, *fine)
    return (pressure, residual)


def solution(mesh):
    spec = P("gz", "gy", "gx")
    return jax.shard_map(
        local, mesh=mesh, in_specs=(spec, spec), out_specs=(spec, spec), check_vma=False
    )
```

```python
import jax
import jax.numpy as jnp
from jax import lax
from jax.experimental import pallas as pl
from jax.experimental.pallas import tpu as pltpu
from jax.sharding import PartitionSpec as P

RELAXATION = 0.8
F32 = jnp.float32
VMEM_LIMIT = 32 * 1024 * 1024


def turn(v, shift, axis):
    size = v.shape[axis]
    shift = shift % size
    return v if shift == 0 else pltpu.roll(v, shift, axis)


def ahead(v, axis):
    return turn(v, -1, axis)


def behind(v, axis):
    return turn(v, 1, axis)


def index_of(shape, axis):
    return lax.broadcasted_iota(jnp.int32, shape, axis)


def matmul(a, b):
    return lax.dot_general(
        a, b, (((1,), (0,)), ((), ())), precision=lax.Precision.HIGHEST, preferred_element_type=F32
    )


def planes(lo, hi, body, unroll=2):
    trips = (hi - lo) // unroll
    if trips > 1:

        def step(i, carry):
            for k in range(unroll):
                body(lo + i * unroll + k)
            return carry

        lax.fori_loop(0, trips, step, 0)
    else:
        trips = 0
    for p in range(lo + trips * unroll, hi):
        body(p)


class Level:
    def __init__(self, refs):
        self.wx, self.wy, self.wz, self.diag, self.inv = refs

    def build(self, frac, scale, lo, hi, wraps, unroll=2):
        half = 0.5 * scale
        self.wz[lo - 1] = half * (frac[lo - 1] + frac[lo])

        def plane(p):
            c, up, down = frac[p], frac[p + 1], frac[p - 1]
            total = 6.0 * c + up + down
            for axis, keep in ((1, self.wx), (0, self.wy)):
                after, before = ahead(c, axis), behind(c, axis)
                weight = half * (c + after)
                if wraps[axis]:
                    at = index_of(c.shape, axis)
                    last = at == c.shape[axis] - 1
                    weight = jnp.where(last, 0.0, weight)
                    after = jnp.where(last, 0.0, after)
                    before = jnp.where(at == 0, 0.0, before)
                keep[p] = weight
                total = total + after + before
            self.wz[p] = half * (c + up)
            diag = half * total
            self.diag[p] = diag
            self.inv[p] = jnp.where(c > 0.0, RELAXATION / jnp.where(c > 0.0, diag, 1.0), 0.0)

        planes(lo, hi, plane, unroll)

    def apply(self, q, p):
        c, wx, wy = q[p], self.wx[p], self.wy[p]
        near = wx * ahead(c, 1) + behind(wx * c, 1) + wy * ahead(c, 0) + behind(wy * c, 0)
        near = near + self.wz[p] * q[p + 1] + self.wz[p - 1] * q[p - 1]
        return c, self.diag[p] * c - near

    def first(self, rhs, out, lo, hi, unroll=2):
        def plane(p):
            out[p] = self.inv[p] * rhs[p]

        planes(lo, hi, plane, unroll)

    def sweep(self, q, rhs, out, lo, hi, unroll=2):
        def plane(p):
            c, applied = self.apply(q, p)
            out[p] = c + self.inv[p] * (rhs[p] - applied)

        planes(lo, hi, plane, unroll)

    def halved_residual(self, q, rhs, out, lo, hi, unroll=1):
        def pair(j):
            _, one = self.apply(q, lo + 2 * j)
            _, two = self.apply(q, lo + 2 * j + 1)
            out[j] = (rhs[lo + 2 * j] - one) + (rhs[lo + 2 * j + 1] - two)

        planes(0, (hi - lo) // 2, pair, unroll)


def halved(values, out, lo, hi):
    def pair(j):
        out[j] = values[lo + 2 * j] + values[lo + 2 * j + 1]

    planes(0, (hi - lo) // 2, pair)


def rows_of(ref, count):
    _, rows, lanes = ref.shape
    return ref[0:count].reshape(count * rows, lanes)


def gather_pairs(lanes, out_lanes, first, place, count):
    at, to = index_of((lanes, out_lanes), 0), index_of((lanes, out_lanes), 1) - place
    pair = jnp.remainder(at - first, lanes)
    hit = (pair >= 2 * to) & (pair <= 2 * to + 1) & (to >= 0) & (to < count)
    return jnp.where(hit, 0.125, 0.0).astype(F32)


def spread_pairs(lanes, out_lanes, first, start, count):
    at, to = index_of((lanes, out_lanes), 0) - first, index_of((lanes, out_lanes), 1)
    pair = jnp.remainder(to - start, out_lanes)
    hit = (pair >= 2 * at) & (pair <= 2 * at + 1) & (at >= 0) & (at < count)
    return jnp.where(hit, 1.0, 0.0).astype(F32)


def inside(okay):
    return jnp.where(okay, 1.0, 0.0).astype(F32)


def copies(pairs, sems):
    started = [pltpu.make_async_copy(a, b, sems.at[i]) for i, (a, b) in enumerate(pairs)]
    for copy in started:
        copy.start()
    return started


def pack_x_kernel(source, fraction, s, f, to_left, to_right, sems):
    for copy in copies(((source, s), (fraction, f)), sems):
        copy.wait()
    lane = index_of((16, 128), 1)
    for z in range(8):
        a, b, c, d = s[z], s[z + 8], f[z], f[z + 8]
        to_left[z] = jnp.where(
            lane < 32,
            a,
            jnp.where(lane < 64, turn(b, 32, 1), jnp.where(lane < 96, turn(c, 64, 1), turn(d, 96, 1))),
        )
        to_right[z] = jnp.where(
            lane >= 96,
            a,
            jnp.where(lane >= 64, turn(b, 96, 1), jnp.where(lane >= 32, turn(c, 64, 1), turn(d, 32, 1))),
        )


def pack_y_kernel(s, f, from_right, from_left, halo, to_low, to_high):
    ix = lax.axis_index("gx")
    left = inside(ix > 0)
    right = inside(ix < lax.axis_size("gx") - 1)
    lane = index_of((16, 128), 1)
    is_right = (lane < 32) | ((lane >= 64) & (lane < 96))
    for z in range(8):
        r, l = from_right[z] * right, from_left[z] * left
        halo[z] = jnp.where(is_right, r, l)
        halo[z + 8] = jnp.where(is_right, turn(r, 96, 1), turn(l, 32, 1))
    for k, ref in enumerate((s, f, halo)):
        to_low[k] = ref[:, 0:8, :]
        to_high[k] = ref[:, 8:16, :]


def pack_z_kernel(s, f, halo, y_low, y_high, to_low, to_high):
    iy, ny = lax.axis_index("gy"), lax.axis_size("gy")
    low, high = inside(iy > 0), inside(iy < ny - 1)
    for out, start in ((to_low, 0), (to_high, 9)):
        for k, ref in enumerate((s, f, halo)):
            for j in range(7):
                z = start + j
                out[k, j, 0:8, :] = y_low[k, z] * low
                out[k, j, 8:24, :] = ref[z]
                out[k, j, 24:32, :] = y_high[k, z] * high


def down_kernel(s, f, halo, y_low, y_high, z_low, z_high, *refs):
    kept, own1, message, payload = refs[:7], refs[7], refs[8], refs[9]
    F, Q, T, U, V, f1, F1, q1, d1, *w1 = refs[10:24]
    S, D0, *w0 = refs[24:31]
    sems = refs[31]
    iz, iy = lax.axis_index("gz"), lax.axis_index("gy")
    nz, ny = lax.axis_size("gz"), lax.axis_size("gy")
    for p in (0, 31):
        S[p] = jnp.zeros((32, 256), F32)
        F[p] = jnp.zeros((32, 256), F32)

    def put(z0, y0, depth, height, scale, plane):
        edge = index_of((height, 128), 1)
        edge = (edge < 32) | (edge >= 96)

        def body(k):
            a, b, h = plane(k)
            if scale is not None:
                a, b, h = a * scale, b * scale, h * scale
            rows = pl.ds(y0, height)
            S[z0 + k, rows, 0:128] = a
            F[z0 + k, rows, 0:128] = b
            S[z0 + k, rows, 128:256] = jnp.where(edge, h, 0.0)
            F[z0 + k, rows, 128:256] = jnp.where(edge, turn(h, 64, 1), 0.0)

        planes(0, depth, body, 4)

    put(8, 8, 16, 16, None, lambda k: (s[k], f[k], halo[k]))
    for ref, y0, okay in ((y_low, 0, iy > 0), (y_high, 24, iy < ny - 1)):
        put(8, y0, 16, 8, inside(okay), lambda k, ref=ref: (ref[0, k], ref[1, k], ref[2, k]))
    for ref, z0, okay in ((z_low, 1, iz > 0), (z_high, 24, iz < nz - 1)):
        put(z0, 0, 7, 32, inside(okay), lambda k, ref=ref: (ref[0, k], ref[1, k], ref[2, k]))

    started = copies(((S, kept[0]),), sems)
    level = Level(w0)
    level.build(F, 1.0, 2, 30, (False, False))
    started += copies(tuple(zip(w0, kept[2:])), sems.at[1:6])
    level.first(S, Q, 2, 30)
    level.sweep(Q, S, D0, 3, 29)
    started += copies(((D0, kept[1]),), sems.at[6:7])
    level.halved_residual(D0, S, T, 4, 28)
    C = gather_pairs(256, 128, 0, 0, 128)

    def coarse(count, out, start):
        U[0:count] = matmul(rows_of(T, count), C).reshape(count, 32, 128)
        for j in range(count):
            out[start + j] = U[j, pl.ds(0, 16, 2), :] + U[j, pl.ds(1, 16, 2), :]

    coarse(12, f1, 1)
    halved(F, T, 2, 30)
    coarse(14, F1, 0)
    for j in range(8):
        message[j] = f1[3 + j, 4:12, :]
        message[8 + j] = F1[3 + j, 4:12, :]
    started += copies(((message.at[0:16], own1),), sems.at[7:8])

    level = Level(w1)
    level.build(F1, 0.25, 1, 13, (False, False))
    level.first(f1, q1, 1, 13)
    level.sweep(q1, f1, d1, 2, 12)
    level.halved_residual(d1, f1, V, 3, 11)
    first = matmul(rows_of(V, 4), gather_pairs(128, 128, 112, 0, 48))
    halved(F1, V, 3, 11)
    both = first + matmul(rows_of(V, 4), gather_pairs(128, 128, 112, 64, 48))
    V[0:4] = both.reshape(4, 16, 128)
    for j in range(4):
        rows = V[j, pl.ds(4, 4, 2), :] + V[j, pl.ds(5, 4, 2), :]
        message[16 + j // 2, 4 * (j % 2) : 4 * (j % 2) + 4, :] = rows
    payload[...] = message[16:18]
    for copy in started:
        copy.wait()


def spread_y_kernel(message, y_low, y_high, far, to_low, to_high):
    iy, ny = lax.axis_index("gy"), lax.axis_size("gy")
    low, high = inside(iy > 0), inside(iy < ny - 1)
    for out, start in ((to_low, 0), (to_high, 2)):
        for k in range(2):
            for j in range(6):
                at, z = (6 * k + j) * 3, 8 * k + start + j
                out[at] = y_low[z] * low
                out[at + 1] = message[z]
                out[at + 2] = y_high[z] * high
        for step, ref, first in ((0, message, 16), (-1, y_low, 16), (1, y_high, 16), (2, far, 0)):
            at = 36 + 2 * jnp.remainder(iy + step + ny, ny)
            for k in range(2):
                out[at + k] = ref[first + k]


def spread_z_kernel(own, z_low, z_high, out):
    for k, ref in enumerate((z_low, own, z_high)):
        out[8 * k : 8 * k + 8] = ref[36:44]


def middle_kernel(own, before, after, payload, f2h, F2h, d2h, *refs):
    f2, F2, d2, q2, T, U, *w2, sems = refs
    iz, nz = lax.axis_index("gz"), lax.axis_size("gz")
    lane = index_of((8, 128), 1)
    keep = lane < 48
    zero = jnp.zeros((16, 128), F32)
    for ref in (f2, F2, q2, d2):
        ref[0] = zero
        ref[33] = zero
    for ref, start in ((before, -4), (own, -1), (after, 2)):
        for k in range(3):
            base = 1 + 4 * jnp.remainder(iz + start + k + nz, nz)
            for gy in range(4):
                for j in range(2):
                    block = ref[8 * k + 2 * gy + j]
                    rhs, frac = jnp.where(keep, block, 0.0), jnp.where(keep, turn(block, 64, 1), 0.0)
                    for half in range(2):
                        rows = slice(4 * half, 4 * half + 4)
                        f2[base + 2 * j + half, 4 * gy : 4 * gy + 4, :] = rhs[rows]
                        F2[base + 2 * j + half, 4 * gy : 4 * gy + 4, :] = frac[rows]
    started = copies(((f2, f2h), (F2, F2h)), sems)
    level = Level(w2)
    level.build(F2, 0.25**2, 1, 33, (True, False), 4)
    level.first(f2, q2, 1, 33, 4)
    level.sweep(q2, f2, d2, 1, 33, 4)
    started += copies(((d2, d2h),), sems.at[2:3])
    C = gather_pairs(128, 128, 8, 0, 16)
    for field in range(2):
        if field == 0:
            level.halved_residual(d2, f2, T, 1, 33, 2)
        else:
            halved(F2, T, 1, 33)
        U[...] = matmul(rows_of(T, 16), C).reshape(16, 16, 128)
        for zh in range(2):
            total = None
            for zl in range(8):
                z = zh * 8 + zl
                part = U[z, pl.ds(0, 8, 2), :] + U[z, pl.ds(1, 8, 2), :]
                part = turn(part, 16 * zl, 1)
                total = part if total is None else total + part
            for d in range(8):
                payload[d, 2 * field + zh] = total
    for copy in started:
        copy.wait()


def bottom(frac, rhs, half):
    shape = (8, 128)
    row, lane = index_of(shape, 0), index_of(shape, 1)
    used = lane < 32
    odd = jnp.remainder(row, 2) == 1
    y_near = jnp.where(odd, behind(frac, 0), ahead(frac, 0))
    z_up = jnp.where(row >= 6, 0.0, turn(frac, -2, 0))
    z_down = jnp.where(row < 2, 0.0, turn(frac, 2, 0))
    x_up = jnp.where(lane < 31, ahead(frac, 1), 0.0)
    x_down = jnp.where(lane > 0, behind(frac, 1), 0.0)
    diag = half * (6.0 * frac + y_near + z_up + z_down + x_up + x_down)
    after = jnp.where(lane < 31, -half * (frac + x_up), 0.0)
    before = jnp.where((lane > 0) & used, -half * (frac + x_down), 0.0)
    A, C, D, g = [], [], [], []
    for i in range(8):
        here = row == i
        z, y = i // 2, i % 2
        linked = (row == 2 * z + 1 - y) | (row == i - 2) | (row == i + 2)
        mine = jnp.broadcast_to(frac[i : i + 1], shape)
        block = jnp.where(here, diag, jnp.where(linked, -half * (mine + frac), 0.0))
        D.append(jnp.where(used, block, jnp.where(here, 1.0, 0.0)))
        A.append(jnp.where(here, before, 0.0))
        C.append(jnp.where(here, after, 0.0))
        g.append(jnp.broadcast_to(jnp.where(used[:1], rhs[i : i + 1], 0.0), shape))

    def pick(v, k):
        return jnp.broadcast_to(v[k : k + 1], shape)

    def divide(D, others):
        D, others = list(D), [list(o) for o in others]
        for k in range(8):
            inverse = 1.0 / pick(D[k], k)
            D[k] = D[k] * inverse
            for o in others:
                o[k] = o[k] * inverse
            for i in range(8):
                if i != k:
                    factor = pick(D[i], k)
                    D[i] = D[i] - factor * D[k]
                    for o in others:
                        o[i] = o[i] - factor * o[k]
        return others

    step = 1
    while step < 32:
        X, Y, h = divide(D, (A, C, g))
        Xl, Yl, hl = [[turn(v, step, 1) for v in o] for o in (X, Y, h)]
        Xr, Yr, hr = [[turn(v, -step, 1) for v in o] for o in (X, Y, h)]
        nA, nC, nD, ng = [], [], [], []
        for i in range(8):
            d, a, c, r = D[i], None, None, g[i]
            for k in range(8):
                pa, pc = pick(A[i], k), pick(C[i], k)
                d = d - (pa * Yl[k] + pc * Xr[k])
                r = r - (pa * hl[k] + pc * hr[k])
                a = -pa * Xl[k] if a is None else a - pa * Xl[k]
                c = -pc * Yr[k] if c is None else c - pc * Yr[k]
            nA.append(a)
            nC.append(c)
            nD.append(d)
            ng.append(r)
        A, C, D, g = nA, nC, nD, ng
        step *= 2
    (u,) = divide(D, (g,))
    out = jnp.zeros(shape, F32)
    for i in range(8):
        out = jnp.where((row == i) & used, u[i], out)
    return out


def up_kernel(got, *refs):
    far, refs = refs[:15], refs[15:]
    pressure, residual, refs = refs[0], refs[1], refs[2:]
    near, sems = refs[:15], refs[15]
    started = copies(tuple(zip(far, near)), sems)
    own1, y_low, y_high, z_low, z_high, f2, F2, d2, S, D0, wx0, wy0, wz0, g0, i0 = near
    refs = refs[16:]
    f3, F3, q3, d3, f4, F4, q4, d4 = refs[:8]
    w3, w4, w2, w1 = refs[8:13], refs[13:18], refs[18:23], refs[23:28]
    T3, g5, F5, qa2, qb2, T2, f1, F1, qa1, qb1, T1, U1, T0, U0, qa0, qb0 = refs[28:]
    iz, iy, ix = lax.axis_index("gz"), lax.axis_index("gy"), lax.axis_index("gx")
    nz = lax.axis_size("gz")
    lane = index_of((8, 128), 1)
    row = index_of((8, 128), 0)
    zero = jnp.zeros((8, 128), F32)

    for ref in (f3, F3, q3, d3):
        ref[0] = zero
        ref[17] = zero
    for ref in (f4, F4, q4, d4):
        ref[0] = zero
        ref[9] = zero
    for field, ref in enumerate((f3, F3)):
        for zh in range(2):
            blocks = [got[d, 2 * field + zh] for d in range(8)]
            for zl in range(8):
                total = turn(blocks[0], -16 * zl, 1)
                for d in range(1, 8):
                    total = jnp.where(lane >= 16 * d, turn(blocks[d], 16 * (d - zl), 1), total)
                ref[1 + zh * 8 + zl] = total

    three, four = Level(w3), Level(w4)
    three.build(F3, 0.25**3, 1, 17, (True, True), 16)
    three.first(f3, q3, 1, 17, 16)
    three.sweep(q3, f3, d3, 1, 17, 16)
    C = gather_pairs(128, 128, 0, 0, 64)
    for field in range(2):
        if field == 0:
            three.halved_residual(d3, f3, T3, 1, 17, 8)
        else:
            halved(F3, T3, 1, 17)
        T3[0:8] = matmul(rows_of(T3, 8), C).reshape(8, 8, 128)
        out = (f4, F4)[field]
        for j in range(8):
            out[1 + j] = zero
            out[1 + j, 0:4, :] = T3[j, pl.ds(0, 4, 2), :] + T3[j, pl.ds(1, 4, 2), :]
    four.build(F4, 0.25**4, 1, 9, (False, False), 8)
    four.first(f4, q4, 1, 9, 8)
    four.sweep(q4, f4, d4, 1, 9, 8)
    for field in range(2):
        if field == 0:
            four.halved_residual(d4, f4, T3, 1, 9, 4)
        else:
            halved(F4, T3, 1, 9)
        T3[0:4] = matmul(rows_of(T3, 4), C).reshape(4, 8, 128)
        out = (g5, F5)[field]
        for j in range(4):
            out[2 * j : 2 * j + 2, :] = T3[j, pl.ds(0, 2, 2), :] + T3[j, pl.ds(1, 2, 2), :]
    corr5 = bottom(F5[...], g5[...], 0.5 * 0.25**5)

    double = spread_pairs(128, 128, 0, 0, 64)
    wide = matmul(corr5, double)
    for z in range(4):
        plane = jnp.where(row < 2, wide[2 * z : 2 * z + 1], jnp.where(row < 4, wide[2 * z + 1 : 2 * z + 2], 0.0))
        for k in (0, 1):
            p = 1 + 2 * z + k
            q4[p] = d4[p] + jnp.where(F4[p] > 0.0, plane, 0.0)
    four.sweep(q4, f4, d4, 1, 9, 8)
    four.sweep(d4, f4, q4, 1, 9, 8)

    T3[0:8] = matmul(rows_of(q4.at[1:9], 8), double).reshape(8, 8, 128)
    for j in range(8):
        part = T3[j, 0:4, :]
        T3[8, pl.ds(0, 4, 2), :] = part
        T3[8, pl.ds(1, 4, 2), :] = part
        plane = T3[8]
        for k in (0, 1):
            p = 1 + 2 * j + k
            q3[p] = d3[p] + plane
    three.sweep(q3, f3, d3, 1, 17, 16)
    three.sweep(d3, f3, q3, 1, 17, 16)

    for copy in started[5:8]:
        copy.wait()
    two = Level(w2)
    two.build(F2, 0.25**2, 1, 33, (True, False), 4)
    shift = jnp.remainder(4 - 16 * ix, 128)
    for j in range(16):
        T2[0, j] = pltpu.roll(q3[1 + j], shift, 1)
    T2[1] = matmul(T2[0].reshape(128, 128), spread_pairs(128, 128, 0, 0, 24)).reshape(16, 8, 128)
    zero2 = jnp.zeros((16, 128), F32)
    for ref in (qa2, qb2):
        ref[0] = zero2
        ref[33] = zero2
    for j in range(16):
        part = T2[1, j]
        qb2[1, pl.ds(0, 8, 2), :] = part
        qb2[1, pl.ds(1, 8, 2), :] = part
        plane = qb2[1]
        for k in (0, 1):
            p = 1 + 2 * j + k
            qa2[p] = d2[p] + jnp.where(F2[p] > 0.0, plane, 0.0)
    two.sweep(qa2, f2, qb2, 1, 33, 4)
    two.sweep(qb2, f2, qa2, 1, 33, 4)

    for copy in started[:5]:
        copy.wait()
    iy, ny = lax.axis_index("gy"), lax.axis_size("gy")
    low, high, under, over = inside(iy > 0), inside(iy < ny - 1), inside(iz > 0), inside(iz < nz - 1)
    for k, ref in enumerate((f1, F1)):
        for z in range(8):
            ref[8 + z, 0:8, :] = y_low[8 * k + z] * low
            ref[8 + z, 8:16, :] = own1[8 * k + z]
            ref[8 + z, 16:24, :] = y_high[8 * k + z] * high
        for j in range(6):
            for t in range(3):
                at = (6 * k + j) * 3 + t
                ref[2 + j, 8 * t : 8 * t + 8, :] = z_low[at] * under
                ref[16 + j, 8 * t : 8 * t + 8, :] = z_high[at] * over
    one = Level(w1)
    one.build(F1, 0.25, 3, 21, (False, False))
    one.first(f1, qa1, 3, 21)
    one.sweep(qa1, f1, qb1, 4, 20)
    shift = jnp.remainder(4 - 4 * iy, 16)
    for j in range(8):
        at = jnp.clip(4 * iz - 2 + j, 0, 31)
        U1[j] = pltpu.roll(qa2[1 + at], shift, 0)
    U1[...] = matmul(rows_of(U1, 8), spread_pairs(128, 128, 0, 112, 48)).reshape(8, 16, 128)
    for j in range(8):
        part = U1[j, 0:12, :]
        T1[pl.ds(0, 12, 2), :] = part
        T1[pl.ds(1, 12, 2), :] = part
        plane = T1[...]
        for k in (0, 1):
            p = 4 + 2 * j + k
            qa1[p] = qb1[p] + jnp.where(F1[p] > 0.0, plane, 0.0)
    one.sweep(qa1, f1, qb1, 5, 19)
    one.sweep(qb1, f1, qa1, 6, 18)

    for copy in started[8:]:
        copy.wait()
    zero_level = Level((wx0, wy0, wz0, g0, i0))
    T0[...] = matmul(qa1[6:18].reshape(288, 128), spread_pairs(128, 256, 0, 0, 128)).reshape(12, 24, 256)

    def refine(j):
        for half in (0, 1):
            part = T0[j, 4:20, 128 * half : 128 * half + 128]
            U0[half, pl.ds(0, 16, 2), :] = part
            U0[half, pl.ds(1, 16, 2), :] = part
        plane = jnp.concatenate([U0[0], U0[1]], axis=1)
        for k in (0, 1):
            p = 4 + 2 * j + k
            qa0[p] = D0[p] + jnp.where(i0[p] > 0.0, plane, 0.0)

    planes(0, 12, refine, 1)
    zero_level.sweep(qa0, S, qb0, 6, 26)
    zero_level.sweep(qb0, S, qa0, 7, 25)

    def finish(p):
        c, applied = zero_level.apply(qa0, p)
        pressure[p - 8] = c[8:24, 0:128]
        residual[p - 8] = (S[p] - applied)[8:24, 0:128]

    planes(8, 24, finish)


def call(kernel, name, ins, outs, scratch=()):
    anywhere = pl.BlockSpec(memory_space=pl.ANY)
    spec = {"v": pl.BlockSpec(memory_space=pltpu.VMEM), "n": pl.BlockSpec(memory_space=pltpu.VMEM), "h": anywhere}
    kind = {"v": pltpu.VMEM, "h": pltpu.HBM, "n": jax.ShapeDtypeStruct}
    space = {"v": pltpu.VMEM, "h": pltpu.HBM}

    def run(*args):
        args = [pltpu.with_memory_space_constraint(a, space[k]) if k in space else a for a, k in zip(args, ins)]
        return pl.pallas_call(
            kernel,
            out_shape=[kind[k](shape, F32) for k, shape in outs],
            in_specs=[spec[k] for k in ins],
            out_specs=[spec[k] for k, _ in outs],
            scratch_shapes=[pltpu.VMEM(shape, F32) if isinstance(shape, tuple) else shape for shape in scratch],
            compiler_params=pltpu.CompilerParams(vmem_limit_bytes=VMEM_LIMIT),
            name=name,
        )(*args)

    return run


def ring(axis, step):
    size = lax.axis_size(axis)
    return [(i, (i + step) % size) for i in range(size)]


def exchange(to_low, to_high, axis, reach=1):
    return lax.ppermute(to_high, axis, ring(axis, reach)), lax.ppermute(to_low, axis, ring(axis, -reach))


BIG, MID, MID2, WIDE1 = (32, 32, 256), (14, 16, 128), (34, 16, 128), (24, 24, 128)
THREE, FOUR = (18, 8, 128), (10, 8, 128)


def local(source, fraction):
    def dma(count):
        return pltpu.SemaphoreType.DMA((count,))

    own, strip = (16, 16, 128), (8, 16, 128)
    s, f, to_left, to_right = call(
        pack_x_kernel, "pack_x", "hh", [("v", own)] * 2 + [("v", strip)] * 2, [dma(2)]
    )(source, fraction)
    from_left, from_right = exchange(to_left, to_right, "gx")
    rows = (3, 16, 8, 128)
    halo, to_low, to_high = call(pack_y_kernel, "pack_y", "vvvv", [("v", own), ("v", rows), ("v", rows)])(
        s, f, from_right, from_left
    )
    y_low, y_high = exchange(to_low, to_high, "gy")
    layers = (3, 7, 32, 128)
    to_low, to_high = call(pack_z_kernel, "pack_z", "vvvvv", [("v", layers)] * 2)(s, f, halo, y_low, y_high)
    z_low, z_high = exchange(to_low, to_high, "gz")
    *fine, own1, message, payload = call(
        down_kernel,
        "down",
        "vvvvvvv",
        [("h", BIG)] * 7 + [("h", (16, 8, 128)), ("v", (18, 8, 128)), ("v", (2, 8, 128))],
        [BIG, BIG, (14, 32, 256), (14, 32, 128), (4, 16, 128)] + [MID] * 9 + [BIG] * 7 + [dma(8)],
    )(s, f, halo, y_low, y_high, z_low, z_high)

    y_low, y_high = exchange(message, message, "gy")
    opposite = lax.ppermute(payload, "gy", ring("gy", 2))
    layers = (44, 8, 128)
    to_low, to_high = call(spread_y_kernel, "spread_y", "vvvv", [("v", layers)] * 2)(message, y_low, y_high, opposite)
    z_low, z_high = exchange(to_low, to_high, "gz")
    (near,) = call(spread_z_kernel, "spread_z", "vvv", [("v", (24, 8, 128))])(to_low, z_low, z_high)
    before, after = exchange(near, near, "gz", 3)
    payload, f2, F2, d2 = call(
        middle_kernel,
        "middle",
        "vvv",
        [("v", (8, 4, 8, 128))] + [("h", MID2)] * 3,
        [MID2] * 4 + [(16, 16, 128), (16, 16, 128)] + [MID2] * 5 + [dma(3)],
    )(near, before, after)
    got = lax.all_to_all(payload, "gx", 0, 0)
    kept = [own1, y_low, y_high, z_low, z_high, f2, F2, d2, *fine]
    pressure, residual = call(
        up_kernel,
        "up",
        "v" + "h" * 15,
        [("n", own)] * 2,
        [(16, 8, 128)]
        + [(18, 8, 128)] * 2
        + [(44, 8, 128)] * 2
        + [MID2] * 3
        + [BIG] * 7
        + [dma(15)]
        + [THREE] * 4
        + [FOUR] * 4
        + [THREE] * 5
        + [FOUR] * 5
        + [MID2] * 5
        + [WIDE1] * 5
        + [(9, 8, 128), (8, 128), (8, 128), MID2, MID2, (2, 16, 8, 128)]
        + [WIDE1] * 4
        + [(24, 128), (8, 16, 128), (12, 24, 256), (2, 32, 128), BIG, BIG],
    )(got, *kept)
    return (pressure, residual)


def solution(mesh):
    spec = P("gz", "gy", "gx")
    return jax.shard_map(
        local, mesh=mesh, in_specs=(spec, spec), out_specs=(spec, spec), check_vma=False
    )
```

```python
import jax
import jax.numpy as jnp
from jax import lax
from jax.experimental import pallas as pl
from jax.experimental.pallas import tpu as pltpu
from jax.sharding import PartitionSpec as P

RELAXATION = 0.8
F32 = jnp.float32
VMEM_LIMIT = 32 * 1024 * 1024


def turn(v, shift, axis):
    size = v.shape[axis]
    shift = shift % size
    return v if shift == 0 else pltpu.roll(v, shift, axis)


def ahead(v, axis):
    return turn(v, -1, axis)


def behind(v, axis):
    return turn(v, 1, axis)


def index_of(shape, axis):
    return lax.broadcasted_iota(jnp.int32, shape, axis)


def matmul(a, b):
    b = b.astype(jnp.bfloat16)
    total = None
    for part in range(3):
        piece = a.astype(jnp.bfloat16)
        product = lax.dot_general(piece, b, (((1,), (0,)), ((), ())), preferred_element_type=F32)
        total = product if total is None else total + product
        if part < 2:
            a = a - piece.astype(F32)
    return total


def planes(lo, hi, body, unroll=10):
    trips = (hi - lo) // unroll
    if trips > 1:

        def step(i, carry):
            for k in range(unroll):
                body(lo + i * unroll + k)
            return carry

        lax.fori_loop(0, trips, step, 0)
    else:
        trips = 0
    for p in range(lo + trips * unroll, hi):
        body(p)


class Level:
    def __init__(self, refs):
        self.wx, self.wy, self.wz, self.diag, self.inv = refs

    def build(self, frac, scale, lo, hi, wraps, unroll=10):
        half = 0.5 * scale
        self.wz[lo - 1] = half * (frac[lo - 1] + frac[lo])

        def plane(p):
            c, up, down = frac[p], frac[p + 1], frac[p - 1]
            total = 6.0 * c + up + down
            for axis, keep in ((1, self.wx), (0, self.wy)):
                after, before = ahead(c, axis), behind(c, axis)
                weight = half * (c + after)
                if wraps[axis]:
                    at = index_of(c.shape, axis)
                    last = at == c.shape[axis] - 1
                    weight = jnp.where(last, 0.0, weight)
                    after = jnp.where(last, 0.0, after)
                    before = jnp.where(at == 0, 0.0, before)
                keep[p] = weight
                total = total + after + before
            self.wz[p] = half * (c + up)
            diag = half * total
            self.diag[p] = diag
            self.inv[p] = jnp.where(c > 0.0, RELAXATION / jnp.where(c > 0.0, diag, 1.0), 0.0)

        planes(lo, hi, plane, unroll)

    def apply(self, q, p):
        c, wx, wy = q[p], self.wx[p], self.wy[p]
        near = wx * ahead(c, 1) + behind(wx * c, 1) + wy * ahead(c, 0) + behind(wy * c, 0)
        near = near + self.wz[p] * q[p + 1] + self.wz[p - 1] * q[p - 1]
        return c, self.diag[p] * c - near

    def first(self, rhs, out, lo, hi, unroll=10):
        def plane(p):
            out[p] = self.inv[p] * rhs[p]

        planes(lo, hi, plane, unroll)

    def sweep(self, q, rhs, out, lo, hi, unroll=10):
        def plane(p):
            c, applied = self.apply(q, p)
            out[p] = c + self.inv[p] * (rhs[p] - applied)

        planes(lo, hi, plane, unroll)

    def halved_residual(self, q, rhs, out, lo, hi, unroll=4):
        def pair(j):
            _, one = self.apply(q, lo + 2 * j)
            _, two = self.apply(q, lo + 2 * j + 1)
            out[j] = (rhs[lo + 2 * j] - one) + (rhs[lo + 2 * j + 1] - two)

        planes(0, (hi - lo) // 2, pair, unroll)


def halved(values, out, lo, hi):
    def pair(j):
        out[j] = values[lo + 2 * j] + values[lo + 2 * j + 1]

    planes(0, (hi - lo) // 2, pair)


def rows_of(ref, count):
    _, rows, lanes = ref.shape
    return ref[0:count].reshape(count * rows, lanes)


def gather_pairs(lanes, out_lanes, first, place, count):
    at, to = index_of((lanes, out_lanes), 0), index_of((lanes, out_lanes), 1) - place
    pair = jnp.remainder(at - first, lanes)
    hit = (pair >= 2 * to) & (pair <= 2 * to + 1) & (to >= 0) & (to < count)
    return jnp.where(hit, 0.125, 0.0).astype(F32)


def spread_pairs(lanes, out_lanes, first, start, count):
    at, to = index_of((lanes, out_lanes), 0) - first, index_of((lanes, out_lanes), 1)
    pair = jnp.remainder(to - start, out_lanes)
    hit = (pair >= 2 * at) & (pair <= 2 * at + 1) & (at >= 0) & (at < count)
    return jnp.where(hit, 1.0, 0.0).astype(F32)


def inside(okay):
    return jnp.where(okay, 1.0, 0.0).astype(F32)


def copies(pairs, sems):
    started = [pltpu.make_async_copy(a, b, sems.at[i]) for i, (a, b) in enumerate(pairs)]
    for copy in started:
        copy.start()
    return started


def pack_x_kernel(source, fraction, s, f, to_left, to_right, sems):
    for copy in copies(((source, s), (fraction, f)), sems):
        copy.wait()
    lane = index_of((16, 128), 1)
    for z in range(8):
        a, b, c, d = s[z], s[z + 8], f[z], f[z + 8]
        to_left[z] = jnp.where(
            lane < 32,
            a,
            jnp.where(lane < 64, turn(b, 32, 1), jnp.where(lane < 96, turn(c, 64, 1), turn(d, 96, 1))),
        )
        to_right[z] = jnp.where(
            lane >= 96,
            a,
            jnp.where(lane >= 64, turn(b, 96, 1), jnp.where(lane >= 32, turn(c, 64, 1), turn(d, 32, 1))),
        )


def pack_y_kernel(s, f, from_right, from_left, halo, to_low, to_high):
    ix = lax.axis_index("gx")
    left = inside(ix > 0)
    right = inside(ix < lax.axis_size("gx") - 1)
    lane = index_of((16, 128), 1)
    is_right = (lane < 32) | ((lane >= 64) & (lane < 96))
    for z in range(8):
        r, l = from_right[z] * right, from_left[z] * left
        halo[z] = jnp.where(is_right, r, l)
        halo[z + 8] = jnp.where(is_right, turn(r, 96, 1), turn(l, 32, 1))
    for k, ref in enumerate((s, f, halo)):
        to_low[k] = ref[:, 0:8, :]
        to_high[k] = ref[:, 8:16, :]


def pack_z_kernel(s, f, halo, y_low, y_high, to_low, to_high):
    iy, ny = lax.axis_index("gy"), lax.axis_size("gy")
    low, high = inside(iy > 0), inside(iy < ny - 1)
    for out, start in ((to_low, 0), (to_high, 9)):
        for k, ref in enumerate((s, f, halo)):
            for j in range(7):
                z = start + j
                out[k, j, 0:8, :] = y_low[k, z] * low
                out[k, j, 8:24, :] = ref[z]
                out[k, j, 24:32, :] = y_high[k, z] * high


def down_kernel(s, f, halo, y_low, y_high, z_low, z_high, *refs):
    kept, own1, f1, F1 = refs[:7], refs[7], refs[8], refs[9]
    F, Q, T, U, V, S, D0, *w0, sems = refs[10:]
    iz, iy = lax.axis_index("gz"), lax.axis_index("gy")
    nz, ny = lax.axis_size("gz"), lax.axis_size("gy")
    for p in (0, 31):
        S[p] = jnp.zeros((32, 256), F32)
        F[p] = jnp.zeros((32, 256), F32)

    def put(z0, y0, depth, height, scale, plane):
        edge = index_of((height, 128), 1)
        edge = (edge < 32) | (edge >= 96)

        def body(k):
            a, b, h = plane(k)
            if scale is not None:
                a, b, h = a * scale, b * scale, h * scale
            rows = pl.ds(y0, height)
            S[z0 + k, rows, 0:128] = a
            F[z0 + k, rows, 0:128] = b
            S[z0 + k, rows, 128:256] = jnp.where(edge, h, 0.0)
            F[z0 + k, rows, 128:256] = jnp.where(edge, turn(h, 64, 1), 0.0)

        planes(0, depth, body, 4)

    put(8, 8, 16, 16, None, lambda k: (s[k], f[k], halo[k]))
    for ref, y0, okay in ((y_low, 0, iy > 0), (y_high, 24, iy < ny - 1)):
        put(8, y0, 16, 8, inside(okay), lambda k, ref=ref: (ref[0, k], ref[1, k], ref[2, k]))
    for ref, z0, okay in ((z_low, 1, iz > 0), (z_high, 24, iz < nz - 1)):
        put(z0, 0, 7, 32, inside(okay), lambda k, ref=ref: (ref[0, k], ref[1, k], ref[2, k]))

    started = copies(((S.at[5:27], kept[0].at[5:27]),), sems)
    level = Level(w0)
    level.build(F, 1.0, 2, 30, (False, False))
    started += copies(tuple((a.at[5:27], b.at[5:27]) for a, b in zip(w0, kept[2:])), sems.at[1:6])
    level.first(S, Q, 2, 30)
    level.sweep(Q, S, D0, 3, 29)
    started += copies(((D0.at[5:27], kept[1].at[5:27]),), sems.at[6:7])
    level.halved_residual(D0, S, T, 4, 28)
    C = gather_pairs(256, 128, 0, 0, 128)

    def coarse(count, out, start):
        for j in range(count):
            for half in range(2):
                lanes = slice(128 * half, 128 * half + 128)
                V[j, half] = T[j, :, lanes]
                U[j, :, lanes] = V[j, half, pl.ds(0, 16, 2), :] + V[j, half, pl.ds(1, 16, 2), :]
        out[start : start + count] = matmul(rows_of(U, count), C).reshape(count, 16, 128)

    coarse(12, f1, 1)
    halved(F, T, 2, 30)
    coarse(14, F1, 0)
    for j in range(8):
        own1[j] = f1[3 + j, 4:12, :]
        own1[8 + j] = F1[3 + j, 4:12, :]
    for copy in started:
        copy.wait()


def down_one_kernel(f1, F1, payload, V, q1, d1, *w1):
    level = Level(w1)
    level.build(F1, 0.25, 1, 13, (False, False))
    level.first(f1, q1, 1, 13)
    level.sweep(q1, f1, d1, 2, 12)
    level.halved_residual(d1, f1, V, 3, 11)
    first = matmul(rows_of(V, 4), gather_pairs(128, 128, 112, 0, 48))
    halved(F1, V, 3, 11)
    both = first + matmul(rows_of(V, 4), gather_pairs(128, 128, 112, 64, 48))
    V[0:4] = both.reshape(4, 16, 128)
    for j in range(4):
        rows = V[j, pl.ds(4, 4, 2), :] + V[j, pl.ds(5, 4, 2), :]
        for d in range(32):
            payload[d, 4 * j : 4 * j + 4, :] = rows


def spread_y_kernel(own, y_low, y_high, to_low, to_high):
    iy, ny = lax.axis_index("gy"), lax.axis_size("gy")
    low, high = inside(iy > 0), inside(iy < ny - 1)
    for out, start in ((to_low, 0), (to_high, 2)):
        for k in range(2):
            for j in range(6):
                at, z = (6 * k + j) * 3, 8 * k + start + j
                out[at] = y_low[z] * low
                out[at + 1] = own[z]
                out[at + 2] = y_high[z] * high


def middle_kernel(got, own, y_low, y_high, payload, f2h, F2h, d2h, own_h, y_low_h, y_high_h, *refs):
    f2, F2, d2, q2, T, U, *w2, sems = refs
    started = copies(((own, own_h), (y_low, y_low_h), (y_high, y_high_h)), sems)
    keep = index_of((16, 128), 1) < 48
    zero = jnp.zeros((16, 128), F32)
    for ref in (f2, F2, q2, d2):
        ref[0] = zero
        ref[33] = zero
    for gy in range(4):
        for gz in range(8):
            block = got[gy * 8 + gz]
            rhs, frac = jnp.where(keep, block, 0.0), jnp.where(keep, turn(block, 64, 1), 0.0)
            for j in range(4):
                f2[1 + gz * 4 + j, 4 * gy : 4 * gy + 4, :] = rhs[4 * j : 4 * j + 4]
                F2[1 + gz * 4 + j, 4 * gy : 4 * gy + 4, :] = frac[4 * j : 4 * j + 4]
    started += copies(((f2, f2h), (F2, F2h)), sems.at[3:5])
    level = Level(w2)
    level.build(F2, 0.25**2, 1, 33, (True, False), 16)
    level.first(f2, q2, 1, 33, 16)
    level.sweep(q2, f2, d2, 1, 33, 16)
    started += copies(((d2, d2h),), sems.at[5:6])
    C = gather_pairs(128, 128, 8, 0, 16)
    for field in range(2):
        if field == 0:
            level.halved_residual(d2, f2, T, 1, 33, 2)
        else:
            halved(F2, T, 1, 33)
        U[...] = matmul(rows_of(T, 16), C).reshape(16, 16, 128)
        for zh in range(2):
            total = None
            for zl in range(8):
                z = zh * 8 + zl
                part = U[z, pl.ds(0, 8, 2), :] + U[z, pl.ds(1, 8, 2), :]
                part = turn(part, 16 * zl, 1)
                total = part if total is None else total + part
            for d in range(8):
                payload[d, 2 * field + zh] = total
    for copy in started:
        copy.wait()


def bottom(frac, rhs, half):
    shape = (8, 128)
    row, lane = index_of(shape, 0), index_of(shape, 1)
    used = lane < 32
    odd = jnp.remainder(row, 2) == 1
    y_near = jnp.where(odd, behind(frac, 0), ahead(frac, 0))
    z_up = jnp.where(row >= 6, 0.0, turn(frac, -2, 0))
    z_down = jnp.where(row < 2, 0.0, turn(frac, 2, 0))
    x_up = jnp.where(lane < 31, ahead(frac, 1), 0.0)
    x_down = jnp.where(lane > 0, behind(frac, 1), 0.0)
    diag = half * (6.0 * frac + y_near + z_up + z_down + x_up + x_down)
    after = jnp.where(lane < 31, -half * (frac + x_up), 0.0)
    before = jnp.where((lane > 0) & used, -half * (frac + x_down), 0.0)
    A, C, D, g = [], [], [], []
    for i in range(8):
        here = row == i
        z, y = i // 2, i % 2
        linked = (row == 2 * z + 1 - y) | (row == i - 2) | (row == i + 2)
        mine = jnp.broadcast_to(frac[i : i + 1], shape)
        block = jnp.where(here, diag, jnp.where(linked, -half * (mine + frac), 0.0))
        D.append(jnp.where(used, block, jnp.where(here, 1.0, 0.0)))
        A.append(jnp.where(here, before, 0.0))
        C.append(jnp.where(here, after, 0.0))
        g.append(jnp.broadcast_to(jnp.where(used[:1], rhs[i : i + 1], 0.0), shape))

    def pick(v, k):
        return jnp.broadcast_to(v[k : k + 1], shape)

    def divide(D, others):
        D, others = list(D), [list(o) for o in others]
        for k in range(8):
            inverse = 1.0 / pick(D[k], k)
            D[k] = D[k] * inverse
            for o in others:
                o[k] = o[k] * inverse
            for i in range(8):
                if i != k:
                    factor = pick(D[i], k)
                    D[i] = D[i] - factor * D[k]
                    for o in others:
                        o[i] = o[i] - factor * o[k]
        return others

    step = 1
    while step < 32:
        X, Y, h = divide(D, (A, C, g))
        Xl, Yl, hl = [[turn(v, step, 1) for v in o] for o in (X, Y, h)]
        Xr, Yr, hr = [[turn(v, -step, 1) for v in o] for o in (X, Y, h)]
        nA, nC, nD, ng = [], [], [], []
        for i in range(8):
            d, a, c, r = D[i], None, None, g[i]
            for k in range(8):
                pa, pc = pick(A[i], k), pick(C[i], k)
                d = d - (pa * Yl[k] + pc * Xr[k])
                r = r - (pa * hl[k] + pc * hr[k])
                a = -pa * Xl[k] if a is None else a - pa * Xl[k]
                c = -pc * Yr[k] if c is None else c - pc * Yr[k]
            nA.append(a)
            nC.append(c)
            nD.append(d)
            ng.append(r)
        A, C, D, g = nA, nC, nD, ng
        step *= 2
    (u,) = divide(D, (g,))
    out = jnp.zeros(shape, F32)
    for i in range(8):
        out = jnp.where((row == i) & used, u[i], out)
    return out


def up_kernel(got, *refs):
    far, refs = refs[:15], refs[15:]
    pressure, residual, refs = refs[0], refs[1], refs[2:]
    near, sems = refs[:15], refs[15]
    iz, iy, ix = lax.axis_index("gz"), lax.axis_index("gy"), lax.axis_index("gx")
    nz, ny = lax.axis_size("gz"), lax.axis_size("gy")
    start = jnp.clip(4 * iz - 4, 0, 20)

    def part(a, b):
        if b.shape == BIG:
            return a.at[5:27], b.at[5:27]
        if b.shape == WINDOW:
            return a.at[pl.ds(start, 14)], b
        return a, b

    started = copies(tuple(part(a, b) for a, b in zip(far, near)), sems)
    own1, y_low, y_high, z_low, z_high, f2, F2, d2, S, D0, wx0, wy0, wz0, g0, i0 = near
    refs = refs[16:]
    f3, F3, q3, d3, f4, F4, q4, d4 = refs[:8]
    w3, w4, w2, w1 = refs[8:13], refs[13:18], refs[18:23], refs[23:28]
    T3, g5, F5, qa2, qb2, T2, T2y, f1, F1, qa1, qb1, T1, U1, T0, U0, qa0, qb0, kept_p, kept_r, out_sems = refs[28:]
    lane = index_of((8, 128), 1)
    row = index_of((8, 128), 0)
    zero = jnp.zeros((8, 128), F32)

    for ref in (f3, F3, q3, d3):
        ref[0] = zero
        ref[17] = zero
    for ref in (f4, F4, q4, d4):
        ref[0] = zero
        ref[9] = zero
    for field, ref in enumerate((f3, F3)):
        for zh in range(2):
            blocks = [got[d, 2 * field + zh] for d in range(8)]
            for zl in range(8):
                total = turn(blocks[0], -16 * zl, 1)
                for d in range(1, 8):
                    total = jnp.where(lane >= 16 * d, turn(blocks[d], 16 * (d - zl), 1), total)
                ref[1 + zh * 8 + zl] = total

    three, four = Level(w3), Level(w4)
    three.build(F3, 0.25**3, 1, 17, (True, True), 16)
    three.first(f3, q3, 1, 17, 16)
    three.sweep(q3, f3, d3, 1, 17, 16)
    C = gather_pairs(128, 128, 0, 0, 64)
    for field in range(2):
        if field == 0:
            three.halved_residual(d3, f3, T3, 1, 17, 8)
        else:
            halved(F3, T3, 1, 17)
        T3[0:8] = matmul(rows_of(T3, 8), C).reshape(8, 8, 128)
        out = (f4, F4)[field]
        for j in range(8):
            out[1 + j] = zero
            out[1 + j, 0:4, :] = T3[j, pl.ds(0, 4, 2), :] + T3[j, pl.ds(1, 4, 2), :]
    four.build(F4, 0.25**4, 1, 9, (False, False), 8)
    four.first(f4, q4, 1, 9, 8)
    four.sweep(q4, f4, d4, 1, 9, 8)
    for field in range(2):
        if field == 0:
            four.halved_residual(d4, f4, T3, 1, 9, 4)
        else:
            halved(F4, T3, 1, 9)
        T3[0:4] = matmul(rows_of(T3, 4), C).reshape(4, 8, 128)
        out = (g5, F5)[field]
        for j in range(4):
            out[2 * j : 2 * j + 2, :] = T3[j, pl.ds(0, 2, 2), :] + T3[j, pl.ds(1, 2, 2), :]
    corr5 = bottom(F5[...], g5[...], 0.5 * 0.25**5)

    double = spread_pairs(128, 128, 0, 0, 64)
    wide = matmul(corr5, double)
    for z in range(4):
        plane = jnp.where(row < 2, wide[2 * z : 2 * z + 1], jnp.where(row < 4, wide[2 * z + 1 : 2 * z + 2], 0.0))
        for k in (0, 1):
            p = 1 + 2 * z + k
            q4[p] = d4[p] + jnp.where(F4[p] > 0.0, plane, 0.0)
    four.sweep(q4, f4, d4, 1, 9, 8)
    four.sweep(d4, f4, q4, 1, 9, 8)

    T3[0:8] = matmul(rows_of(q4.at[1:9], 8), double).reshape(8, 8, 128)
    for j in range(8):
        part = T3[j, 0:4, :]
        T3[8, pl.ds(0, 4, 2), :] = part
        T3[8, pl.ds(1, 4, 2), :] = part
        plane = T3[8]
        for k in (0, 1):
            p = 1 + 2 * j + k
            q3[p] = d3[p] + plane
    three.sweep(q3, f3, d3, 1, 17, 16)
    three.sweep(d3, f3, q3, 1, 17, 16)

    for copy in started[5:8]:
        copy.wait()
    two = Level(w2)
    two.build(F2, 0.25**2, 1, 13, (True, False), 12)
    shift = jnp.remainder(4 - 16 * ix, 128)
    for j in range(6):
        T2[0, j] = pltpu.roll(q3[1 + start // 2 + j], shift, 1)
    T2[1] = matmul(T2[0].reshape(48, 128), spread_pairs(128, 128, 0, 0, 24)).reshape(6, 8, 128)
    zero2 = jnp.zeros((16, 128), F32)
    for ref in (qa2, qb2):
        ref[0] = zero2
        ref[13] = zero2
    for j in range(6):
        rows = T2[1, j]
        T2y[j, pl.ds(0, 8, 2), :] = rows
        T2y[j, pl.ds(1, 8, 2), :] = rows
        plane = T2y[j]
        for k in (0, 1):
            p = 1 + 2 * j + k
            qa2[p] = d2[p] + jnp.where(F2[p] > 0.0, plane, 0.0)
    two.sweep(qa2, f2, qb2, 1, 13, 12)
    two.sweep(qb2, f2, qa2, 1, 13, 12)

    for copy in started[:5]:
        copy.wait()
    low, high, under, over = inside(iy > 0), inside(iy < ny - 1), inside(iz > 0), inside(iz < nz - 1)
    for k, ref in enumerate((f1, F1)):
        for z in range(8):
            ref[8 + z, 0:8, :] = y_low[8 * k + z] * low
            ref[8 + z, 8:16, :] = own1[8 * k + z]
            ref[8 + z, 16:24, :] = y_high[8 * k + z] * high
        for j in range(6):
            for t in range(3):
                at = (6 * k + j) * 3 + t
                ref[2 + j, 8 * t : 8 * t + 8, :] = z_low[at] * under
                ref[16 + j, 8 * t : 8 * t + 8, :] = z_high[at] * over
    one = Level(w1)
    one.build(F1, 0.25, 3, 21, (False, False))
    one.first(f1, qa1, 3, 21)
    one.sweep(qa1, f1, qb1, 4, 20)
    shift = jnp.remainder(4 - 4 * iy, 16)
    for j in range(8):
        at = jnp.clip(4 * iz - 2 + j, 0, 31) - start
        U1[j] = pltpu.roll(qa2[1 + at], shift, 0)
    U1[...] = matmul(rows_of(U1, 8), spread_pairs(128, 128, 0, 112, 48)).reshape(8, 16, 128)
    for j in range(8):
        part = U1[j, 0:12, :]
        T1[j, pl.ds(0, 12, 2), :] = part
        T1[j, pl.ds(1, 12, 2), :] = part
        plane = T1[j]
        for k in (0, 1):
            p = 4 + 2 * j + k
            qa1[p] = qb1[p] + jnp.where(F1[p] > 0.0, plane, 0.0)
    one.sweep(qa1, f1, qb1, 5, 19)
    one.sweep(qb1, f1, qa1, 6, 18)

    for copy in started[8:]:
        copy.wait()
    zero_level = Level((wx0, wy0, wz0, g0, i0))
    T0[...] = matmul(qa1[6:18].reshape(288, 128), spread_pairs(128, 256, 0, 0, 128)).reshape(12, 24, 256)

    def refine(j):
        for half in (0, 1):
            part = T0[j, 4:20, 128 * half : 128 * half + 128]
            U0[half, j, pl.ds(0, 16, 2), :] = part
            U0[half, j, pl.ds(1, 16, 2), :] = part
        plane = jnp.concatenate([U0[0, j], U0[1, j]], axis=1)
        for k in (0, 1):
            p = 4 + 2 * j + k
            qa0[p] = D0[p] + jnp.where(i0[p] > 0.0, plane, 0.0)

    planes(0, 12, refine, 4)
    zero_level.sweep(qa0, S, qb0, 6, 26)
    zero_level.sweep(qb0, S, qa0, 7, 25)

    def finish(p):
        c, applied = zero_level.apply(qa0, p)
        kept_p[p - 8] = c[8:24, 0:128]
        kept_r[p - 8] = (S[p] - applied)[8:24, 0:128]

    started = []
    for k in (0, 8):
        planes(8 + k, 16 + k, finish, 8)
        at = slice(k, k + 8)
        pairs = ((kept_p.at[at], pressure.at[at]), (kept_r.at[at], residual.at[at]))
        started += copies(pairs, out_sems.at[k // 4 : k // 4 + 2])
    for copy in started:
        copy.wait()


def call(kernel, name, ins, outs, scratch=()):
    anywhere = pl.BlockSpec(memory_space=pl.ANY)
    spec = {"v": pl.BlockSpec(memory_space=pltpu.VMEM), "n": pl.BlockSpec(memory_space=pltpu.VMEM), "h": anywhere}
    kind = {"v": pltpu.VMEM, "h": pltpu.HBM, "n": jax.ShapeDtypeStruct}
    space = {"v": pltpu.VMEM, "h": pltpu.HBM}

    def run(*args):
        args = [pltpu.with_memory_space_constraint(a, space[k]) if k in space else a for a, k in zip(args, ins)]
        return pl.pallas_call(
            kernel,
            out_shape=[kind[k](shape, F32) for k, shape in outs],
            in_specs=[spec[k] for k in ins],
            out_specs=[spec[k] for k, _ in outs],
            scratch_shapes=[pltpu.VMEM(shape, F32) if isinstance(shape, tuple) else shape for shape in scratch],
            compiler_params=pltpu.CompilerParams(vmem_limit_bytes=VMEM_LIMIT),
            name=name,
        )(*args)

    return run


def ring(axis, step):
    size = lax.axis_size(axis)
    return [(i, (i + step) % size) for i in range(size)]


def exchange(to_low, to_high, axis, reach=1):
    return lax.ppermute(to_high, axis, ring(axis, reach)), lax.ppermute(to_low, axis, ring(axis, -reach))


BIG, MID, MID2, WIDE1 = (32, 32, 256), (14, 16, 128), (34, 16, 128), (24, 24, 128)
WINDOW = (14, 16, 128)
THREE, FOUR = (18, 8, 128), (10, 8, 128)


def local(source, fraction):
    def dma(count):
        return pltpu.SemaphoreType.DMA((count,))

    own, strip = (16, 16, 128), (8, 16, 128)
    s, f, to_left, to_right = call(
        pack_x_kernel, "pack_x", "hh", [("v", own)] * 2 + [("v", strip)] * 2, [dma(2)]
    )(source, fraction)
    from_left, from_right = exchange(to_left, to_right, "gx")
    rows = (3, 16, 8, 128)
    halo, to_low, to_high = call(pack_y_kernel, "pack_y", "vvvv", [("v", own), ("v", rows), ("v", rows)])(
        s, f, from_right, from_left
    )
    y_low, y_high = exchange(to_low, to_high, "gy")
    layers = (3, 7, 32, 128)
    to_low, to_high = call(pack_z_kernel, "pack_z", "vvvvv", [("v", layers)] * 2)(s, f, halo, y_low, y_high)
    z_low, z_high = exchange(to_low, to_high, "gz")
    *fine, own1, f1, F1 = call(
        down_kernel,
        "down",
        "vvvvvvv",
        [("h", BIG)] * 7 + [("v", (16, 8, 128)), ("v", MID), ("v", MID)],
        [BIG, BIG, (14, 32, 256), (14, 16, 256), (14, 2, 32, 128)] + [BIG] * 7 + [dma(7)],
    )(s, f, halo, y_low, y_high, z_low, z_high)
    y_low, y_high = exchange(own1, own1, "gy")
    (payload,) = call(
        down_one_kernel, "down_one", "vv", [("v", (32, 16, 128))], [(4, 16, 128)] + [MID] * 7
    )(f1, F1)
    got = lax.all_to_all(payload, ("gy", "gz"), 0, 0)
    layers = (36, 8, 128)
    to_low, to_high = call(spread_y_kernel, "spread_y", "vvv", [("v", layers)] * 2)(own1, y_low, y_high)
    z_low, z_high = exchange(to_low, to_high, "gz")
    payload, *kept = call(
        middle_kernel,
        "middle",
        "vvvv",
        [("v", (8, 4, 8, 128))] + [("h", MID2)] * 3 + [("h", (16, 8, 128))] * 3,
        [MID2] * 4 + [(16, 16, 128), (16, 16, 128)] + [MID2] * 5 + [dma(6)],
    )(got, own1, y_low, y_high)
    got = lax.all_to_all(payload, "gx", 0, 0)
    f2, F2, d2, own1, y_low, y_high = kept
    kept = [own1, y_low, y_high, z_low, z_high, f2, F2, d2, *fine]
    pressure, residual = call(
        up_kernel,
        "up",
        "v" + "h" * 15,
        [("h", own)] * 2,
        [(16, 8, 128)] * 3
        + [layers] * 2
        + [WINDOW] * 3
        + [BIG] * 7
        + [dma(15)]
        + [THREE] * 4
        + [FOUR] * 4
        + [THREE] * 5
        + [FOUR] * 5
        + [WINDOW] * 5
        + [WIDE1] * 5
        + [(9, 8, 128), (8, 128), (8, 128), WINDOW, WINDOW, (2, 6, 8, 128), (6, 16, 128)]
        + [WIDE1] * 4
        + [(8, 24, 128), (8, 16, 128), (12, 24, 256), (2, 12, 32, 128), BIG, BIG, own, own, dma(4)],
    )(got, *kept)
    return (pressure, residual)


def solution(mesh):
    spec = P("gz", "gy", "gx")
    return jax.shard_map(
        local, mesh=mesh, in_specs=(spec, spec), out_specs=(spec, spec), check_vma=False
    )
```

```python
import jax
import jax.numpy as jnp
from jax import lax
from jax.experimental import pallas as pl
from jax.experimental.pallas import tpu as pltpu
from jax.sharding import PartitionSpec as P

RELAXATION = 0.8
F32 = jnp.float32
VMEM_LIMIT = 32 * 1024 * 1024


def turn(v, shift, axis):
    size = v.shape[axis]
    shift = shift % size
    return v if shift == 0 else pltpu.roll(v, shift, axis)


def ahead(v, axis):
    return turn(v, -1, axis)


def behind(v, axis):
    return turn(v, 1, axis)


def index_of(shape, axis):
    return lax.broadcasted_iota(jnp.int32, shape, axis)


def matmul(a, b):
    b = b.astype(jnp.bfloat16)
    total = None
    for part in range(3):
        piece = a.astype(jnp.bfloat16)
        product = lax.dot_general(piece, b, (((1,), (0,)), ((), ())), preferred_element_type=F32)
        total = product if total is None else total + product
        if part < 2:
            a = a - piece.astype(F32)
    return total


def planes(lo, hi, body, unroll=10):
    trips = (hi - lo) // unroll
    if trips > 1:

        def step(i, carry):
            for k in range(unroll):
                body(lo + i * unroll + k)
            return carry

        lax.fori_loop(0, trips, step, 0)
    else:
        trips = 0
    for p in range(lo + trips * unroll, hi):
        body(p)


class Level:
    def __init__(self, refs):
        self.wx, self.wy, self.wz, self.diag, self.inv = refs

    def build(self, frac, scale, lo, hi, wraps, unroll=10):
        half = 0.5 * scale
        self.wz[lo - 1] = half * (frac[lo - 1] + frac[lo])

        def plane(p):
            c, up, down = frac[p], frac[p + 1], frac[p - 1]
            total = 6.0 * c + up + down
            for axis, keep in ((1, self.wx), (0, self.wy)):
                after, before = ahead(c, axis), behind(c, axis)
                weight = half * (c + after)
                if wraps[axis]:
                    at = index_of(c.shape, axis)
                    last = at == c.shape[axis] - 1
                    weight = jnp.where(last, 0.0, weight)
                    after = jnp.where(last, 0.0, after)
                    before = jnp.where(at == 0, 0.0, before)
                keep[p] = weight
                total = total + after + before
            self.wz[p] = half * (c + up)
            diag = half * total
            self.diag[p] = diag
            self.inv[p] = jnp.where(c > 0.0, RELAXATION / jnp.where(c > 0.0, diag, 1.0), 0.0)

        planes(lo, hi, plane, unroll)

    def near(self, q, p):
        c, wx, wy = q[p], self.wx[p], self.wy[p]
        total = wx * ahead(c, 1) + behind(wx * c, 1) + wy * ahead(c, 0) + behind(wy * c, 0)
        return c, total + self.wz[p] * q[p + 1] + self.wz[p - 1] * q[p - 1]

    def residual(self, q, rhs, p):
        c, near = self.near(q, p)
        return c, rhs[p] + near - self.diag[p] * c

    def first(self, rhs, out, lo, hi, unroll=10):
        def plane(p):
            out[p] = self.inv[p] * rhs[p]

        planes(lo, hi, plane, unroll)

    def sweep(self, q, rhs, out, lo, hi, unroll=10):
        def plane(p):
            c, near = self.near(q, p)
            out[p] = (1.0 - RELAXATION) * c + self.inv[p] * (rhs[p] + near)

        planes(lo, hi, plane, unroll)

    def halved_residual(self, q, rhs, out, lo, hi, unroll=4):
        def pair(j):
            _, one = self.residual(q, rhs, lo + 2 * j)
            _, two = self.residual(q, rhs, lo + 2 * j + 1)
            out[j] = one + two

        planes(0, (hi - lo) // 2, pair, unroll)


def halved(values, out, lo, hi):
    def pair(j):
        out[j] = values[lo + 2 * j] + values[lo + 2 * j + 1]

    planes(0, (hi - lo) // 2, pair)


def rows_of(ref, count):
    _, rows, lanes = ref.shape
    return ref[0:count].reshape(count * rows, lanes)


def gather_pairs(lanes, out_lanes, first, place, count):
    at, to = index_of((lanes, out_lanes), 0), index_of((lanes, out_lanes), 1) - place
    pair = jnp.remainder(at - first, lanes)
    hit = (pair >= 2 * to) & (pair <= 2 * to + 1) & (to >= 0) & (to < count)
    return jnp.where(hit, 0.125, 0.0).astype(F32)


def spread_pairs(lanes, out_lanes, first, start, count):
    at, to = index_of((lanes, out_lanes), 0) - first, index_of((lanes, out_lanes), 1)
    pair = jnp.remainder(to - start, out_lanes)
    hit = (pair >= 2 * at) & (pair <= 2 * at + 1) & (at >= 0) & (at < count)
    return jnp.where(hit, 1.0, 0.0).astype(F32)


def inside(okay):
    return jnp.where(okay, 1.0, 0.0).astype(F32)


def copies(pairs, sems):
    started = [pltpu.make_async_copy(a, b, sems.at[i]) for i, (a, b) in enumerate(pairs)]
    for copy in started:
        copy.start()
    return started


def pack_x_kernel(source, fraction, s, f, to_left, to_right, sems):
    quarters = [slice(4 * k, 4 * k + 4) for k in range(4)]
    for copy in copies([(a.at[k], b.at[k]) for a, b in ((source, s), (fraction, f)) for k in quarters], sems):
        copy.wait()
    lane = index_of((16, 128), 1)
    for z in range(8):
        a, b, c, d = s[z], s[z + 8], f[z], f[z + 8]
        to_left[z] = jnp.where(
            lane < 32,
            a,
            jnp.where(lane < 64, turn(b, 32, 1), jnp.where(lane < 96, turn(c, 64, 1), turn(d, 96, 1))),
        )
        to_right[z] = jnp.where(
            lane >= 96,
            a,
            jnp.where(lane >= 64, turn(b, 96, 1), jnp.where(lane >= 32, turn(c, 64, 1), turn(d, 32, 1))),
        )


def pack_y_kernel(s, f, from_right, from_left, halo, to_low, to_high):
    ix = lax.axis_index("gx")
    left = inside(ix > 0)
    right = inside(ix < lax.axis_size("gx") - 1)
    lane = index_of((16, 128), 1)
    is_right = (lane < 32) | ((lane >= 64) & (lane < 96))
    for z in range(8):
        r, l = from_right[z] * right, from_left[z] * left
        halo[z] = jnp.where(is_right, r, l)
        halo[z + 8] = jnp.where(is_right, turn(r, 96, 1), turn(l, 32, 1))
    for k, ref in enumerate((s, f, halo)):
        to_low[k] = ref[:, 0:8, :]
        to_high[k] = ref[:, 8:16, :]


def pack_z_kernel(s, f, halo, y_low, y_high, to_low, to_high):
    iy, ny = lax.axis_index("gy"), lax.axis_size("gy")
    low, high = inside(iy > 0), inside(iy < ny - 1)
    for out, start in ((to_low, 0), (to_high, 9)):
        for k, ref in enumerate((s, f, halo)):
            for j in range(7):
                z = start + j
                out[k, j, 0:8, :] = y_low[k, z] * low
                out[k, j, 8:24, :] = ref[z]
                out[k, j, 24:32, :] = y_high[k, z] * high


def put(S, F, z0, y0, depth, height, scale, plane):
    edge = index_of((height, 128), 1)
    edge = (edge < 32) | (edge >= 96)

    def body(k):
        a, b, h = plane(k)
        if scale is not None:
            a, b, h = a * scale, b * scale, h * scale
        rows = pl.ds(y0, height)
        S[z0 + k, rows, 0:128] = a
        F[z0 + k, rows, 0:128] = b
        S[z0 + k, rows, 128:256] = jnp.where(edge, h, 0.0)
        F[z0 + k, rows, 128:256] = jnp.where(edge, turn(h, 64, 1), 0.0)

    planes(0, depth, body, 4)


SOURCE, DIAG, WEIGHTS, RESULT = (0, 1), (1, 2), (2, 6), (6, 7)
INNER = {SOURCE: ((8, 24),), DIAG: ((9, 23),), WEIGHTS: ((9, 23),), RESULT: ((10, 22),)}
OUTER = {
    SOURCE: ((6, 8), (24, 26)),
    DIAG: ((8, 9), (23, 24)),
    WEIGHTS: ((5, 9), (23, 27)),
    RESULT: ((5, 10), (22, 27)),
}


def layers_of(source, target, spans, which):
    return [
        (source.at[a:b, lo:hi], target.at[a:b, lo:hi]) for a, b in which for lo, hi in spans[(a, b)]
    ]


def split(fine):
    return fine.at[0], fine.at[6], [fine.at[k] for k in (2, 3, 4, 1, 5)]


def coarse_rows(T, U, V, count):
    for j in range(count):
        for half in range(2):
            lanes = slice(128 * half, 128 * half + 128)
            V[j, half] = T[j, :, lanes]
            U[j, :, lanes] = V[j, half, pl.ds(0, 16, 2), :] + V[j, half, pl.ds(1, 16, 2), :]
    return matmul(rows_of(U, count), gather_pairs(256, 128, 0, 0, 128)).reshape(count, 16, 128)


def inner_kernel(s, f, halo, y_low, y_high, *refs):
    fine, F, Q, f1, F1, kept, T, U, V, sems = refs
    S, D0, w0 = split(fine)
    iy, ny = lax.axis_index("gy"), lax.axis_size("gy")
    put(S, F, 8, 8, 16, 16, None, lambda k: (s[k], f[k], halo[k]))
    for ref, y0, okay in ((y_low, 0, iy > 0), (y_high, 24, iy < ny - 1)):
        put(S, F, 8, y0, 16, 8, inside(okay), lambda k, ref=ref: (ref[0, k], ref[1, k], ref[2, k]))
    level = Level(w0)
    level.build(F, 1.0, 9, 23, (False, False), 7)
    level.first(S, Q, 9, 23, 14)
    level.sweep(Q, S, D0, 10, 22, 6)
    started = copies(layers_of(fine, kept, INNER, INNER), sems)
    level.halved_residual(D0, S, T, 12, 20)
    halved(F, T.at[4:12], 8, 24)
    both = coarse_rows(T, U, V, 12)
    f1[5:9] = both[0:4]
    F1[3:11] = both[4:12]
    for copy in started:
        copy.wait()


def down_kernel(z_low, z_high, *refs):
    fine, F, Q, f1, F1, kept, own1, payload = refs[5:13]
    T, U, V, V1, q1, d1, *w1, sems = refs[13:]
    S, D0, w0 = split(fine)
    iz, nz = lax.axis_index("gz"), lax.axis_size("gz")
    for p in (0, 31):
        S[p] = jnp.zeros((32, 256), F32)
        F[p] = jnp.zeros((32, 256), F32)
    for ref, z0, okay in ((z_low, 1, iz > 0), (z_high, 24, iz < nz - 1)):
        put(S, F, z0, 0, 7, 32, inside(okay), lambda k, ref=ref: (ref[0, k], ref[1, k], ref[2, k]))

    level = Level(w0)
    for lo, hi in ((2, 9), (23, 30)):
        level.build(F, 1.0, lo, hi, (False, False), 7)
        level.first(S, Q, lo, hi, 7)
    started = copies(layers_of(fine, kept, OUTER, (SOURCE, DIAG, WEIGHTS)), sems)
    level.sweep(Q, S, D0, 3, 10, 7)
    level.sweep(Q, S, D0, 22, 29, 7)
    started += copies(layers_of(fine, kept, OUTER, (RESULT,)), sems.at[6:8])
    level.halved_residual(D0, S, T, 4, 12)
    level.halved_residual(D0, S, T.at[4:8], 20, 28)
    halved(F, T.at[8:11], 2, 8)
    halved(F, T.at[11:14], 24, 30)
    both = coarse_rows(T, U, V, 14)
    f1[1:5] = both[0:4]
    f1[9:13] = both[4:8]
    F1[0:3] = both[8:11]
    F1[11:14] = both[11:14]
    for j in range(8):
        own1[j] = f1[3 + j, 4:12, :]
        own1[8 + j] = F1[3 + j, 4:12, :]

    level = Level(w1)
    level.build(F1, 0.25, 1, 13, (False, False))
    level.first(f1, q1, 1, 13)
    level.sweep(q1, f1, d1, 2, 12)
    level.halved_residual(d1, f1, V1, 3, 11)
    first = matmul(rows_of(V1, 4), gather_pairs(128, 128, 112, 0, 48))
    halved(F1, V1, 3, 11)
    both = first + matmul(rows_of(V1, 4), gather_pairs(128, 128, 112, 64, 48))
    V1[0:4] = both.reshape(4, 16, 128)
    for j in range(4):
        rows = V1[j, pl.ds(4, 4, 2), :] + V1[j, pl.ds(5, 4, 2), :]
        for d in range(32):
            payload[d, 4 * j : 4 * j + 4, :] = rows
    for copy in started:
        copy.wait()


def spread_y_kernel(own, y_low, y_high, to_low, to_high, rows):
    iy, ny = lax.axis_index("gy"), lax.axis_size("gy")
    low, high = inside(iy > 0), inside(iy < ny - 1)
    for out, start, depth in ((to_low, 0, 6), (to_high, 2, 6), (rows, 0, 8)):
        for k in range(2):
            for j in range(depth):
                at, z = (depth * k + j) * 3, 8 * k + start + j
                out[at] = y_low[z] * low
                out[at + 1] = own[z]
                out[at + 2] = y_high[z] * high


def wide_kernel(rows, z_low, z_high, f1, d1, *refs):
    w1, F1, q1 = refs[:5], refs[5], refs[6]
    iz, nz = lax.axis_index("gz"), lax.axis_size("gz")
    under, over = inside(iz > 0), inside(iz < nz - 1)
    for k, ref in enumerate((f1, F1)):
        for t in range(3):
            at = slice(8 * t, 8 * t + 8)
            for z in range(8):
                ref[8 + z, at, :] = rows[(8 * k + z) * 3 + t]
            for j in range(6):
                ref[2 + j, at, :] = z_low[(6 * k + j) * 3 + t] * under
                ref[16 + j, at, :] = z_high[(6 * k + j) * 3 + t] * over
    one = Level(w1)
    one.build(F1, 0.25, 3, 21, (False, False), 9)
    one.first(f1, q1, 3, 21, 18)
    one.sweep(q1, f1, d1, 4, 20, 8)


def middle_kernel(got, after, payload, f2h, F2h, d2h, *refs):
    f2, F2, d2, q2, T, U, *w2, sems = refs
    keep = index_of((16, 128), 1) < 48
    zero = jnp.zeros((16, 128), F32)
    for ref in (f2, F2, q2, d2):
        ref[0] = zero
        ref[33] = zero
    for gy in range(4):
        for gz in range(8):
            block = got[gy * 8 + gz]
            rhs, frac = jnp.where(keep, block, 0.0), jnp.where(keep, turn(block, 64, 1), 0.0)
            for j in range(4):
                f2[1 + gz * 4 + j, 4 * gy : 4 * gy + 4, :] = rhs[4 * j : 4 * j + 4]
                F2[1 + gz * 4 + j, 4 * gy : 4 * gy + 4, :] = frac[4 * j : 4 * j + 4]
    started = copies(((f2, f2h), (F2, F2h)), sems)
    level = Level(w2)
    level.build(F2, 0.25**2, 1, 33, (True, False), 16)
    level.first(f2, q2, 1, 33, 16)
    level.sweep(q2, f2, d2, 1, 33, 16)
    started += copies(((d2, d2h),), sems.at[2:3])
    C = gather_pairs(128, 128, 8, 0, 16)
    for field in range(2):
        if field == 0:
            level.halved_residual(d2, f2, T, 1, 33, 2)
        else:
            halved(F2, T, 1, 33)
        U[...] = matmul(rows_of(T, 16), C).reshape(16, 16, 128)
        for zh in range(2):
            total = None
            for zl in range(8):
                z = zh * 8 + zl
                part = U[z, pl.ds(0, 8, 2), :] + U[z, pl.ds(1, 8, 2), :]
                part = turn(part, 16 * zl, 1)
                total = part if total is None else total + part
            for d in range(8):
                payload[d, 2 * field + zh] = total
    for copy in started:
        copy.wait()


def bottom(frac, rhs, half):
    shape = (8, 128)
    row, lane = index_of(shape, 0), index_of(shape, 1)
    used = lane < 32
    odd = jnp.remainder(row, 2) == 1
    y_near = jnp.where(odd, behind(frac, 0), ahead(frac, 0))
    z_up = jnp.where(row >= 6, 0.0, turn(frac, -2, 0))
    z_down = jnp.where(row < 2, 0.0, turn(frac, 2, 0))
    x_up = jnp.where(lane < 31, ahead(frac, 1), 0.0)
    x_down = jnp.where(lane > 0, behind(frac, 1), 0.0)
    diag = half * (6.0 * frac + y_near + z_up + z_down + x_up + x_down)
    after = jnp.where(lane < 31, -half * (frac + x_up), 0.0)
    before = jnp.where((lane > 0) & used, -half * (frac + x_down), 0.0)
    A, C, D, g = [], [], [], []
    for i in range(8):
        here = row == i
        z, y = i // 2, i % 2
        linked = (row == 2 * z + 1 - y) | (row == i - 2) | (row == i + 2)
        mine = jnp.broadcast_to(frac[i : i + 1], shape)
        block = jnp.where(here, diag, jnp.where(linked, -half * (mine + frac), 0.0))
        D.append(jnp.where(used, block, jnp.where(here, 1.0, 0.0)))
        A.append(jnp.where(here, before, 0.0))
        C.append(jnp.where(here, after, 0.0))
        g.append(jnp.broadcast_to(jnp.where(used[:1], rhs[i : i + 1], 0.0), shape))

    def pick(v, k):
        return jnp.broadcast_to(v[k : k + 1], shape)

    def divide(D, others):
        D, others = list(D), [list(o) for o in others]
        for k in range(8):
            inverse = 1.0 / pick(D[k], k)
            D[k] = D[k] * inverse
            for o in others:
                o[k] = o[k] * inverse
            for i in range(8):
                if i != k:
                    factor = pick(D[i], k)
                    D[i] = D[i] - factor * D[k]
                    for o in others:
                        o[i] = o[i] - factor * o[k]
        return others

    step = 1
    while step < 32:
        X, Y, h = divide(D, (A, C, g))
        Xl, Yl, hl = [[turn(v, step, 1) for v in o] for o in (X, Y, h)]
        Xr, Yr, hr = [[turn(v, -step, 1) for v in o] for o in (X, Y, h)]
        nA, nC, nD, ng = [], [], [], []
        for i in range(8):
            d, a, c, r = D[i], None, None, g[i]
            for k in range(8):
                pa, pc = pick(A[i], k), pick(C[i], k)
                d = d - (pa * Yl[k] + pc * Xr[k])
                r = r - (pa * hl[k] + pc * hr[k])
                a = -pa * Xl[k] if a is None else a - pa * Xl[k]
                c = -pc * Yr[k] if c is None else c - pc * Yr[k]
            nA.append(a)
            nC.append(c)
            nD.append(d)
            ng.append(r)
        A, C, D, g = nA, nC, nD, ng
        step *= 2
    (u,) = divide(D, (g,))
    out = jnp.zeros(shape, F32)
    for i in range(8):
        out = jnp.where((row == i) & used, u[i], out)
    return out


def up_kernel(got, *refs):
    f1, qb1, *w1 = refs[:7]
    refs = refs[7:]
    far, refs = refs[:5], refs[5:]
    pressure, residual, refs = refs[0], refs[1], refs[2:]
    near, sems = refs[:4], refs[4]
    iz, iy, ix = lax.axis_index("gz"), lax.axis_index("gy"), lax.axis_index("gx")
    nz, ny = lax.axis_size("gz"), lax.axis_size("gy")
    start = jnp.clip(4 * iz - 4, 0, 20)

    pairs = [(a.at[pl.ds(start, 14)], b) for a, b in zip(far[:3], near)]
    for which in ((WEIGHTS, RESULT, SOURCE), (DIAG,)):
        pairs += layers_of(far[3], near[3], INNER, which) + layers_of(far[4], near[3], OUTER, which)
    started = copies(pairs, sems)
    f2, F2, d2, fine = near
    S, D0, w0 = split(fine)
    refs = refs[5:]
    f3, F3, q3, d3, f4, F4, q4, d4 = refs[:8]
    w3, w4, w2 = refs[8:13], refs[13:18], refs[18:23]
    T3, g5, F5, qa2, qb2, T2, T2y, qa1, qc1, T1, U1, T0, U0, qa0, qb0, kept_p, kept_r, out_sems = refs[23:]
    lane = index_of((8, 128), 1)
    row = index_of((8, 128), 0)
    zero = jnp.zeros((8, 128), F32)

    for ref in (f3, F3, q3, d3):
        ref[0] = zero
        ref[17] = zero
    for ref in (f4, F4, q4, d4):
        ref[0] = zero
        ref[9] = zero
    for field, ref in enumerate((f3, F3)):
        for zh in range(2):
            blocks = [got[d, 2 * field + zh] for d in range(8)]
            for zl in range(8):
                total = turn(blocks[0], -16 * zl, 1)
                for d in range(1, 8):
                    total = jnp.where(lane >= 16 * d, turn(blocks[d], 16 * (d - zl), 1), total)
                ref[1 + zh * 8 + zl] = total

    three, four = Level(w3), Level(w4)
    three.build(F3, 0.25**3, 1, 17, (True, True), 16)
    three.first(f3, q3, 1, 17, 16)
    three.sweep(q3, f3, d3, 1, 17, 16)
    C = gather_pairs(128, 128, 0, 0, 64)
    for field in range(2):
        if field == 0:
            three.halved_residual(d3, f3, T3, 1, 17, 8)
        else:
            halved(F3, T3, 1, 17)
        T3[0:8] = matmul(rows_of(T3, 8), C).reshape(8, 8, 128)
        out = (f4, F4)[field]
        for j in range(8):
            out[1 + j] = zero
            out[1 + j, 0:4, :] = T3[j, pl.ds(0, 4, 2), :] + T3[j, pl.ds(1, 4, 2), :]
    four.build(F4, 0.25**4, 1, 9, (False, False), 8)
    four.first(f4, q4, 1, 9, 8)
    four.sweep(q4, f4, d4, 1, 9, 8)
    for field in range(2):
        if field == 0:
            four.halved_residual(d4, f4, T3, 1, 9, 4)
        else:
            halved(F4, T3, 1, 9)
        T3[0:4] = matmul(rows_of(T3, 4), C).reshape(4, 8, 128)
        out = (g5, F5)[field]
        for j in range(4):
            out[2 * j : 2 * j + 2, :] = T3[j, pl.ds(0, 2, 2), :] + T3[j, pl.ds(1, 2, 2), :]
    corr5 = bottom(F5[...], g5[...], 0.5 * 0.25**5)

    double = spread_pairs(128, 128, 0, 0, 64)
    wide = matmul(corr5, double)
    for z in range(4):
        plane = jnp.where(row < 2, wide[2 * z : 2 * z + 1], jnp.where(row < 4, wide[2 * z + 1 : 2 * z + 2], 0.0))
        for k in (0, 1):
            p = 1 + 2 * z + k
            q4[p] = d4[p] + jnp.where(F4[p] > 0.0, plane, 0.0)
    four.sweep(q4, f4, d4, 1, 9, 8)
    four.sweep(d4, f4, q4, 1, 9, 8)

    T3[0:8] = matmul(rows_of(q4.at[1:9], 8), double).reshape(8, 8, 128)
    for j in range(8):
        part = T3[j, 0:4, :]
        T3[8, pl.ds(0, 4, 2), :] = part
        T3[8, pl.ds(1, 4, 2), :] = part
        plane = T3[8]
        for k in (0, 1):
            p = 1 + 2 * j + k
            q3[p] = d3[p] + plane
    three.sweep(q3, f3, d3, 1, 17, 16)
    three.sweep(d3, f3, q3, 1, 17, 16)

    for copy in started[:3]:
        copy.wait()
    two = Level(w2)
    two.build(F2, 0.25**2, 1, 13, (True, False), 12)
    shift = jnp.remainder(4 - 16 * ix, 128)
    for j in range(6):
        T2[0, j] = pltpu.roll(q3[1 + start // 2 + j], shift, 1)
    T2[1] = matmul(T2[0].reshape(48, 128), spread_pairs(128, 128, 0, 0, 24)).reshape(6, 8, 128)
    zero2 = jnp.zeros((16, 128), F32)
    for ref in (qa2, qb2):
        ref[0] = zero2
        ref[13] = zero2
    for j in range(6):
        rows = T2[1, j]
        T2y[j, pl.ds(0, 8, 2), :] = rows
        T2y[j, pl.ds(1, 8, 2), :] = rows
        plane = T2y[j]
        for k in (0, 1):
            p = 1 + 2 * j + k
            qa2[p] = d2[p] + jnp.where(F2[p] > 0.0, plane, 0.0)
    two.sweep(qa2, f2, qb2, 1, 13, 12)
    two.sweep(qb2, f2, qa2, 1, 13, 12)

    one = Level(w1)
    shift = jnp.remainder(4 - 4 * iy, 16)
    for j in range(8):
        at = jnp.clip(4 * iz - 2 + j, 0, 31) - start
        U1[j] = pltpu.roll(qa2[1 + at], shift, 0)
    U1[...] = matmul(rows_of(U1, 8), spread_pairs(128, 128, 0, 112, 48)).reshape(8, 16, 128)
    for j in range(8):
        part = U1[j, 0:12, :]
        T1[j, pl.ds(0, 12, 2), :] = part
        T1[j, pl.ds(1, 12, 2), :] = part
        plane = T1[j]
        for k in (0, 1):
            p = 4 + 2 * j + k
            qa1[p] = qb1[p] + jnp.where(one.inv[p] > 0.0, plane, 0.0)
    one.sweep(qa1, f1, qc1, 5, 19, 7)
    one.sweep(qc1, f1, qa1, 6, 18, 6)

    for copy in started[3:12]:
        copy.wait()
    zero_level = Level(w0)
    T0[...] = matmul(qa1[6:18].reshape(288, 128), spread_pairs(128, 256, 0, 0, 128)).reshape(12, 24, 256)

    def refine(j):
        for half in (0, 1):
            part = T0[j, 4:20, 128 * half : 128 * half + 128]
            U0[half, j, pl.ds(0, 16, 2), :] = part
            U0[half, j, pl.ds(1, 16, 2), :] = part
        plane = jnp.concatenate([U0[0, j], U0[1, j]], axis=1)
        for k in (0, 1):
            p = 4 + 2 * j + k
            qa0[p] = D0[p] + jnp.where(zero_level.inv[p] > 0.0, plane, 0.0)

    planes(0, 12, refine, 4)
    zero_level.sweep(qa0, S, qb0, 6, 26)
    zero_level.sweep(qb0, S, qa0, 7, 25)

    def finish(p):
        c, rest = zero_level.residual(qa0, S, p)
        kept_p[p - 8] = c[8:24, 0:128]
        kept_r[p - 8] = rest[8:24, 0:128]

    for copy in started[12:]:
        copy.wait()
    started = []
    for k in (0, 8):
        planes(8 + k, 16 + k, finish, 8)
        at = slice(k, k + 8)
        pairs = ((kept_p.at[at], pressure.at[at]), (kept_r.at[at], residual.at[at]))
        started += copies(pairs, out_sems.at[k // 4 : k // 4 + 2])
    for copy in started:
        copy.wait()


def call(kernel, name, ins, outs, scratch=(), aliases=()):
    anywhere = pl.BlockSpec(memory_space=pl.ANY)
    spec = {"v": pl.BlockSpec(memory_space=pltpu.VMEM), "n": pl.BlockSpec(memory_space=pltpu.VMEM), "h": anywhere}
    kind = {"v": pltpu.VMEM, "h": pltpu.HBM, "n": jax.ShapeDtypeStruct}
    space = {"v": pltpu.VMEM, "h": pltpu.HBM}

    def run(*args):
        args = [pltpu.with_memory_space_constraint(a, space[k]) if k in space else a for a, k in zip(args, ins)]
        return pl.pallas_call(
            kernel,
            out_shape=[kind[k](shape, F32) for k, shape in outs],
            in_specs=[spec[k] for k in ins],
            out_specs=[spec[k] for k, _ in outs],
            scratch_shapes=[pltpu.VMEM(shape, F32) if isinstance(shape, tuple) else shape for shape in scratch],
            compiler_params=pltpu.CompilerParams(vmem_limit_bytes=VMEM_LIMIT),
            input_output_aliases=dict(aliases),
            name=name,
        )(*args)

    return run


def ring(axis, step):
    size = lax.axis_size(axis)
    return [(i, (i + step) % size) for i in range(size)]


def exchange(to_low, to_high, axis, reach=1):
    return lax.ppermute(to_high, axis, ring(axis, reach)), lax.ppermute(to_low, axis, ring(axis, -reach))


FINE, BIG, MID, MID2, WIDE1 = (7, 32, 32, 256), (32, 32, 256), (14, 16, 128), (34, 16, 128), (24, 24, 128)
WINDOW = (14, 16, 128)
THREE, FOUR = (18, 8, 128), (10, 8, 128)


def local(source, fraction):
    def dma(count):
        return pltpu.SemaphoreType.DMA((count,))

    own, strip = (16, 16, 128), (8, 16, 128)
    s, f, to_left, to_right = call(
        pack_x_kernel, "pack_x", "hh", [("v", own)] * 2 + [("v", strip)] * 2, [dma(8)]
    )(source, fraction)
    from_left, from_right = exchange(to_left, to_right, "gx")
    rows = (3, 16, 8, 128)
    halo, to_low, to_high = call(pack_y_kernel, "pack_y", "vvvv", [("v", own), ("v", rows), ("v", rows)])(
        s, f, from_right, from_left
    )
    y_halos = exchange(to_low, to_high, "gy")
    layers = (3, 7, 32, 128)
    to_low, to_high = call(pack_z_kernel, "pack_z", "vvvvv", [("v", layers)] * 2)(s, f, halo, *y_halos)
    z_low, z_high = exchange(to_low, to_high, "gz")
    coarse = [(14, 32, 256), (14, 16, 256), (14, 2, 32, 128)]
    *inner, fine_inner = call(
        inner_kernel,
        "inner",
        "vvvvv",
        [("v", FINE), ("v", BIG), ("v", BIG), ("v", MID), ("v", MID), ("h", FINE)],
        [*coarse, dma(4)],
    )(s, f, halo, *y_halos)
    fine, own1, payload = call(
        down_kernel,
        "down",
        "v" * 7,
        [("v", FINE), ("v", BIG), ("v", BIG), ("v", MID), ("v", MID), ("h", FINE)]
        + [("v", (16, 8, 128)), ("v", (32, 16, 128))],
        [*coarse, (4, 16, 128)] + [MID] * 7 + [dma(8)],
        [(2 + i, i) for i in range(5)],
    )(z_low, z_high, *inner)[5:]
    y_low, y_high = exchange(own1, own1, "gy")
    got = lax.all_to_all(payload, ("gy", "gz"), 0, 0)
    layers = (36, 8, 128)
    to_low, to_high, rows = call(
        spread_y_kernel, "spread_y", "vvv", [("v", layers)] * 2 + [("v", (48, 8, 128))]
    )(own1, y_low, y_high)
    z_low, z_high = exchange(to_low, to_high, "gz")
    one = call(wide_kernel, "wide", "vvv", [("v", WIDE1)] * 7, [WIDE1] * 2)(rows, z_low, z_high)
    payload, *kept = call(
        middle_kernel,
        "middle",
        "vv",
        [("v", (8, 4, 8, 128))] + [("h", MID2)] * 3,
        [MID2] * 4 + [(16, 16, 128), (16, 16, 128)] + [MID2] * 5 + [dma(3)],
    )(got, rows)
    got = lax.all_to_all(payload, "gx", 0, 0)
    pressure, residual = call(
        up_kernel,
        "up",
        "v" * 8 + "h" * 5,
        [("h", own)] * 2,
        [WINDOW] * 3
        + [FINE]
        + [dma(15)]
        + [THREE] * 4
        + [FOUR] * 4
        + [THREE] * 5
        + [FOUR] * 5
        + [WINDOW] * 5
        + [(9, 8, 128), (8, 128), (8, 128), WINDOW, WINDOW, (2, 6, 8, 128), (6, 16, 128)]
        + [WIDE1] * 2
        + [(8, 24, 128), (8, 16, 128), (12, 24, 256), (2, 12, 32, 128), BIG, BIG, own, own, dma(4)],
    )(got, *one, *kept, fine_inner, fine)
    return (pressure, residual)


def solution(mesh):
    spec = P("gz", "gy", "gx")
    return jax.shard_map(
        local, mesh=mesh, in_specs=(spec, spec), out_specs=(spec, spec), check_vma=False
    )
```

```python
import jax
import jax.numpy as jnp
from jax import lax
from jax.experimental import pallas as pl
from jax.experimental.pallas import tpu as pltpu
from jax.sharding import PartitionSpec as P

RELAXATION = 0.8
F32 = jnp.float32
VMEM_LIMIT = 32 * 1024 * 1024


def turn(v, shift, axis):
    size = v.shape[axis]
    shift = shift % size
    return v if shift == 0 else pltpu.roll(v, shift, axis)


def ahead(v, axis):
    return turn(v, -1, axis)


def behind(v, axis):
    return turn(v, 1, axis)


def index_of(shape, axis):
    return lax.broadcasted_iota(jnp.int32, shape, axis)


def matmul(a, b):
    b = b.astype(jnp.bfloat16)
    total = None
    for part in range(3):
        piece = a.astype(jnp.bfloat16)
        product = lax.dot_general(piece, b, (((1,), (0,)), ((), ())), preferred_element_type=F32)
        total = product if total is None else total + product
        if part < 2:
            a = a - piece.astype(F32)
    return total


def planes(lo, hi, body, unroll=10):
    trips = (hi - lo) // unroll
    if trips > 1:

        def step(i, carry):
            for k in range(unroll):
                body(lo + i * unroll + k)
            return carry

        lax.fori_loop(0, trips, step, 0)
    else:
        trips = 0
    for p in range(lo + trips * unroll, hi):
        body(p)


class Level:
    def __init__(self, refs):
        self.wx, self.wy, self.wz, self.diag, self.inv = refs

    def build(self, frac, scale, lo, hi, wraps, unroll=10):
        half = 0.5 * scale
        self.wz[lo - 1] = half * (frac[lo - 1] + frac[lo])

        def plane(p):
            c, up, down = frac[p], frac[p + 1], frac[p - 1]
            total = 6.0 * c + up + down
            for axis, keep in ((1, self.wx), (0, self.wy)):
                after, before = ahead(c, axis), behind(c, axis)
                weight = half * (c + after)
                if wraps[axis]:
                    at = index_of(c.shape, axis)
                    last = at == c.shape[axis] - 1
                    weight = jnp.where(last, 0.0, weight)
                    after = jnp.where(last, 0.0, after)
                    before = jnp.where(at == 0, 0.0, before)
                keep[p] = weight
                total = total + after + before
            self.wz[p] = half * (c + up)
            diag = half * total
            self.diag[p] = diag
            self.inv[p] = jnp.where(c > 0.0, RELAXATION / jnp.where(c > 0.0, diag, 1.0), 0.0)

        planes(lo, hi, plane, unroll)

    def near(self, q, p):
        c, wx, wy = q[p], self.wx[p], self.wy[p]
        total = wx * ahead(c, 1) + behind(wx * c, 1) + wy * ahead(c, 0) + behind(wy * c, 0)
        return c, total + self.wz[p] * q[p + 1] + self.wz[p - 1] * q[p - 1]

    def residual(self, q, rhs, p):
        c, near = self.near(q, p)
        return c, rhs[p] + near - self.diag[p] * c

    def first(self, rhs, out, lo, hi, unroll=10):
        def plane(p):
            out[p] = self.inv[p] * rhs[p]

        planes(lo, hi, plane, unroll)

    def sweep(self, q, rhs, out, lo, hi, unroll=10):
        def plane(p):
            c, near = self.near(q, p)
            out[p] = (1.0 - RELAXATION) * c + self.inv[p] * (rhs[p] + near)

        planes(lo, hi, plane, unroll)

    def halved_residual(self, q, rhs, out, lo, hi, unroll=4):
        def pair(j):
            _, one = self.residual(q, rhs, lo + 2 * j)
            _, two = self.residual(q, rhs, lo + 2 * j + 1)
            out[j] = one + two

        planes(0, (hi - lo) // 2, pair, unroll)


def halved(values, out, lo, hi):
    def pair(j):
        out[j] = values[lo + 2 * j] + values[lo + 2 * j + 1]

    planes(0, (hi - lo) // 2, pair)


def rows_of(ref, count):
    _, rows, lanes = ref.shape
    return ref[0:count].reshape(count * rows, lanes)


def gather_pairs(lanes, out_lanes, first, place, count):
    at, to = index_of((lanes, out_lanes), 0), index_of((lanes, out_lanes), 1) - place
    pair = jnp.remainder(at - first, lanes)
    hit = (pair >= 2 * to) & (pair <= 2 * to + 1) & (to >= 0) & (to < count)
    return jnp.where(hit, 0.125, 0.0).astype(F32)


def spread_pairs(lanes, out_lanes, first, start, count):
    at, to = index_of((lanes, out_lanes), 0) - first, index_of((lanes, out_lanes), 1)
    pair = jnp.remainder(to - start, out_lanes)
    hit = (pair >= 2 * at) & (pair <= 2 * at + 1) & (at >= 0) & (at < count)
    return jnp.where(hit, 1.0, 0.0).astype(F32)


def inside(okay):
    return jnp.where(okay, 1.0, 0.0).astype(F32)


def copies(pairs, sems):
    started = [pltpu.make_async_copy(a, b, sems.at[i]) for i, (a, b) in enumerate(pairs)]
    for copy in started:
        copy.start()
    return started


def pack_x_kernel(source, fraction, s, f, to_left, to_right, sems):
    quarters = [slice(4 * k, 4 * k + 4) for k in range(4)]
    for copy in copies([(a.at[k], b.at[k]) for a, b in ((source, s), (fraction, f)) for k in quarters], sems):
        copy.wait()
    lane = index_of((16, 128), 1)
    for z in range(8):
        a, b, c, d = s[z], s[z + 8], f[z], f[z + 8]
        to_left[z] = jnp.where(
            lane < 32,
            a,
            jnp.where(lane < 64, turn(b, 32, 1), jnp.where(lane < 96, turn(c, 64, 1), turn(d, 96, 1))),
        )
        to_right[z] = jnp.where(
            lane >= 96,
            a,
            jnp.where(lane >= 64, turn(b, 96, 1), jnp.where(lane >= 32, turn(c, 64, 1), turn(d, 32, 1))),
        )


ROWS = (6, 7, 7)
ROWS_ONE = (5, 6)


def tiles_of(rows, own):
    return [
        (k, depth, t)
        for k in range(len(rows))
        for depth in range(1, rows[k] + 1)
        for t in range(own + 2)
        if 0 < t <= own or depth < rows[k]
    ]


TILES, TILES_ONE = tiles_of(ROWS, 2), tiles_of(ROWS_ONE, 1)


def unpack_y(message, out, rows, low):
    at = 0
    for k, count in enumerate(rows):
        for j in range(8):
            source = j - (8 - count) if low else j
            if 0 <= source < count:
                out[k, :, j, :] = message[at + source]
            else:
                out[k, :, j, :] = jnp.zeros(message.shape[1:], F32)
        at += count


def pack_y_kernel(s, f, from_right, from_left, halo, to_low, to_high):
    ix = lax.axis_index("gx")
    left = inside(ix > 0)
    right = inside(ix < lax.axis_size("gx") - 1)
    lane = index_of((16, 128), 1)
    is_right = (lane < 32) | ((lane >= 64) & (lane < 96))
    for z in range(8):
        r, l = from_right[z] * right, from_left[z] * left
        halo[z] = jnp.where(is_right, r, l)
        halo[z + 8] = jnp.where(is_right, turn(r, 96, 1), turn(l, 32, 1))
    at = 0
    for count, ref in zip(ROWS, (s, f, halo)):
        for j in range(count):
            to_low[at + j] = ref[:, j, :]
            to_high[at + j] = ref[:, 16 - count + j, :]
        at += count


def pack_z_kernel(s, f, halo, from_low, from_high, to_low, to_high, y_low, y_high):
    unpack_y(from_low, y_low, ROWS, True)
    unpack_y(from_high, y_high, ROWS, False)
    iy, ny = lax.axis_index("gy"), lax.axis_size("gy")
    low, high = inside(iy > 0), inside(iy < ny - 1)
    for i, (k, depth, t) in enumerate(TILES):
        for out, z in ((to_low, depth - 1), (to_high, 16 - depth)):
            if t == 0:
                out[i] = y_low[k, z] * low
            elif t == 3:
                out[i] = y_high[k, z] * high
            else:
                out[i] = (s, f, halo)[k][z, 8 * t - 8 : 8 * t, :]


def put(S, F, z0, y0, depth, height, scale, plane):
    edge = index_of((height, 128), 1)
    edge = (edge < 32) | (edge >= 96)

    def body(k):
        a, b, h = plane(k)
        if scale is not None:
            a, b, h = a * scale, b * scale, h * scale
        rows = pl.ds(y0, height)
        S[z0 + k, rows, 0:128] = a
        F[z0 + k, rows, 0:128] = b
        S[z0 + k, rows, 128:256] = jnp.where(edge, h, 0.0)
        F[z0 + k, rows, 128:256] = jnp.where(edge, turn(h, 64, 1), 0.0)

    planes(0, depth, body, 4)


SOURCE, DIAG, WEIGHTS, INVERSE, RESULT = (0, 1), (1, 2), (2, 5), (5, 6), (6, 7)
INNER = {SOURCE: ((8, 24),), DIAG: ((9, 23),), WEIGHTS: ((9, 23),), INVERSE: ((9, 23),), RESULT: ((10, 22),)}
OUTER = {
    SOURCE: ((6, 8), (24, 26)),
    DIAG: ((8, 9), (23, 24)),
    WEIGHTS: ((5, 9), (23, 26)),
    INVERSE: ((5, 9), (23, 27)),
    RESULT: ((5, 10), (22, 27)),
}


def layers_of(source, target, spans, which):
    return [
        (source.at[a:b, lo:hi], target.at[a:b, lo:hi]) for a, b in which for lo, hi in spans[(a, b)]
    ]


def split(fine):
    return fine.at[0], fine.at[6], [fine.at[k] for k in (2, 3, 4, 1, 5)]


def coarse_rows(T, U, V, count):
    for j in range(count):
        for half in range(2):
            lanes = slice(128 * half, 128 * half + 128)
            V[j, half] = T[j, :, lanes]
            U[j, :, lanes] = V[j, half, pl.ds(0, 16, 2), :] + V[j, half, pl.ds(1, 16, 2), :]
    return matmul(rows_of(U, count), gather_pairs(256, 128, 0, 0, 128)).reshape(count, 16, 128)


def inner_kernel(s, f, halo, from_low, from_high, *refs):
    fine, F, Q, f1, F1, kept, T, U, V, y_low, y_high, sems = refs
    unpack_y(from_low, y_low, ROWS, True)
    unpack_y(from_high, y_high, ROWS, False)
    S, D0, w0 = split(fine)
    iy, ny = lax.axis_index("gy"), lax.axis_size("gy")
    put(S, F, 8, 8, 16, 16, None, lambda k: (s[k], f[k], halo[k]))
    for ref, y0, okay in ((y_low, 0, iy > 0), (y_high, 24, iy < ny - 1)):
        put(S, F, 8, y0, 16, 8, inside(okay), lambda k, ref=ref: (ref[0, k], ref[1, k], ref[2, k]))
    level = Level(w0)
    level.build(F, 1.0, 9, 23, (False, False), 7)
    level.first(S, Q, 9, 23, 14)
    level.sweep(Q, S, D0, 10, 22, 6)
    started = copies(layers_of(fine, kept, INNER, INNER), sems)
    level.halved_residual(D0, S, T, 12, 20)
    halved(F, T.at[4:12], 8, 24)
    both = coarse_rows(T, U, V, 12)
    f1[5:9] = both[0:4]
    F1[3:11] = both[4:12]
    for copy in started:
        copy.wait()


def down_kernel(z_low, z_high, *refs):
    fine, F, Q, f1, F1, kept, own1, to_low, to_high, payload = refs[5:15]
    T, U, V, V1, q1, d1, *w1, sems = refs[15:]
    S, D0, w0 = split(fine)
    iz, nz = lax.axis_index("gz"), lax.axis_size("gz")
    for p in (0, 31):
        S[p] = jnp.zeros((32, 256), F32)
        F[p] = jnp.zeros((32, 256), F32)
    zero = jnp.zeros((8, 128), F32)

    def layer(ref, depth):
        tiles = [[ref[TILES.index((k, depth, t))] if (k, depth, t) in TILES else zero for t in range(4)] for k in range(3)]
        return [jnp.concatenate(four, axis=0) for four in tiles]

    for ref, z0, okay in ((z_low, 1, iz > 0), (z_high, 24, iz < nz - 1)):
        put(S, F, z0, 0, 7, 32, inside(okay), lambda k, ref=ref, z0=z0: layer(ref, 7 - k if z0 == 1 else 1 + k))

    level = Level(w0)
    for lo, hi in ((2, 9), (23, 30)):
        level.build(F, 1.0, lo, hi, (False, False), 7)
        level.first(S, Q, lo, hi, 7)
    started = copies(layers_of(fine, kept, OUTER, (SOURCE, DIAG, WEIGHTS, INVERSE)), sems)
    level.sweep(Q, S, D0, 3, 10, 7)
    level.sweep(Q, S, D0, 22, 29, 7)
    started += copies(layers_of(fine, kept, OUTER, (RESULT,)), sems.at[8:10])
    level.halved_residual(D0, S, T, 4, 12)
    level.halved_residual(D0, S, T.at[4:8], 20, 28)
    halved(F, T.at[8:11], 2, 8)
    halved(F, T.at[11:14], 24, 30)
    both = coarse_rows(T, U, V, 14)
    f1[1:5] = both[0:4]
    f1[9:13] = both[4:8]
    F1[0:3] = both[8:11]
    F1[11:14] = both[11:14]
    for j in range(8):
        own1[j] = f1[3 + j, 4:12, :]
        own1[8 + j] = F1[3 + j, 4:12, :]
    at = 0
    for ref, count in zip((f1, F1), ROWS_ONE):
        for j in range(count):
            to_low[at + j] = ref[3:11, 4 + j, :]
            to_high[at + j] = ref[3:11, 12 - count + j, :]
        at += count

    level = Level(w1)
    level.build(F1, 0.25, 1, 13, (False, False))
    level.first(f1, q1, 1, 13)
    level.sweep(q1, f1, d1, 2, 12)
    level.halved_residual(d1, f1, V1, 3, 11)
    first = matmul(rows_of(V1, 4), gather_pairs(128, 128, 112, 0, 48))
    halved(F1, V1, 3, 11)
    both = first + matmul(rows_of(V1, 4), gather_pairs(128, 128, 112, 64, 48))
    V1[0:4] = both.reshape(4, 16, 128)
    for j in range(4):
        rows = V1[j, pl.ds(4, 4, 2), :] + V1[j, pl.ds(5, 4, 2), :]
        for d in range(32):
            payload[d, 4 * j : 4 * j + 4, :] = rows
    for copy in started:
        copy.wait()


def spread_y_kernel(own, from_low, from_high, to_low, to_high, rows, y_low, y_high):
    unpack_y(from_low, y_low, ROWS_ONE, True)
    unpack_y(from_high, y_high, ROWS_ONE, False)
    iy, ny = lax.axis_index("gy"), lax.axis_size("gy")
    low, high = inside(iy > 0), inside(iy < ny - 1)
    for k in range(2):
        for z in range(8):
            at = (8 * k + z) * 3
            rows[at] = y_low[k, z] * low
            rows[at + 1] = own[8 * k + z]
            rows[at + 2] = y_high[k, z] * high
    for i, (k, depth, t) in enumerate(TILES_ONE):
        to_low[i] = rows[(8 * k + depth - 1) * 3 + t]
        to_high[i] = rows[(8 * k + 8 - depth) * 3 + t]


def wide_kernel(rows, z_low, z_high, f1, d1, *refs):
    w1, F1, q1 = refs[:5], refs[5], refs[6]
    iz, nz = lax.axis_index("gz"), lax.axis_size("gz")
    under, over = inside(iz > 0), inside(iz < nz - 1)
    zero = jnp.zeros((8, 128), F32)
    for k, ref in enumerate((f1, F1)):
        for t in range(3):
            at = slice(8 * t, 8 * t + 8)
            for z in range(8):
                ref[8 + z, at, :] = rows[(8 * k + z) * 3 + t]
            for depth in range(1, 7):
                there = (k, depth, t) in TILES_ONE
                i = TILES_ONE.index((k, depth, t)) if there else 0
                ref[8 - depth, at, :] = z_low[i] * under if there else zero
                ref[15 + depth, at, :] = z_high[i] * over if there else zero
    one = Level(w1)
    one.build(F1, 0.25, 3, 21, (False, False), 9)
    one.first(f1, q1, 3, 21, 18)
    one.sweep(q1, f1, d1, 4, 20, 8)


def window_start():
    return jnp.clip(4 * lax.axis_index("gz") - 4, 0, 20)


def middle_kernel(got, after, payload, f2h, F2h, d2h, *refs):
    *refs, part, part_sems = refs
    f2, F2, d2, q2, T, U, *w2, sems = refs
    keep = index_of((16, 128), 1) < 48
    zero = jnp.zeros((16, 128), F32)
    for ref in (f2, F2, q2, d2):
        ref[0] = zero
        ref[33] = zero
    for gy in range(4):
        for gz in range(8):
            block = got[gy * 8 + gz]
            rhs, frac = jnp.where(keep, block, 0.0), jnp.where(keep, turn(block, 64, 1), 0.0)
            for j in range(4):
                f2[1 + gz * 4 + j, 4 * gy : 4 * gy + 4, :] = rhs[4 * j : 4 * j + 4]
                F2[1 + gz * 4 + j, 4 * gy : 4 * gy + 4, :] = frac[4 * j : 4 * j + 4]
    at = pl.ds(window_start(), 14)
    started = copies(((f2.at[at], f2h), (F2.at[at], F2h)), sems)
    level = Level(w2)
    C = gather_pairs(128, 128, 8, 0, 16)

    def send(field):
        U[...] = matmul(rows_of(T, 16), C).reshape(16, 16, 128)
        for zh in range(2):
            total = None
            for zl in range(8):
                z = zh * 8 + zl
                rows = U[z, pl.ds(0, 8, 2), :] + U[z, pl.ds(1, 8, 2), :]
                rows = turn(rows, 16 * zl, 1)
                total = rows if total is None else total + rows
            part[2 * field + zh] = total
        at = slice(2 * field, 2 * field + 2)
        return copies([(part.at[at], payload.at[d, at]) for d in range(8)], part_sems.at[8 * field : 8 * field + 8])

    halved(F2, T, 1, 33)
    started += send(1)
    level.build(F2, 0.25**2, 1, 33, (True, False), 16)
    level.first(f2, q2, 1, 33, 16)
    level.sweep(q2, f2, d2, 1, 33, 16)
    started += copies(((d2.at[at], d2h),), sems.at[2:3])
    level.halved_residual(d2, f2, T, 1, 33, 8)
    started += send(0)
    for copy in started:
        copy.wait()


def bottom(frac, rhs, half):
    shape = (8, 128)
    row, lane = index_of(shape, 0), index_of(shape, 1)
    used = lane < 32
    odd = jnp.remainder(row, 2) == 1
    y_near = jnp.where(odd, behind(frac, 0), ahead(frac, 0))
    z_up = jnp.where(row >= 6, 0.0, turn(frac, -2, 0))
    z_down = jnp.where(row < 2, 0.0, turn(frac, 2, 0))
    x_up = jnp.where(lane < 31, ahead(frac, 1), 0.0)
    x_down = jnp.where(lane > 0, behind(frac, 1), 0.0)
    diag = half * (6.0 * frac + y_near + z_up + z_down + x_up + x_down)
    after = jnp.where(lane < 31, -half * (frac + x_up), 0.0)
    before = jnp.where((lane > 0) & used, -half * (frac + x_down), 0.0)
    A, C, D, g = [], [], [], []
    for i in range(8):
        here = row == i
        z, y = i // 2, i % 2
        linked = (row == 2 * z + 1 - y) | (row == i - 2) | (row == i + 2)
        mine = jnp.broadcast_to(frac[i : i + 1], shape)
        block = jnp.where(here, diag, jnp.where(linked, -half * (mine + frac), 0.0))
        D.append(jnp.where(used, block, jnp.where(here, 1.0, 0.0)))
        A.append(jnp.where(here, before, 0.0))
        C.append(jnp.where(here, after, 0.0))
        g.append(jnp.broadcast_to(jnp.where(used[:1], rhs[i : i + 1], 0.0), shape))

    def pick(v, k):
        return jnp.broadcast_to(v[k : k + 1], shape)

    def divide(D, others):
        D, others = list(D), [list(o) for o in others]
        for k in range(8):
            inverse = 1.0 / pick(D[k], k)
            D[k] = D[k] * inverse
            for o in others:
                o[k] = o[k] * inverse
            for i in range(8):
                if i != k:
                    factor = pick(D[i], k)
                    D[i] = D[i] - factor * D[k]
                    for o in others:
                        o[i] = o[i] - factor * o[k]
        return others

    step = 1
    while step < 32:
        X, Y, h = divide(D, (A, C, g))
        Xl, Yl, hl = [[turn(v, step, 1) for v in o] for o in (X, Y, h)]
        Xr, Yr, hr = [[turn(v, -step, 1) for v in o] for o in (X, Y, h)]
        nA, nC, nD, ng = [], [], [], []
        for i in range(8):
            d, a, c, r = D[i], None, None, g[i]
            for k in (i,) if step == 1 else range(8):
                pa, pc = pick(A[i], k), pick(C[i], k)
                d = d - (pa * Yl[k] + pc * Xr[k])
                r = r - (pa * hl[k] + pc * hr[k])
                a = -pa * Xl[k] if a is None else a - pa * Xl[k]
                c = -pc * Yr[k] if c is None else c - pc * Yr[k]
            nA.append(a)
            nC.append(c)
            nD.append(d)
            ng.append(r)
        A, C, D, g = nA, nC, nD, ng
        step *= 2
    (u,) = divide(D, (g,))
    out = jnp.zeros(shape, F32)
    for i in range(8):
        out = jnp.where((row == i) & used, u[i], out)
    return out


def up_kernel(got, *refs):
    f1, qb1, *w1 = refs[:7]
    refs = refs[7:]
    far, refs = refs[:5], refs[5:]
    pressure, residual, refs = refs[0], refs[1], refs[2:]
    near, sems = refs[:4], refs[4]
    iz, iy, ix = lax.axis_index("gz"), lax.axis_index("gy"), lax.axis_index("gx")
    nz, ny = lax.axis_size("gz"), lax.axis_size("gy")
    start = window_start()
    pairs = list(zip(far[:3], near))
    for which in ((RESULT, INVERSE), (WEIGHTS, SOURCE), (DIAG,)):
        pairs += layers_of(far[3], near[3], INNER, which) + layers_of(far[4], near[3], OUTER, which)
    started = copies(pairs, sems)
    f2, F2, d2, fine = near
    S, D0, w0 = split(fine)
    refs = refs[5:]
    f3, F3, q3, d3, f4, F4, q4, d4 = refs[:8]
    w3, w4, w2 = refs[8:13], refs[13:18], refs[18:23]
    T3, g5, F5, qa2, qb2, T2, T2y, qa1, qc1, T1, U1, T0, U0, qa0, qb0, kept_p, kept_r, out_sems = refs[23:]
    lane = index_of((8, 128), 1)
    row = index_of((8, 128), 0)
    zero = jnp.zeros((8, 128), F32)

    for ref in (f3, F3, q3, d3):
        ref[0] = zero
        ref[17] = zero
    for ref in (f4, F4, q4, d4):
        ref[0] = zero
        ref[9] = zero
    for field, ref in enumerate((f3, F3)):
        for zh in range(2):
            blocks = [got[d, 2 * field + zh] for d in range(8)]
            for zl in range(8):
                total = turn(blocks[0], -16 * zl, 1)
                for d in range(1, 8):
                    total = jnp.where(lane >= 16 * d, turn(blocks[d], 16 * (d - zl), 1), total)
                ref[1 + zh * 8 + zl] = total

    three, four = Level(w3), Level(w4)
    three.build(F3, 0.25**3, 1, 17, (True, True), 16)
    three.first(f3, q3, 1, 17, 16)
    three.sweep(q3, f3, d3, 1, 17, 16)
    C = gather_pairs(128, 128, 0, 0, 64)
    for field in range(2):
        if field == 0:
            three.halved_residual(d3, f3, T3, 1, 17, 8)
        else:
            halved(F3, T3, 1, 17)
        T3[0:8] = matmul(rows_of(T3, 8), C).reshape(8, 8, 128)
        out = (f4, F4)[field]
        for j in range(8):
            out[1 + j] = zero
            out[1 + j, 0:4, :] = T3[j, pl.ds(0, 4, 2), :] + T3[j, pl.ds(1, 4, 2), :]
    four.build(F4, 0.25**4, 1, 9, (False, False), 8)
    four.first(f4, q4, 1, 9, 8)
    four.sweep(q4, f4, d4, 1, 9, 8)
    for field in range(2):
        if field == 0:
            four.halved_residual(d4, f4, T3, 1, 9, 4)
        else:
            halved(F4, T3, 1, 9)
        T3[0:4] = matmul(rows_of(T3, 4), C).reshape(4, 8, 128)
        out = (g5, F5)[field]
        for j in range(4):
            out[2 * j : 2 * j + 2, :] = T3[j, pl.ds(0, 2, 2), :] + T3[j, pl.ds(1, 2, 2), :]
    corr5 = bottom(F5[...], g5[...], 0.5 * 0.25**5)

    double = spread_pairs(128, 128, 0, 0, 64)
    wide = matmul(corr5, double)
    for z in range(4):
        plane = jnp.where(row < 2, wide[2 * z : 2 * z + 1], jnp.where(row < 4, wide[2 * z + 1 : 2 * z + 2], 0.0))
        for k in (0, 1):
            p = 1 + 2 * z + k
            q4[p] = d4[p] + jnp.where(F4[p] > 0.0, plane, 0.0)
    four.sweep(q4, f4, d4, 1, 9, 8)
    four.sweep(d4, f4, q4, 1, 9, 8)

    T3[0:8] = matmul(rows_of(q4.at[1:9], 8), double).reshape(8, 8, 128)
    for j in range(8):
        part = T3[j, 0:4, :]
        T3[8, pl.ds(0, 4, 2), :] = part
        T3[8, pl.ds(1, 4, 2), :] = part
        plane = T3[8]
        for k in (0, 1):
            p = 1 + 2 * j + k
            q3[p] = d3[p] + plane
    three.sweep(q3, f3, d3, 1, 17, 16)
    three.sweep(d3, f3, q3, 1, 17, 16)

    for copy in started[:3]:
        copy.wait()
    two = Level(w2)
    two.build(F2, 0.25**2, 1, 13, (True, False), 12)
    shift = jnp.remainder(4 - 16 * ix, 128)
    for j in range(6):
        T2[0, j] = pltpu.roll(q3[1 + start // 2 + j], shift, 1)
    T2[1] = matmul(T2[0].reshape(48, 128), spread_pairs(128, 128, 0, 0, 24)).reshape(6, 8, 128)
    zero2 = jnp.zeros((16, 128), F32)
    for ref in (qa2, qb2):
        ref[0] = zero2
        ref[13] = zero2
    for j in range(6):
        rows = T2[1, j]
        T2y[j, pl.ds(0, 8, 2), :] = rows
        T2y[j, pl.ds(1, 8, 2), :] = rows
        plane = T2y[j]
        for k in (0, 1):
            p = 1 + 2 * j + k
            qa2[p] = d2[p] + jnp.where(F2[p] > 0.0, plane, 0.0)
    two.sweep(qa2, f2, qb2, 1, 13, 12)
    two.sweep(qb2, f2, qa2, 1, 13, 12)

    one = Level(w1)
    shift = jnp.remainder(4 - 4 * iy, 16)
    for j in range(8):
        at = jnp.clip(4 * iz - 2 + j, 0, 31) - start
        U1[j] = pltpu.roll(qa2[1 + at], shift, 0)
    U1[...] = matmul(rows_of(U1, 8), spread_pairs(128, 128, 0, 112, 48)).reshape(8, 16, 128)
    for j in range(8):
        part = U1[j, 0:12, :]
        T1[j, pl.ds(0, 12, 2), :] = part
        T1[j, pl.ds(1, 12, 2), :] = part
        plane = T1[j]
        for k in (0, 1):
            p = 4 + 2 * j + k
            qa1[p] = qb1[p] + jnp.where(one.inv[p] > 0.0, plane, 0.0)
    one.sweep(qa1, f1, qc1, 5, 19, 7)
    one.sweep(qc1, f1, qa1, 6, 18, 6)

    zero_level = Level(w0)
    T0[...] = matmul(qa1[6:18].reshape(288, 128), spread_pairs(128, 256, 0, 0, 128)).reshape(12, 24, 256)

    def refine(j):
        for half in (0, 1):
            part = T0[j, 4:20, 128 * half : 128 * half + 128]
            U0[half, j, pl.ds(0, 16, 2), :] = part
            U0[half, j, pl.ds(1, 16, 2), :] = part
        plane = jnp.concatenate([U0[0, j], U0[1, j]], axis=1)
        for k in (0, 1):
            p = 4 + 2 * j + k
            qa0[p] = D0[p] + jnp.where(zero_level.inv[p] > 0.0, plane, 0.0)

    for copy in started[3:9]:
        copy.wait()
    planes(0, 12, refine, 4)
    for copy in started[9:15]:
        copy.wait()
    zero_level.sweep(qa0, S, qb0, 6, 26)
    zero_level.sweep(qb0, S, qa0, 7, 25)

    def finish(p):
        c, rest = zero_level.residual(qa0, S, p)
        kept_p[p - 8] = c[8:24, 0:128]
        kept_r[p - 8] = rest[8:24, 0:128]

    for copy in started[15:]:
        copy.wait()
    started = []
    for k in (0, 8):
        planes(8 + k, 16 + k, finish, 8)
        at = slice(k, k + 8)
        pairs = ((kept_p.at[at], pressure.at[at]), (kept_r.at[at], residual.at[at]))
        started += copies(pairs, out_sems.at[k // 4 : k // 4 + 2])
    for copy in started:
        copy.wait()


def call(kernel, name, ins, outs, scratch=(), aliases=()):
    anywhere = pl.BlockSpec(memory_space=pl.ANY)
    spec = {"v": pl.BlockSpec(memory_space=pltpu.VMEM), "n": pl.BlockSpec(memory_space=pltpu.VMEM), "h": anywhere}
    kind = {"v": pltpu.VMEM, "h": pltpu.HBM, "n": jax.ShapeDtypeStruct}
    space = {"v": pltpu.VMEM, "h": pltpu.HBM}

    def run(*args):
        args = [pltpu.with_memory_space_constraint(a, space[k]) if k in space else a for a, k in zip(args, ins)]
        return pl.pallas_call(
            kernel,
            out_shape=[kind[k](shape, F32) for k, shape in outs],
            in_specs=[spec[k] for k in ins],
            out_specs=[spec[k] for k, _ in outs],
            scratch_shapes=[pltpu.VMEM(shape, F32) if isinstance(shape, tuple) else shape for shape in scratch],
            compiler_params=pltpu.CompilerParams(vmem_limit_bytes=VMEM_LIMIT),
            input_output_aliases=dict(aliases),
            name=name,
        )(*args)

    return run


def ring(axis, step):
    size = lax.axis_size(axis)
    return [(i, (i + step) % size) for i in range(size)]


def exchange(to_low, to_high, axis, reach=1):
    return lax.ppermute(to_high, axis, ring(axis, reach)), lax.ppermute(to_low, axis, ring(axis, -reach))


FINE, BIG, MID, MID2, WIDE1 = (7, 32, 32, 256), (32, 32, 256), (14, 16, 128), (34, 16, 128), (24, 24, 128)
WINDOW = (14, 16, 128)
THREE, FOUR = (18, 8, 128), (10, 8, 128)


def local(source, fraction):
    def dma(count):
        return pltpu.SemaphoreType.DMA((count,))

    own, strip = (16, 16, 128), (8, 16, 128)
    s, f, to_left, to_right = call(
        pack_x_kernel, "pack_x", "hh", [("v", own)] * 2 + [("v", strip)] * 2, [dma(8)]
    )(source, fraction)
    from_left, from_right = exchange(to_left, to_right, "gx")
    rows = (sum(ROWS), 16, 128)
    halo, to_low, to_high = call(pack_y_kernel, "pack_y", "vvvv", [("v", own), ("v", rows), ("v", rows)])(
        s, f, from_right, from_left
    )
    y_halos = exchange(to_low, to_high, "gy")
    layers = (len(TILES), 8, 128)
    to_low, to_high = call(pack_z_kernel, "pack_z", "vvvvv", [("v", layers)] * 2, [(3, 16, 8, 128)] * 2)(
        s, f, halo, *y_halos
    )
    z_low, z_high = exchange(to_low, to_high, "gz")
    coarse = [(14, 32, 256), (14, 16, 256), (14, 2, 32, 128)]
    *inner, fine_inner = call(
        inner_kernel,
        "inner",
        "vvvvv",
        [("v", FINE), ("v", BIG), ("v", BIG), ("v", MID), ("v", MID), ("h", FINE)],
        [*coarse, (3, 16, 8, 128), (3, 16, 8, 128), dma(5)],
    )(s, f, halo, *y_halos)
    rows = (sum(ROWS_ONE), 8, 128)
    fine, own1, to_low, to_high, payload = call(
        down_kernel,
        "down",
        "v" * 7,
        [("v", FINE), ("v", BIG), ("v", BIG), ("v", MID), ("v", MID), ("h", FINE)]
        + [("v", (16, 8, 128)), ("v", rows), ("v", rows), ("v", (32, 16, 128))],
        [*coarse, (4, 16, 128)] + [MID] * 7 + [dma(10)],
        [(2 + i, i) for i in range(5)],
    )(z_low, z_high, *inner)[5:]
    y_low, y_high = exchange(to_low, to_high, "gy")
    got = lax.all_to_all(payload, ("gy", "gz"), 0, 0)
    layers = (len(TILES_ONE), 8, 128)
    to_low, to_high, rows = call(
        spread_y_kernel,
        "spread_y",
        "vvv",
        [("v", layers)] * 2 + [("v", (48, 8, 128))],
        [(2, 8, 8, 128)] * 2,
    )(own1, y_low, y_high)
    z_low, z_high = exchange(to_low, to_high, "gz")
    one = call(wide_kernel, "wide", "vvv", [("v", WIDE1)] * 7, [WIDE1] * 2)(rows, z_low, z_high)
    payload, *kept = call(
        middle_kernel,
        "middle",
        "vv",
        [("h", (8, 4, 8, 128))] + [("h", WINDOW)] * 3,
        [MID2] * 4 + [(16, 16, 128), (16, 16, 128)] + [MID2] * 5 + [dma(3), (4, 8, 128), dma(16)],
    )(got, rows)
    got = lax.all_to_all(payload, "gx", 0, 0)
    pressure, residual = call(
        up_kernel,
        "up",
        "v" * 8 + "h" * 5,
        [("h", own)] * 2,
        [WINDOW] * 3
        + [FINE]
        + [dma(18)]
        + [THREE] * 4
        + [FOUR] * 4
        + [THREE] * 5
        + [FOUR] * 5
        + [WINDOW] * 5
        + [(9, 8, 128), (8, 128), (8, 128), WINDOW, WINDOW, (2, 6, 8, 128), (6, 16, 128)]
        + [WIDE1] * 2
        + [(8, 24, 128), (8, 16, 128), (12, 24, 256), (2, 12, 32, 128), BIG, BIG, own, own, dma(4)],
    )(got, *one, *kept, fine_inner, fine)
    return (pressure, residual)


def solution(mesh):
    spec = P("gz", "gy", "gx")
    return jax.shard_map(
        local, mesh=mesh, in_specs=(spec, spec), out_specs=(spec, spec), check_vma=False
    )
```

```python
import jax
import jax.numpy as jnp
from jax import lax
from jax.experimental import pallas as pl
from jax.experimental.pallas import tpu as pltpu
from jax.sharding import PartitionSpec as P

RELAXATION = 0.8
F32 = jnp.float32
VMEM_LIMIT = 32 * 1024 * 1024


def turn(v, shift, axis):
    size = v.shape[axis]
    shift = shift % size
    return v if shift == 0 else pltpu.roll(v, shift, axis)


def ahead(v, axis):
    return turn(v, -1, axis)


def behind(v, axis):
    return turn(v, 1, axis)


def index_of(shape, axis):
    return lax.broadcasted_iota(jnp.int32, shape, axis)


def matmul(a, b):
    b = b.astype(jnp.bfloat16)
    total = None
    for part in range(3):
        piece = a.astype(jnp.bfloat16)
        product = lax.dot_general(piece, b, (((1,), (0,)), ((), ())), preferred_element_type=F32)
        total = product if total is None else total + product
        if part < 2:
            a = a - piece.astype(F32)
    return total


def planes(lo, hi, body, unroll=10):
    trips = (hi - lo) // unroll
    if trips > 1:

        def step(i, carry):
            for k in range(unroll):
                body(lo + i * unroll + k)
            return carry

        lax.fori_loop(0, trips, step, 0)
    else:
        trips = 0
    for p in range(lo + trips * unroll, hi):
        body(p)


class Level:
    def __init__(self, refs):
        self.wx, self.wy, self.wz, self.diag, self.inv = refs

    def build(self, frac, scale, lo, hi, wraps, unroll=10):
        half = 0.5 * scale
        self.wz[lo - 1] = half * (frac[lo - 1] + frac[lo])

        def plane(p):
            c, up, down = frac[p], frac[p + 1], frac[p - 1]
            total = 6.0 * c + up + down
            for axis, keep in ((1, self.wx), (0, self.wy)):
                after, before = ahead(c, axis), behind(c, axis)
                weight = half * (c + after)
                if wraps[axis]:
                    at = index_of(c.shape, axis)
                    last = at == c.shape[axis] - 1
                    weight = jnp.where(last, 0.0, weight)
                    after = jnp.where(last, 0.0, after)
                    before = jnp.where(at == 0, 0.0, before)
                keep[p] = weight
                total = total + after + before
            self.wz[p] = half * (c + up)
            diag = half * total
            self.diag[p] = diag
            self.inv[p] = jnp.where(c > 0.0, RELAXATION / jnp.where(c > 0.0, diag, 1.0), 0.0)

        planes(lo, hi, plane, unroll)

    def near(self, q, p):
        c, wx, wy = q[p], self.wx[p], self.wy[p]
        total = wx * ahead(c, 1) + behind(wx * c, 1) + wy * ahead(c, 0) + behind(wy * c, 0)
        return c, total + self.wz[p] * q[p + 1] + self.wz[p - 1] * q[p - 1]

    def residual(self, q, rhs, p):
        c, near = self.near(q, p)
        return c, rhs[p] + near - self.diag[p] * c

    def first(self, rhs, out, lo, hi, unroll=10):
        def plane(p):
            out[p] = self.inv[p] * rhs[p]

        planes(lo, hi, plane, unroll)

    def sweep(self, q, rhs, out, lo, hi, unroll=10):
        def plane(p):
            c, near = self.near(q, p)
            out[p] = (1.0 - RELAXATION) * c + self.inv[p] * (rhs[p] + near)

        planes(lo, hi, plane, unroll)

    def halved_residual(self, q, rhs, out, lo, hi, unroll=4):
        def pair(j):
            _, one = self.residual(q, rhs, lo + 2 * j)
            _, two = self.residual(q, rhs, lo + 2 * j + 1)
            out[j] = one + two

        planes(0, (hi - lo) // 2, pair, unroll)


def halved(values, out, lo, hi):
    def pair(j):
        out[j] = values[lo + 2 * j] + values[lo + 2 * j + 1]

    planes(0, (hi - lo) // 2, pair)


def rows_of(ref, count):
    _, rows, lanes = ref.shape
    return ref[0:count].reshape(count * rows, lanes)


def gather_pairs(lanes, out_lanes, first, place, count):
    at, to = index_of((lanes, out_lanes), 0), index_of((lanes, out_lanes), 1) - place
    pair = jnp.remainder(at - first, lanes)
    hit = (pair >= 2 * to) & (pair <= 2 * to + 1) & (to >= 0) & (to < count)
    return jnp.where(hit, 0.125, 0.0).astype(F32)


def spread_pairs(lanes, out_lanes, first, start, count):
    at, to = index_of((lanes, out_lanes), 0) - first, index_of((lanes, out_lanes), 1)
    pair = jnp.remainder(to - start, out_lanes)
    hit = (pair >= 2 * at) & (pair <= 2 * at + 1) & (at >= 0) & (at < count)
    return jnp.where(hit, 1.0, 0.0).astype(F32)


def inside(okay):
    return jnp.where(okay, 1.0, 0.0).astype(F32)


def copies(pairs, sems):
    started = [pltpu.make_async_copy(a, b, sems.at[i]) for i, (a, b) in enumerate(pairs)]
    for copy in started:
        copy.start()
    return started


def pack_x_kernel(source, fraction, s, f, to_left, to_right, sems):
    quarters = [slice(4 * k, 4 * k + 4) for k in range(4)]
    for copy in copies([(a.at[k], b.at[k]) for a, b in ((source, s), (fraction, f)) for k in quarters], sems):
        copy.wait()
    lane = index_of((16, 128), 1)
    for z in range(8):
        a, b, c, d = s[z], s[z + 8], f[z], f[z + 8]
        to_left[z] = jnp.where(
            lane < 32,
            a,
            jnp.where(lane < 64, turn(b, 32, 1), jnp.where(lane < 96, turn(c, 64, 1), turn(d, 96, 1))),
        )
        to_right[z] = jnp.where(
            lane >= 96,
            a,
            jnp.where(lane >= 64, turn(b, 96, 1), jnp.where(lane >= 32, turn(c, 64, 1), turn(d, 32, 1))),
        )


ROWS = (6, 7, 7)
ROWS_ONE = (5, 6)


def tiles_of(rows, own):
    return [
        (k, depth, t)
        for k in range(len(rows))
        for depth in range(1, rows[k] + 1)
        for t in range(own + 2)
        if 0 < t <= own or depth < rows[k]
    ]


TILES, TILES_ONE = tiles_of(ROWS, 2), tiles_of(ROWS_ONE, 1)


def unpack_y(message, out, rows, low):
    at = 0
    for k, count in enumerate(rows):
        for j in range(8):
            source = j - (8 - count) if low else j
            if 0 <= source < count:
                out[k, :, j, :] = message[at + source]
            else:
                out[k, :, j, :] = jnp.zeros(message.shape[1:], F32)
        at += count


def pack_y_kernel(s, f, from_right, from_left, halo, to_low, to_high):
    ix = lax.axis_index("gx")
    left = inside(ix > 0)
    right = inside(ix < lax.axis_size("gx") - 1)
    lane = index_of((16, 128), 1)
    is_right = (lane < 32) | ((lane >= 64) & (lane < 96))
    for z in range(8):
        r, l = from_right[z] * right, from_left[z] * left
        halo[z] = jnp.where(is_right, r, l)
        halo[z + 8] = jnp.where(is_right, turn(r, 96, 1), turn(l, 32, 1))
    at = 0
    for count, ref in zip(ROWS, (s, f, halo)):
        for j in range(count):
            to_low[at + j] = ref[:, j, :]
            to_high[at + j] = ref[:, 16 - count + j, :]
        at += count


def pack_z_kernel(s, f, halo, from_low, from_high, to_low, to_high, y_low, y_high):
    unpack_y(from_low, y_low, ROWS, True)
    unpack_y(from_high, y_high, ROWS, False)
    iy, ny = lax.axis_index("gy"), lax.axis_size("gy")
    low, high = inside(iy > 0), inside(iy < ny - 1)
    for i, (k, depth, t) in enumerate(TILES):
        for out, z in ((to_low, depth - 1), (to_high, 16 - depth)):
            if t == 0:
                out[i] = y_low[k, z] * low
            elif t == 3:
                out[i] = y_high[k, z] * high
            else:
                out[i] = (s, f, halo)[k][z, 8 * t - 8 : 8 * t, :]


def put(S, F, z0, y0, depth, height, scale, plane):
    edge = index_of((height, 128), 1)
    edge = (edge < 32) | (edge >= 96)

    def body(k):
        a, b, h = plane(k)
        if scale is not None:
            a, b, h = a * scale, b * scale, h * scale
        rows = pl.ds(y0, height)
        S[z0 + k, rows, 0:128] = a
        F[z0 + k, rows, 0:128] = b
        S[z0 + k, rows, 128:256] = jnp.where(edge, h, 0.0)
        F[z0 + k, rows, 128:256] = jnp.where(edge, turn(h, 64, 1), 0.0)

    planes(0, depth, body, 4)


SOURCE, DIAG, WEIGHTS, INVERSE, RESULT = (0, 1), (1, 2), (2, 5), (5, 6), (6, 7)
INNER = {SOURCE: ((8, 24),), DIAG: ((9, 23),), WEIGHTS: ((9, 23),), INVERSE: ((9, 23),), RESULT: ((10, 22),)}
OUTER = {
    SOURCE: ((6, 8), (24, 26)),
    DIAG: ((8, 9), (23, 24)),
    WEIGHTS: ((5, 9), (23, 26)),
    INVERSE: ((5, 9), (23, 27)),
    RESULT: ((5, 10), (22, 27)),
}


def layers_of(source, target, spans, which):
    return [
        (source.at[a:b, lo:hi], target.at[a:b, lo:hi]) for a, b in which for lo, hi in spans[(a, b)]
    ]


def split(fine):
    return fine.at[0], fine.at[6], [fine.at[k] for k in (2, 3, 4, 1, 5)]


def coarse_rows(T, U, V, count):
    for j in range(count):
        for half in range(2):
            lanes = slice(128 * half, 128 * half + 128)
            V[j, half] = T[j, :, lanes]
            U[j, :, lanes] = V[j, half, pl.ds(0, 16, 2), :] + V[j, half, pl.ds(1, 16, 2), :]
    return matmul(rows_of(U, count), gather_pairs(256, 128, 0, 0, 128)).reshape(count, 16, 128)


def inner_kernel(s, f, halo, from_low, from_high, *refs):
    fine, F, Q, f1, F1, kept, T, U, V, y_low, y_high, sems = refs
    unpack_y(from_low, y_low, ROWS, True)
    unpack_y(from_high, y_high, ROWS, False)
    S, D0, w0 = split(fine)
    iy, ny = lax.axis_index("gy"), lax.axis_size("gy")
    put(S, F, 8, 8, 16, 16, None, lambda k: (s[k], f[k], halo[k]))
    for ref, y0, okay in ((y_low, 0, iy > 0), (y_high, 24, iy < ny - 1)):
        put(S, F, 8, y0, 16, 8, inside(okay), lambda k, ref=ref: (ref[0, k], ref[1, k], ref[2, k]))
    level = Level(w0)
    level.build(F, 1.0, 9, 23, (False, False), 7)
    level.first(S, Q, 9, 23, 14)
    level.sweep(Q, S, D0, 10, 22, 6)
    started = copies(layers_of(fine, kept, INNER, INNER), sems)
    level.halved_residual(D0, S, T, 12, 20)
    halved(F, T.at[4:12], 8, 24)
    both = coarse_rows(T, U, V, 12)
    f1[5:9] = both[0:4]
    F1[3:11] = both[4:12]
    for copy in started:
        copy.wait()


def down_kernel(z_low, z_high, *refs):
    fine, F, Q, f1, F1, kept, own1, to_low, to_high, payload = refs[5:15]
    T, U, V, V1, q1, d1, *w1, sems, sent, sent_sem = refs[15:]
    S, D0, w0 = split(fine)
    iz, nz = lax.axis_index("gz"), lax.axis_size("gz")
    for p in (0, 31):
        S[p] = jnp.zeros((32, 256), F32)
        F[p] = jnp.zeros((32, 256), F32)
    zero = jnp.zeros((8, 128), F32)

    def layer(ref, depth):
        tiles = [[ref[TILES.index((k, depth, t))] if (k, depth, t) in TILES else zero for t in range(4)] for k in range(3)]
        return [jnp.concatenate(four, axis=0) for four in tiles]

    for ref, z0, okay in ((z_low, 1, iz > 0), (z_high, 24, iz < nz - 1)):
        put(S, F, z0, 0, 7, 32, inside(okay), lambda k, ref=ref, z0=z0: layer(ref, 7 - k if z0 == 1 else 1 + k))

    level = Level(w0)
    for lo, hi in ((2, 9), (23, 30)):
        level.build(F, 1.0, lo, hi, (False, False), 7)
        level.first(S, Q, lo, hi, 7)
    started = copies(layers_of(fine, kept, OUTER, (SOURCE, DIAG, WEIGHTS, INVERSE)), sems)
    level.sweep(Q, S, D0, 3, 10, 7)
    level.sweep(Q, S, D0, 22, 29, 7)
    started += copies(layers_of(fine, kept, OUTER, (RESULT,)), sems.at[8:10])
    level.halved_residual(D0, S, T, 4, 12)
    level.halved_residual(D0, S, T.at[4:8], 20, 28)
    halved(F, T.at[8:11], 2, 8)
    halved(F, T.at[11:14], 24, 30)
    both = coarse_rows(T, U, V, 14)
    f1[1:5] = both[0:4]
    f1[9:13] = both[4:8]
    F1[0:3] = both[8:11]
    F1[11:14] = both[11:14]
    for j in range(8):
        own1[j] = f1[3 + j, 4:12, :]
        own1[8 + j] = F1[3 + j, 4:12, :]
    at = 0
    for ref, count in zip((f1, F1), ROWS_ONE):
        for j in range(count):
            to_low[at + j] = ref[3:11, 4 + j, :]
            to_high[at + j] = ref[3:11, 12 - count + j, :]
        at += count

    level = Level(w1)
    level.build(F1, 0.25, 1, 13, (False, False))
    level.first(f1, q1, 1, 13)
    level.sweep(q1, f1, d1, 2, 12)
    level.halved_residual(d1, f1, V1, 3, 11)
    first = matmul(rows_of(V1, 4), gather_pairs(128, 128, 112, 0, 48))
    halved(F1, V1, 3, 11)
    both = first + matmul(rows_of(V1, 4), gather_pairs(128, 128, 112, 64, 48))
    V1[0:4] = both.reshape(4, 16, 128)
    for j in range(4):
        rows = V1[j, pl.ds(4, 4, 2), :] + V1[j, pl.ds(5, 4, 2), :]
        for d in range(32):
            sent[d, 4 * j : 4 * j + 4, :] = rows
    started += copies(((sent, payload),), sent_sem)
    for copy in started:
        copy.wait()


def spread_y_kernel(own, from_low, from_high, to_low, to_high, rows, y_low, y_high):
    unpack_y(from_low, y_low, ROWS_ONE, True)
    unpack_y(from_high, y_high, ROWS_ONE, False)
    iy, ny = lax.axis_index("gy"), lax.axis_size("gy")
    low, high = inside(iy > 0), inside(iy < ny - 1)
    for k in range(2):
        for z in range(8):
            at = (8 * k + z) * 3
            rows[at] = y_low[k, z] * low
            rows[at + 1] = own[8 * k + z]
            rows[at + 2] = y_high[k, z] * high
    for i, (k, depth, t) in enumerate(TILES_ONE):
        to_low[i] = rows[(8 * k + depth - 1) * 3 + t]
        to_high[i] = rows[(8 * k + 8 - depth) * 3 + t]


def wide_kernel(rows, z_low, z_high, f1, d1, *refs):
    w1, F1, q1 = refs[:5], refs[5], refs[6]
    iz, nz = lax.axis_index("gz"), lax.axis_size("gz")
    under, over = inside(iz > 0), inside(iz < nz - 1)
    zero = jnp.zeros((8, 128), F32)
    for k, ref in enumerate((f1, F1)):
        for t in range(3):
            at = slice(8 * t, 8 * t + 8)
            for z in range(8):
                ref[8 + z, at, :] = rows[(8 * k + z) * 3 + t]
            for depth in range(1, 7):
                there = (k, depth, t) in TILES_ONE
                i = TILES_ONE.index((k, depth, t)) if there else 0
                ref[8 - depth, at, :] = z_low[i] * under if there else zero
                ref[15 + depth, at, :] = z_high[i] * over if there else zero
    one = Level(w1)
    one.build(F1, 0.25, 3, 21, (False, False), 9)
    one.first(f1, q1, 3, 21, 18)
    one.sweep(q1, f1, d1, 4, 20, 8)


def window_start():
    return jnp.clip(4 * lax.axis_index("gz") - 4, 0, 20)


def middle_kernel(got, after, payload, f2h, F2h, d2h, *refs):
    *refs, part, part_sems = refs
    f2, F2, d2, q2, T, U, *w2, sems = refs
    keep = index_of((16, 128), 1) < 48
    zero = jnp.zeros((16, 128), F32)
    for ref in (f2, F2, q2, d2):
        ref[0] = zero
        ref[33] = zero
    for gy in range(4):
        for gz in range(8):
            block = got[gy * 8 + gz]
            rhs, frac = jnp.where(keep, block, 0.0), jnp.where(keep, turn(block, 64, 1), 0.0)
            for j in range(4):
                f2[1 + gz * 4 + j, 4 * gy : 4 * gy + 4, :] = rhs[4 * j : 4 * j + 4]
                F2[1 + gz * 4 + j, 4 * gy : 4 * gy + 4, :] = frac[4 * j : 4 * j + 4]
    at = pl.ds(window_start(), 14)
    started = copies(((f2.at[at], f2h), (F2.at[at], F2h)), sems)
    level = Level(w2)
    C = gather_pairs(128, 128, 8, 0, 16)

    def send(field):
        U[...] = matmul(rows_of(T, 16), C).reshape(16, 16, 128)
        for zh in range(2):
            total = None
            for zl in range(8):
                z = zh * 8 + zl
                rows = U[z, pl.ds(0, 8, 2), :] + U[z, pl.ds(1, 8, 2), :]
                rows = turn(rows, 16 * zl, 1)
                total = rows if total is None else total + rows
            part[2 * field + zh] = total
        at = slice(2 * field, 2 * field + 2)
        return copies([(part.at[at], payload.at[d, at]) for d in range(8)], part_sems.at[8 * field : 8 * field + 8])

    halved(F2, T, 1, 33)
    started += send(1)
    level.build(F2, 0.25**2, 1, 33, (True, False), 16)
    level.first(f2, q2, 1, 33, 16)
    level.sweep(q2, f2, d2, 1, 33, 16)
    started += copies(((d2.at[at], d2h),), sems.at[2:3])
    level.halved_residual(d2, f2, T, 1, 33, 8)
    started += send(0)
    for copy in started:
        copy.wait()


def bottom(frac, rhs, half):
    shape = (8, 128)
    row, lane = index_of(shape, 0), index_of(shape, 1)
    used = lane < 32
    odd = jnp.remainder(row, 2) == 1
    y_near = jnp.where(odd, behind(frac, 0), ahead(frac, 0))
    z_up = jnp.where(row >= 6, 0.0, turn(frac, -2, 0))
    z_down = jnp.where(row < 2, 0.0, turn(frac, 2, 0))
    x_up = jnp.where(lane < 31, ahead(frac, 1), 0.0)
    x_down = jnp.where(lane > 0, behind(frac, 1), 0.0)
    diag = half * (6.0 * frac + y_near + z_up + z_down + x_up + x_down)
    after = jnp.where(lane < 31, -half * (frac + x_up), 0.0)
    before = jnp.where((lane > 0) & used, -half * (frac + x_down), 0.0)
    A, C, D, g = [], [], [], []
    for i in range(8):
        here = row == i
        z, y = i // 2, i % 2
        linked = (row == 2 * z + 1 - y) | (row == i - 2) | (row == i + 2)
        mine = jnp.broadcast_to(frac[i : i + 1], shape)
        block = jnp.where(here, diag, jnp.where(linked, -half * (mine + frac), 0.0))
        D.append(jnp.where(used, block, jnp.where(here, 1.0, 0.0)))
        A.append(jnp.where(here, before, 0.0))
        C.append(jnp.where(here, after, 0.0))
        g.append(jnp.broadcast_to(jnp.where(used[:1], rhs[i : i + 1], 0.0), shape))

    def pick(v, k):
        return jnp.broadcast_to(v[k : k + 1], shape)

    def divide(D, others):
        D, others = list(D), [list(o) for o in others]
        for k in range(8):
            inverse = 1.0 / pick(D[k], k)
            D[k] = D[k] * inverse
            for o in others:
                o[k] = o[k] * inverse
            for i in range(8):
                if i != k:
                    factor = pick(D[i], k)
                    D[i] = D[i] - factor * D[k]
                    for o in others:
                        o[i] = o[i] - factor * o[k]
        return others

    step = 1
    while step < 32:
        X, Y, h = divide(D, (A, C, g))
        Xl, Yl, hl = [[turn(v, step, 1) for v in o] for o in (X, Y, h)]
        Xr, Yr, hr = [[turn(v, -step, 1) for v in o] for o in (X, Y, h)]
        nA, nC, nD, ng = [], [], [], []
        for i in range(8):
            d, a, c, r = D[i], None, None, g[i]
            for k in (i,) if step == 1 else range(8):
                pa, pc = pick(A[i], k), pick(C[i], k)
                d = d - (pa * Yl[k] + pc * Xr[k])
                r = r - (pa * hl[k] + pc * hr[k])
                a = -pa * Xl[k] if a is None else a - pa * Xl[k]
                c = -pc * Yr[k] if c is None else c - pc * Yr[k]
            nA.append(a)
            nC.append(c)
            nD.append(d)
            ng.append(r)
        A, C, D, g = nA, nC, nD, ng
        step *= 2
    (u,) = divide(D, (g,))
    out = jnp.zeros(shape, F32)
    for i in range(8):
        out = jnp.where((row == i) & used, u[i], out)
    return out


def up_kernel(got, *refs):
    f1, qb1, *w1 = refs[:7]
    refs = refs[7:]
    far, refs = refs[:5], refs[5:]
    pressure, residual, refs = refs[0], refs[1], refs[2:]
    near, sems = refs[:4], refs[4]
    iz, iy, ix = lax.axis_index("gz"), lax.axis_index("gy"), lax.axis_index("gx")
    nz, ny = lax.axis_size("gz"), lax.axis_size("gy")
    start = window_start()
    pairs = list(zip(far[:3], near))
    for which in ((RESULT, INVERSE), (WEIGHTS, SOURCE), (DIAG,)):
        pairs += layers_of(far[3], near[3], INNER, which) + layers_of(far[4], near[3], OUTER, which)
    started = copies(pairs, sems)
    f2, F2, d2, fine = near
    S, D0, w0 = split(fine)
    refs = refs[5:]
    f3, F3, q3, d3, f4, F4, q4, d4 = refs[:8]
    w3, w4, w2 = refs[8:13], refs[13:18], refs[18:23]
    T3, T4, TF3, TF4, g5, F5, qa2, qb2, T2, T2y, qa1, qc1, T1, U1, T0, U0, qa0, qb0, kept_p, kept_r, out_sems = refs[23:]
    lane = index_of((8, 128), 1)
    row = index_of((8, 128), 0)
    zero = jnp.zeros((8, 128), F32)

    for ref in (f3, F3, q3, d3):
        ref[0] = zero
        ref[17] = zero
    for ref in (f4, F4, q4, d4):
        ref[0] = zero
        ref[9] = zero
    for field, ref in ((1, F3), (0, f3)):
        for zh in range(2):
            blocks = [got[d, 2 * field + zh] for d in range(8)]
            for zl in range(8):
                total = turn(blocks[0], -16 * zl, 1)
                for d in range(1, 8):
                    total = jnp.where(lane >= 16 * d, turn(blocks[d], 16 * (d - zl), 1), total)
                ref[1 + zh * 8 + zl] = total

    three, four = Level(w3), Level(w4)
    C = gather_pairs(128, 128, 0, 0, 64)

    def to_four(T, out):
        T[0:8] = matmul(rows_of(T, 8), C).reshape(8, 8, 128)
        for j in range(8):
            out[1 + j] = zero
            out[1 + j, 0:4, :] = T[j, pl.ds(0, 4, 2), :] + T[j, pl.ds(1, 4, 2), :]

    def to_five(T, out):
        T[0:4] = matmul(rows_of(T, 4), C).reshape(4, 8, 128)
        for j in range(4):
            out[2 * j : 2 * j + 2, :] = T[j, pl.ds(0, 2, 2), :] + T[j, pl.ds(1, 2, 2), :]

    halved(F3, TF3, 1, 17)
    to_four(TF3, F4)
    halved(F4, TF4, 1, 9)
    to_five(TF4, F5)
    three.build(F3, 0.25**3, 1, 17, (True, True), 16)
    three.first(f3, q3, 1, 17, 16)
    three.sweep(q3, f3, d3, 1, 17, 16)
    three.halved_residual(d3, f3, T3, 1, 17, 8)
    to_four(T3, f4)
    four.build(F4, 0.25**4, 1, 9, (False, False), 8)
    four.first(f4, q4, 1, 9, 8)
    four.sweep(q4, f4, d4, 1, 9, 8)
    four.halved_residual(d4, f4, T4, 1, 9, 4)
    to_five(T4, g5)
    corr5 = bottom(F5[...], g5[...], 0.5 * 0.25**5)

    double = spread_pairs(128, 128, 0, 0, 64)
    wide = matmul(corr5, double)
    for z in range(4):
        plane = jnp.where(row < 2, wide[2 * z : 2 * z + 1], jnp.where(row < 4, wide[2 * z + 1 : 2 * z + 2], 0.0))
        for k in (0, 1):
            p = 1 + 2 * z + k
            q4[p] = d4[p] + jnp.where(F4[p] > 0.0, plane, 0.0)
    four.sweep(q4, f4, d4, 1, 9, 8)
    four.sweep(d4, f4, q4, 1, 9, 8)

    T3[0:8] = matmul(rows_of(q4.at[1:9], 8), double).reshape(8, 8, 128)
    for j in range(8):
        part = T3[j, 0:4, :]
        T3[8, pl.ds(0, 4, 2), :] = part
        T3[8, pl.ds(1, 4, 2), :] = part
        plane = T3[8]
        for k in (0, 1):
            p = 1 + 2 * j + k
            q3[p] = d3[p] + plane
    three.sweep(q3, f3, d3, 1, 17, 16)
    three.sweep(d3, f3, q3, 1, 17, 16)

    for copy in started[:3]:
        copy.wait()
    two = Level(w2)
    two.build(F2, 0.25**2, 1, 13, (True, False), 12)
    shift = jnp.remainder(4 - 16 * ix, 128)
    for j in range(6):
        T2[0, j] = pltpu.roll(q3[1 + start // 2 + j], shift, 1)
    T2[1] = matmul(T2[0].reshape(48, 128), spread_pairs(128, 128, 0, 0, 24)).reshape(6, 8, 128)
    zero2 = jnp.zeros((16, 128), F32)
    for ref in (qa2, qb2):
        ref[0] = zero2
        ref[13] = zero2
    for j in range(6):
        rows = T2[1, j]
        T2y[j, pl.ds(0, 8, 2), :] = rows
        T2y[j, pl.ds(1, 8, 2), :] = rows
        plane = T2y[j]
        for k in (0, 1):
            p = 1 + 2 * j + k
            qa2[p] = d2[p] + jnp.where(F2[p] > 0.0, plane, 0.0)
    two.sweep(qa2, f2, qb2, 1, 13, 12)
    two.sweep(qb2, f2, qa2, 1, 13, 12)

    one = Level(w1)
    shift = jnp.remainder(4 - 4 * iy, 16)
    for j in range(8):
        at = jnp.clip(4 * iz - 2 + j, 0, 31) - start
        U1[j] = pltpu.roll(qa2[1 + at], shift, 0)
    U1[...] = matmul(rows_of(U1, 8), spread_pairs(128, 128, 0, 112, 48)).reshape(8, 16, 128)
    for j in range(8):
        part = U1[j, 0:12, :]
        T1[j, pl.ds(0, 12, 2), :] = part
        T1[j, pl.ds(1, 12, 2), :] = part
        plane = T1[j]
        for k in (0, 1):
            p = 4 + 2 * j + k
            qa1[p] = qb1[p] + jnp.where(one.inv[p] > 0.0, plane, 0.0)
    one.sweep(qa1, f1, qc1, 5, 19, 7)
    one.sweep(qc1, f1, qa1, 6, 18, 6)

    zero_level = Level(w0)
    T0[...] = matmul(qa1[6:18].reshape(288, 128), spread_pairs(128, 256, 0, 0, 128)).reshape(12, 24, 256)

    def refine(j):
        for half in (0, 1):
            part = T0[j, 4:20, 128 * half : 128 * half + 128]
            U0[half, j, pl.ds(0, 16, 2), :] = part
            U0[half, j, pl.ds(1, 16, 2), :] = part
        plane = jnp.concatenate([U0[0, j], U0[1, j]], axis=1)
        for k in (0, 1):
            p = 4 + 2 * j + k
            qa0[p] = D0[p] + jnp.where(zero_level.inv[p] > 0.0, plane, 0.0)

    for copy in started[3:9]:
        copy.wait()
    planes(0, 12, refine, 4)
    for copy in started[9:15]:
        copy.wait()
    zero_level.sweep(qa0, S, qb0, 6, 26)
    zero_level.sweep(qb0, S, qa0, 7, 25)

    def finish(p):
        c, rest = zero_level.residual(qa0, S, p)
        kept_p[p - 8] = c[8:24, 0:128]
        kept_r[p - 8] = rest[8:24, 0:128]

    for copy in started[15:]:
        copy.wait()
    started = []
    for k in (0, 8):
        planes(8 + k, 16 + k, finish, 8)
        at = slice(k, k + 8)
        pairs = ((kept_p.at[at], pressure.at[at]), (kept_r.at[at], residual.at[at]))
        started += copies(pairs, out_sems.at[k // 4 : k // 4 + 2])
    for copy in started:
        copy.wait()


def call(kernel, name, ins, outs, scratch=(), aliases=()):
    anywhere = pl.BlockSpec(memory_space=pl.ANY)
    spec = {"v": pl.BlockSpec(memory_space=pltpu.VMEM), "n": pl.BlockSpec(memory_space=pltpu.VMEM), "h": anywhere}
    kind = {"v": pltpu.VMEM, "h": pltpu.HBM, "n": jax.ShapeDtypeStruct}
    space = {"v": pltpu.VMEM, "h": pltpu.HBM}

    def run(*args):
        args = [pltpu.with_memory_space_constraint(a, space[k]) if k in space else a for a, k in zip(args, ins)]
        return pl.pallas_call(
            kernel,
            out_shape=[kind[k](shape, F32) for k, shape in outs],
            in_specs=[spec[k] for k in ins],
            out_specs=[spec[k] for k, _ in outs],
            scratch_shapes=[pltpu.VMEM(shape, F32) if isinstance(shape, tuple) else shape for shape in scratch],
            compiler_params=pltpu.CompilerParams(vmem_limit_bytes=VMEM_LIMIT),
            input_output_aliases=dict(aliases),
            name=name,
        )(*args)

    return run


def ring(axis, step):
    size = lax.axis_size(axis)
    return [(i, (i + step) % size) for i in range(size)]


def exchange(to_low, to_high, axis, reach=1):
    return lax.ppermute(to_high, axis, ring(axis, reach)), lax.ppermute(to_low, axis, ring(axis, -reach))


FINE, BIG, MID, MID2, WIDE1 = (7, 32, 32, 256), (32, 32, 256), (14, 16, 128), (34, 16, 128), (24, 24, 128)
WINDOW = (14, 16, 128)
THREE, FOUR = (18, 8, 128), (10, 8, 128)


def local(source, fraction):
    def dma(count):
        return pltpu.SemaphoreType.DMA((count,))

    own, strip = (16, 16, 128), (8, 16, 128)
    s, f, to_left, to_right = call(
        pack_x_kernel, "pack_x", "hh", [("v", own)] * 2 + [("v", strip)] * 2, [dma(8)]
    )(source, fraction)
    from_left, from_right = exchange(to_left, to_right, "gx")
    rows = (sum(ROWS), 16, 128)
    halo, to_low, to_high = call(pack_y_kernel, "pack_y", "vvvv", [("v", own), ("v", rows), ("v", rows)])(
        s, f, from_right, from_left
    )
    y_halos = exchange(to_low, to_high, "gy")
    layers = (len(TILES), 8, 128)
    to_low, to_high = call(pack_z_kernel, "pack_z", "vvvvv", [("v", layers)] * 2, [(3, 16, 8, 128)] * 2)(
        s, f, halo, *y_halos
    )
    z_low, z_high = exchange(to_low, to_high, "gz")
    coarse = [(14, 32, 256), (14, 16, 256), (14, 2, 32, 128)]
    *inner, fine_inner = call(
        inner_kernel,
        "inner",
        "vvvvv",
        [("v", FINE), ("v", BIG), ("v", BIG), ("v", MID), ("v", MID), ("h", FINE)],
        [*coarse, (3, 16, 8, 128), (3, 16, 8, 128), dma(5)],
    )(s, f, halo, *y_halos)
    rows = (sum(ROWS_ONE), 8, 128)
    fine, own1, to_low, to_high, payload = call(
        down_kernel,
        "down",
        "v" * 7,
        [("v", FINE), ("v", BIG), ("v", BIG), ("v", MID), ("v", MID), ("h", FINE)]
        + [("v", (16, 8, 128)), ("v", rows), ("v", rows), ("h", (32, 16, 128))],
        [*coarse, (4, 16, 128)] + [MID] * 7 + [dma(10), (32, 16, 128), dma(1)],
        [(2 + i, i) for i in range(5)],
    )(z_low, z_high, *inner)[5:]
    y_low, y_high = exchange(to_low, to_high, "gy")
    got = lax.all_to_all(payload, ("gy", "gz"), 0, 0)
    layers = (len(TILES_ONE), 8, 128)
    to_low, to_high, rows = call(
        spread_y_kernel,
        "spread_y",
        "vvv",
        [("v", layers)] * 2 + [("v", (48, 8, 128))],
        [(2, 8, 8, 128)] * 2,
    )(own1, y_low, y_high)
    z_low, z_high = exchange(to_low, to_high, "gz")
    one = call(wide_kernel, "wide", "vvv", [("v", WIDE1)] * 7, [WIDE1] * 2)(rows, z_low, z_high)
    payload, *kept = call(
        middle_kernel,
        "middle",
        "vv",
        [("h", (8, 4, 8, 128))] + [("h", WINDOW)] * 3,
        [MID2] * 4 + [(16, 16, 128), (16, 16, 128)] + [MID2] * 5 + [dma(3), (4, 8, 128), dma(16)],
    )(got, rows)
    got = lax.all_to_all(payload, "gx", 0, 0)
    pressure, residual = call(
        up_kernel,
        "up",
        "v" * 8 + "h" * 5,
        [("h", own)] * 2,
        [WINDOW] * 3
        + [FINE]
        + [dma(18)]
        + [THREE] * 4
        + [FOUR] * 4
        + [THREE] * 5
        + [FOUR] * 5
        + [WINDOW] * 5
        + [(9, 8, 128), (4, 8, 128), (8, 8, 128), (4, 8, 128), (8, 128), (8, 128), WINDOW, WINDOW, (2, 6, 8, 128), (6, 16, 128)]
        + [WIDE1] * 2
        + [(8, 24, 128), (8, 16, 128), (12, 24, 256), (2, 12, 32, 128), BIG, BIG, own, own, dma(4)],
    )(got, *one, *kept, fine_inner, fine)
    return (pressure, residual)


def solution(mesh):
    spec = P("gz", "gy", "gx")
    return jax.shard_map(
        local, mesh=mesh, in_specs=(spec, spec), out_specs=(spec, spec), check_vma=False
    )
```

```python
import jax
import jax.numpy as jnp
from jax import lax
from jax.experimental import pallas as pl
from jax.experimental.pallas import tpu as pltpu
from jax.sharding import PartitionSpec as P

RELAXATION = 0.8
F32 = jnp.float32
VMEM_LIMIT = 32 * 1024 * 1024


def turn(v, shift, axis):
    size = v.shape[axis]
    shift = shift % size
    return v if shift == 0 else pltpu.roll(v, shift, axis)


def ahead(v, axis):
    return turn(v, -1, axis)


def behind(v, axis):
    return turn(v, 1, axis)


def index_of(shape, axis):
    return lax.broadcasted_iota(jnp.int32, shape, axis)


def matmul(a, b):
    b = b.astype(jnp.bfloat16)
    total = None
    for part in range(3):
        piece = a.astype(jnp.bfloat16)
        product = lax.dot_general(piece, b, (((1,), (0,)), ((), ())), preferred_element_type=F32)
        total = product if total is None else total + product
        if part < 2:
            a = a - piece.astype(F32)
    return total


def planes(lo, hi, body, unroll=10):
    trips = (hi - lo) // unroll
    if trips > 1:

        def step(i, carry):
            for k in range(unroll):
                body(lo + i * unroll + k)
            return carry

        lax.fori_loop(0, trips, step, 0)
    else:
        trips = 0
    for p in range(lo + trips * unroll, hi):
        body(p)


class Level:
    def __init__(self, refs):
        self.wx, self.wy, self.wz, self.diag, self.inv = refs

    def build(self, frac, scale, lo, hi, wraps, unroll=10):
        half = 0.5 * scale
        self.wz[lo - 1] = half * (frac[lo - 1] + frac[lo])

        def plane(p):
            c, up, down = frac[p], frac[p + 1], frac[p - 1]
            total = 6.0 * c + up + down
            for axis, keep in ((1, self.wx), (0, self.wy)):
                after, before = ahead(c, axis), behind(c, axis)
                weight = half * (c + after)
                if wraps[axis]:
                    at = index_of(c.shape, axis)
                    last = at == c.shape[axis] - 1
                    weight = jnp.where(last, 0.0, weight)
                    after = jnp.where(last, 0.0, after)
                    before = jnp.where(at == 0, 0.0, before)
                keep[p] = weight
                total = total + after + before
            self.wz[p] = half * (c + up)
            diag = half * total
            self.diag[p] = diag
            self.inv[p] = jnp.where(c > 0.0, RELAXATION / jnp.where(c > 0.0, diag, 1.0), 0.0)

        planes(lo, hi, plane, unroll)

    def near(self, q, p):
        c, wx, wy = q[p], self.wx[p], self.wy[p]
        total = wx * ahead(c, 1) + behind(wx * c, 1) + wy * ahead(c, 0) + behind(wy * c, 0)
        return c, total + self.wz[p] * q[p + 1] + self.wz[p - 1] * q[p - 1]

    def residual(self, q, rhs, p):
        c, near = self.near(q, p)
        return c, rhs[p] + near - self.diag[p] * c

    def first(self, rhs, out, lo, hi, unroll=10):
        def plane(p):
            out[p] = self.inv[p] * rhs[p]

        planes(lo, hi, plane, unroll)

    def sweep(self, q, rhs, out, lo, hi, unroll=10):
        def plane(p):
            c, near = self.near(q, p)
            out[p] = (1.0 - RELAXATION) * c + self.inv[p] * (rhs[p] + near)

        planes(lo, hi, plane, unroll)

    def halved_residual(self, q, rhs, out, lo, hi, unroll=4):
        def pair(j):
            _, one = self.residual(q, rhs, lo + 2 * j)
            _, two = self.residual(q, rhs, lo + 2 * j + 1)
            out[j] = one + two

        planes(0, (hi - lo) // 2, pair, unroll)


def halved(values, out, lo, hi):
    def pair(j):
        out[j] = values[lo + 2 * j] + values[lo + 2 * j + 1]

    planes(0, (hi - lo) // 2, pair)


def rows_of(ref, count):
    _, rows, lanes = ref.shape
    return ref[0:count].reshape(count * rows, lanes)


def gather_pairs(lanes, out_lanes, first, place, count):
    at, to = index_of((lanes, out_lanes), 0), index_of((lanes, out_lanes), 1) - place
    pair = jnp.remainder(at - first, lanes)
    hit = (pair >= 2 * to) & (pair <= 2 * to + 1) & (to >= 0) & (to < count)
    return jnp.where(hit, 0.125, 0.0).astype(F32)


def spread_pairs(lanes, out_lanes, first, start, count):
    at, to = index_of((lanes, out_lanes), 0) - first, index_of((lanes, out_lanes), 1)
    pair = jnp.remainder(to - start, out_lanes)
    hit = (pair >= 2 * at) & (pair <= 2 * at + 1) & (at >= 0) & (at < count)
    return jnp.where(hit, 1.0, 0.0).astype(F32)


def inside(okay):
    return jnp.where(okay, 1.0, 0.0).astype(F32)


def copies(pairs, sems):
    started = [pltpu.make_async_copy(a, b, sems.at[i]) for i, (a, b) in enumerate(pairs)]
    for copy in started:
        copy.start()
    return started


def pack_x_kernel(source, fraction, s, f, to_left, to_right, sems):
    quarters = [slice(4 * k, 4 * k + 4) for k in range(4)]
    for copy in copies([(a.at[k], b.at[k]) for a, b in ((source, s), (fraction, f)) for k in quarters], sems):
        copy.wait()
    lane = index_of((16, 128), 1)
    for z in range(8):
        a, b, c, d = s[z], s[z + 8], f[z], f[z + 8]
        to_left[z] = jnp.where(
            lane < 32,
            a,
            jnp.where(lane < 64, turn(b, 32, 1), jnp.where(lane < 96, turn(c, 64, 1), turn(d, 96, 1))),
        )
        to_right[z] = jnp.where(
            lane >= 96,
            a,
            jnp.where(lane >= 64, turn(b, 96, 1), jnp.where(lane >= 32, turn(c, 64, 1), turn(d, 32, 1))),
        )


ROWS = (6, 7, 7)
ROWS_ONE = (5, 6)


def tiles_of(rows, own):
    return [
        (k, depth, t)
        for k in range(len(rows))
        for depth in range(1, rows[k] + 1)
        for t in range(own + 2)
        if 0 < t <= own or depth < rows[k]
    ]


TILES, TILES_ONE = tiles_of(ROWS, 2), tiles_of(ROWS_ONE, 1)


def unpack_y(message, out, rows, low):
    at = 0
    for k, count in enumerate(rows):
        for j in range(8):
            source = j - (8 - count) if low else j
            if 0 <= source < count:
                out[k, :, j, :] = message[at + source]
            else:
                out[k, :, j, :] = jnp.zeros(message.shape[1:], F32)
        at += count


def pack_rows(arrays, first, to_low, to_high):
    at = sum(ROWS[:first])
    for count, ref in zip(ROWS[first:], arrays):
        for j in range(count):
            to_low[at + j] = ref[:, j, :]
            to_high[at + j] = ref[:, 16 - count + j, :]
        at += count


def pack_own_kernel(s, f, to_low, to_high):
    pack_rows((s, f), 0, to_low, to_high)


def pack_y_kernel(from_right, from_left, low_in, high_in, halo, to_low, to_high):
    ix = lax.axis_index("gx")
    left = inside(ix > 0)
    right = inside(ix < lax.axis_size("gx") - 1)
    lane = index_of((16, 128), 1)
    is_right = (lane < 32) | ((lane >= 64) & (lane < 96))
    for z in range(8):
        r, l = from_right[z] * right, from_left[z] * left
        halo[z] = jnp.where(is_right, r, l)
        halo[z + 8] = jnp.where(is_right, turn(r, 96, 1), turn(l, 32, 1))
    pack_rows((halo,), 2, to_low, to_high)


def pack_z_kernel(s, f, halo, from_low, from_high, to_low, to_high, y_low, y_high):
    unpack_y(from_low, y_low, ROWS, True)
    unpack_y(from_high, y_high, ROWS, False)
    iy, ny = lax.axis_index("gy"), lax.axis_size("gy")
    low, high = inside(iy > 0), inside(iy < ny - 1)
    for i, (k, depth, t) in enumerate(TILES):
        for out, z in ((to_low, depth - 1), (to_high, 16 - depth)):
            if t == 0:
                out[i] = y_low[k, z] * low
            elif t == 3:
                out[i] = y_high[k, z] * high
            else:
                out[i] = (s, f, halo)[k][z, 8 * t - 8 : 8 * t, :]


def put(S, F, z0, y0, depth, height, scale, plane):
    edge = index_of((height, 128), 1)
    edge = (edge < 32) | (edge >= 96)

    def body(k):
        a, b, h = plane(k)
        if scale is not None:
            a, b, h = a * scale, b * scale, h * scale
        rows = pl.ds(y0, height)
        S[z0 + k, rows, 0:128] = a
        F[z0 + k, rows, 0:128] = b
        S[z0 + k, rows, 128:256] = jnp.where(edge, h, 0.0)
        F[z0 + k, rows, 128:256] = jnp.where(edge, turn(h, 64, 1), 0.0)

    planes(0, depth, body, 4)


SOURCE, DIAG, WEIGHTS, INVERSE, RESULT = (0, 1), (1, 2), (2, 5), (5, 6), (6, 7)
INNER = {SOURCE: ((8, 24),), DIAG: ((9, 23),), WEIGHTS: ((9, 23),), INVERSE: ((9, 23),), RESULT: ((10, 22),)}
OUTER = {
    SOURCE: ((6, 8), (24, 26)),
    DIAG: ((8, 9), (23, 24)),
    WEIGHTS: ((5, 9), (23, 26)),
    INVERSE: ((5, 9), (23, 27)),
    RESULT: ((5, 10), (22, 27)),
}


def layers_of(source, target, spans, which):
    return [
        (source.at[a:b, lo:hi], target.at[a:b, lo:hi]) for a, b in which for lo, hi in spans[(a, b)]
    ]


def split(fine):
    return fine.at[0], fine.at[6], [fine.at[k] for k in (2, 3, 4, 1, 5)]


def coarse_rows(T, U, V, count):
    for j in range(count):
        for half in range(2):
            lanes = slice(128 * half, 128 * half + 128)
            V[j, half] = T[j, :, lanes]
            U[j, :, lanes] = V[j, half, pl.ds(0, 16, 2), :] + V[j, half, pl.ds(1, 16, 2), :]
    return matmul(rows_of(U, count), gather_pairs(256, 128, 0, 0, 128)).reshape(count, 16, 128)


def inner_kernel(s, f, halo, from_low, from_high, *refs):
    fine, F, Q, f1, F1, kept, T, U, V, y_low, y_high, sems = refs
    unpack_y(from_low, y_low, ROWS, True)
    unpack_y(from_high, y_high, ROWS, False)
    S, D0, w0 = split(fine)
    iy, ny = lax.axis_index("gy"), lax.axis_size("gy")
    put(S, F, 8, 8, 16, 16, None, lambda k: (s[k], f[k], halo[k]))
    for ref, y0, okay in ((y_low, 0, iy > 0), (y_high, 24, iy < ny - 1)):
        put(S, F, 8, y0, 16, 8, inside(okay), lambda k, ref=ref: (ref[0, k], ref[1, k], ref[2, k]))
    level = Level(w0)
    level.build(F, 1.0, 9, 23, (False, False), 7)
    level.first(S, Q, 9, 23, 14)
    level.sweep(Q, S, D0, 10, 22, 6)
    started = copies(layers_of(fine, kept, INNER, INNER), sems)
    level.halved_residual(D0, S, T, 12, 20)
    halved(F, T.at[4:12], 8, 24)
    both = coarse_rows(T, U, V, 12)
    f1[5:9] = both[0:4]
    F1[3:11] = both[4:12]
    for copy in started:
        copy.wait()


def down_kernel(z_low, z_high, *refs):
    fine, F, Q, f1, F1, kept, own1, to_low, to_high, payload = refs[5:15]
    T, U, V, V1, q1, d1, *w1, sems, sent, sent_sem = refs[15:]
    S, D0, w0 = split(fine)
    iz, nz = lax.axis_index("gz"), lax.axis_size("gz")
    for p in (0, 31):
        S[p] = jnp.zeros((32, 256), F32)
        F[p] = jnp.zeros((32, 256), F32)
    zero = jnp.zeros((8, 128), F32)

    def layer(ref, depth):
        tiles = [[ref[TILES.index((k, depth, t))] if (k, depth, t) in TILES else zero for t in range(4)] for k in range(3)]
        return [jnp.concatenate(four, axis=0) for four in tiles]

    for ref, z0, okay in ((z_low, 1, iz > 0), (z_high, 24, iz < nz - 1)):
        put(S, F, z0, 0, 7, 32, inside(okay), lambda k, ref=ref, z0=z0: layer(ref, 7 - k if z0 == 1 else 1 + k))

    level = Level(w0)
    for lo, hi in ((2, 9), (23, 30)):
        level.build(F, 1.0, lo, hi, (False, False), 7)
        level.first(S, Q, lo, hi, 7)
    started = copies(layers_of(fine, kept, OUTER, (SOURCE, DIAG, WEIGHTS, INVERSE)), sems)
    level.sweep(Q, S, D0, 3, 10, 7)
    level.sweep(Q, S, D0, 22, 29, 7)
    started += copies(layers_of(fine, kept, OUTER, (RESULT,)), sems.at[8:10])
    level.halved_residual(D0, S, T, 4, 12)
    level.halved_residual(D0, S, T.at[4:8], 20, 28)
    halved(F, T.at[8:11], 2, 8)
    halved(F, T.at[11:14], 24, 30)
    both = coarse_rows(T, U, V, 14)
    f1[1:5] = both[0:4]
    f1[9:13] = both[4:8]
    F1[0:3] = both[8:11]
    F1[11:14] = both[11:14]
    for j in range(8):
        own1[j] = f1[3 + j, 4:12, :]
        own1[8 + j] = F1[3 + j, 4:12, :]
    at = 0
    for ref, count in zip((f1, F1), ROWS_ONE):
        for j in range(count):
            to_low[at + j] = ref[3:11, 4 + j, :]
            to_high[at + j] = ref[3:11, 12 - count + j, :]
        at += count

    level = Level(w1)
    level.build(F1, 0.25, 1, 13, (False, False))
    level.first(f1, q1, 1, 13)
    level.sweep(q1, f1, d1, 2, 12)
    level.halved_residual(d1, f1, V1, 3, 11)
    first = matmul(rows_of(V1, 4), gather_pairs(128, 128, 112, 0, 48))
    halved(F1, V1, 3, 11)
    both = first + matmul(rows_of(V1, 4), gather_pairs(128, 128, 112, 64, 48))
    V1[0:4] = both.reshape(4, 16, 128)
    for j in range(4):
        rows = V1[j, pl.ds(4, 4, 2), :] + V1[j, pl.ds(5, 4, 2), :]
        for d in range(32):
            sent[d, 4 * j : 4 * j + 4, :] = rows
    started += copies(((sent, payload),), sent_sem)
    for copy in started:
        copy.wait()


def spread_y_kernel(own, from_low, from_high, to_low, to_high, rows, y_low, y_high):
    unpack_y(from_low, y_low, ROWS_ONE, True)
    unpack_y(from_high, y_high, ROWS_ONE, False)
    iy, ny = lax.axis_index("gy"), lax.axis_size("gy")
    low, high = inside(iy > 0), inside(iy < ny - 1)
    for k in range(2):
        for z in range(8):
            at = (8 * k + z) * 3
            rows[at] = y_low[k, z] * low
            rows[at + 1] = own[8 * k + z]
            rows[at + 2] = y_high[k, z] * high
    for i, (k, depth, t) in enumerate(TILES_ONE):
        to_low[i] = rows[(8 * k + depth - 1) * 3 + t]
        to_high[i] = rows[(8 * k + 8 - depth) * 3 + t]


def wide_kernel(rows, z_low, z_high, f1, d1, *refs):
    w1, F1, q1 = refs[:5], refs[5], refs[6]
    iz, nz = lax.axis_index("gz"), lax.axis_size("gz")
    under, over = inside(iz > 0), inside(iz < nz - 1)
    zero = jnp.zeros((8, 128), F32)
    for k, ref in enumerate((f1, F1)):
        for t in range(3):
            at = slice(8 * t, 8 * t + 8)
            for z in range(8):
                ref[8 + z, at, :] = rows[(8 * k + z) * 3 + t]
            for depth in range(1, 7):
                there = (k, depth, t) in TILES_ONE
                i = TILES_ONE.index((k, depth, t)) if there else 0
                ref[8 - depth, at, :] = z_low[i] * under if there else zero
                ref[15 + depth, at, :] = z_high[i] * over if there else zero
    one = Level(w1)
    one.build(F1, 0.25, 3, 21, (False, False), 9)
    one.first(f1, q1, 3, 21, 18)
    one.sweep(q1, f1, d1, 4, 20, 8)


def window_start():
    return jnp.clip(4 * lax.axis_index("gz") - 4, 0, 20)


def middle_kernel(got, after, payload, f2h, F2h, d2h, *refs):
    *refs, part, part_sems = refs
    f2, F2, d2, q2, T, U, *w2, sems = refs
    keep = index_of((16, 128), 1) < 48
    zero = jnp.zeros((16, 128), F32)
    for ref in (f2, F2, q2, d2):
        ref[0] = zero
        ref[33] = zero
    for gy in range(4):
        for gz in range(8):
            block = got[gy * 8 + gz]
            rhs, frac = jnp.where(keep, block, 0.0), jnp.where(keep, turn(block, 64, 1), 0.0)
            for j in range(4):
                f2[1 + gz * 4 + j, 4 * gy : 4 * gy + 4, :] = rhs[4 * j : 4 * j + 4]
                F2[1 + gz * 4 + j, 4 * gy : 4 * gy + 4, :] = frac[4 * j : 4 * j + 4]
    at = pl.ds(window_start(), 14)
    started = copies(((f2.at[at], f2h), (F2.at[at], F2h)), sems)
    level = Level(w2)
    C = gather_pairs(128, 128, 8, 0, 16)

    def send(field):
        U[...] = matmul(rows_of(T, 16), C).reshape(16, 16, 128)
        for zh in range(2):
            total = None
            for zl in range(8):
                z = zh * 8 + zl
                rows = U[z, pl.ds(0, 8, 2), :] + U[z, pl.ds(1, 8, 2), :]
                rows = turn(rows, 16 * zl, 1)
                total = rows if total is None else total + rows
            part[2 * field + zh] = total
        at = slice(2 * field, 2 * field + 2)
        return copies([(part.at[at], payload.at[d, at]) for d in range(8)], part_sems.at[8 * field : 8 * field + 8])

    halved(F2, T, 1, 33)
    started += send(1)
    level.build(F2, 0.25**2, 1, 33, (True, False), 16)
    level.first(f2, q2, 1, 33, 16)
    level.sweep(q2, f2, d2, 1, 33, 16)
    started += copies(((d2.at[at], d2h),), sems.at[2:3])
    level.halved_residual(d2, f2, T, 1, 33, 8)
    started += send(0)
    for copy in started:
        copy.wait()


def bottom(frac, rhs, half):
    shape = (8, 128)
    row, lane = index_of(shape, 0), index_of(shape, 1)
    used = lane < 32
    odd = jnp.remainder(row, 2) == 1
    y_near = jnp.where(odd, behind(frac, 0), ahead(frac, 0))
    z_up = jnp.where(row >= 6, 0.0, turn(frac, -2, 0))
    z_down = jnp.where(row < 2, 0.0, turn(frac, 2, 0))
    x_up = jnp.where(lane < 31, ahead(frac, 1), 0.0)
    x_down = jnp.where(lane > 0, behind(frac, 1), 0.0)
    diag = half * (6.0 * frac + y_near + z_up + z_down + x_up + x_down)
    after = jnp.where(lane < 31, -half * (frac + x_up), 0.0)
    before = jnp.where((lane > 0) & used, -half * (frac + x_down), 0.0)
    A, C, D, g = [], [], [], []
    for i in range(8):
        here = row == i
        z, y = i // 2, i % 2
        linked = (row == 2 * z + 1 - y) | (row == i - 2) | (row == i + 2)
        mine = jnp.broadcast_to(frac[i : i + 1], shape)
        block = jnp.where(here, diag, jnp.where(linked, -half * (mine + frac), 0.0))
        D.append(jnp.where(used, block, jnp.where(here, 1.0, 0.0)))
        A.append(jnp.where(here, before, 0.0))
        C.append(jnp.where(here, after, 0.0))
        g.append(jnp.broadcast_to(jnp.where(used[:1], rhs[i : i + 1], 0.0), shape))

    def pick(v, k):
        return jnp.broadcast_to(v[k : k + 1], shape)

    def divide(D, others):
        D, others = list(D), [list(o) for o in others]
        for k in range(8):
            inverse = 1.0 / pick(D[k], k)
            D[k] = D[k] * inverse
            for o in others:
                o[k] = o[k] * inverse
            for i in range(8):
                if i != k:
                    factor = pick(D[i], k)
                    D[i] = D[i] - factor * D[k]
                    for o in others:
                        o[i] = o[i] - factor * o[k]
        return others

    step = 1
    while step < 32:
        X, Y, h = divide(D, (A, C, g))
        Xl, Yl, hl = [[turn(v, step, 1) for v in o] for o in (X, Y, h)]
        Xr, Yr, hr = [[turn(v, -step, 1) for v in o] for o in (X, Y, h)]
        nA, nC, nD, ng = [], [], [], []
        for i in range(8):
            d, a, c, r = D[i], None, None, g[i]
            for k in (i,) if step == 1 else range(8):
                pa, pc = pick(A[i], k), pick(C[i], k)
                d = d - (pa * Yl[k] + pc * Xr[k])
                r = r - (pa * hl[k] + pc * hr[k])
                a = -pa * Xl[k] if a is None else a - pa * Xl[k]
                c = -pc * Yr[k] if c is None else c - pc * Yr[k]
            nA.append(a)
            nC.append(c)
            nD.append(d)
            ng.append(r)
        A, C, D, g = nA, nC, nD, ng
        step *= 2
    (u,) = divide(D, (g,))
    out = jnp.zeros(shape, F32)
    for i in range(8):
        out = jnp.where((row == i) & used, u[i], out)
    return out


def up_kernel(got, *refs):
    f1, qb1, *w1 = refs[:7]
    refs = refs[7:]
    far, refs = refs[:5], refs[5:]
    pressure, residual, refs = refs[0], refs[1], refs[2:]
    near, sems = refs[:4], refs[4]
    iz, iy, ix = lax.axis_index("gz"), lax.axis_index("gy"), lax.axis_index("gx")
    nz, ny = lax.axis_size("gz"), lax.axis_size("gy")
    start = window_start()
    pairs = list(zip(far[:3], near))
    for which in ((RESULT, INVERSE), (WEIGHTS, SOURCE), (DIAG,)):
        pairs += layers_of(far[3], near[3], INNER, which) + layers_of(far[4], near[3], OUTER, which)
    started = copies(pairs, sems)
    f2, F2, d2, fine = near
    S, D0, w0 = split(fine)
    refs = refs[5:]
    f3, F3, q3, d3, f4, F4, q4, d4 = refs[:8]
    w3, w4, w2 = refs[8:13], refs[13:18], refs[18:23]
    T3, T4, TF3, TF4, g5, F5, qa2, qb2, T2, T2y, qa1, qc1, T1, U1, T0, U0, qa0, qb0, kept_p, kept_r, out_sems = refs[23:]
    lane = index_of((8, 128), 1)
    row = index_of((8, 128), 0)
    zero = jnp.zeros((8, 128), F32)

    for ref in (f3, F3, q3, d3):
        ref[0] = zero
        ref[17] = zero
    for ref in (f4, F4, q4, d4):
        ref[0] = zero
        ref[9] = zero
    for field, ref in ((1, F3), (0, f3)):
        for zh in range(2):
            blocks = [got[d, 2 * field + zh] for d in range(8)]
            for zl in range(8):
                total = turn(blocks[0], -16 * zl, 1)
                for d in range(1, 8):
                    total = jnp.where(lane >= 16 * d, turn(blocks[d], 16 * (d - zl), 1), total)
                ref[1 + zh * 8 + zl] = total

    three, four = Level(w3), Level(w4)
    C = gather_pairs(128, 128, 0, 0, 64)

    def to_four(T, out):
        T[0:8] = matmul(rows_of(T, 8), C).reshape(8, 8, 128)
        for j in range(8):
            out[1 + j] = zero
            out[1 + j, 0:4, :] = T[j, pl.ds(0, 4, 2), :] + T[j, pl.ds(1, 4, 2), :]

    def to_five(T, out):
        T[0:4] = matmul(rows_of(T, 4), C).reshape(4, 8, 128)
        for j in range(4):
            out[2 * j : 2 * j + 2, :] = T[j, pl.ds(0, 2, 2), :] + T[j, pl.ds(1, 2, 2), :]

    halved(F3, TF3, 1, 17)
    to_four(TF3, F4)
    halved(F4, TF4, 1, 9)
    to_five(TF4, F5)
    three.build(F3, 0.25**3, 1, 17, (True, True), 16)
    three.first(f3, q3, 1, 17, 16)
    three.sweep(q3, f3, d3, 1, 17, 16)
    three.halved_residual(d3, f3, T3, 1, 17, 8)
    to_four(T3, f4)
    four.build(F4, 0.25**4, 1, 9, (False, False), 8)
    four.first(f4, q4, 1, 9, 8)
    four.sweep(q4, f4, d4, 1, 9, 8)
    four.halved_residual(d4, f4, T4, 1, 9, 4)
    to_five(T4, g5)
    corr5 = bottom(F5[...], g5[...], 0.5 * 0.25**5)

    double = spread_pairs(128, 128, 0, 0, 64)
    wide = matmul(corr5, double)
    for z in range(4):
        plane = jnp.where(row < 2, wide[2 * z : 2 * z + 1], jnp.where(row < 4, wide[2 * z + 1 : 2 * z + 2], 0.0))
        for k in (0, 1):
            p = 1 + 2 * z + k
            q4[p] = d4[p] + jnp.where(F4[p] > 0.0, plane, 0.0)
    four.sweep(q4, f4, d4, 1, 9, 8)
    four.sweep(d4, f4, q4, 1, 9, 8)

    T3[0:8] = matmul(rows_of(q4.at[1:9], 8), double).reshape(8, 8, 128)
    for j in range(8):
        part = T3[j, 0:4, :]
        T3[8, pl.ds(0, 4, 2), :] = part
        T3[8, pl.ds(1, 4, 2), :] = part
        plane = T3[8]
        for k in (0, 1):
            p = 1 + 2 * j + k
            q3[p] = d3[p] + plane
    three.sweep(q3, f3, d3, 1, 17, 16)
    three.sweep(d3, f3, q3, 1, 17, 16)

    for copy in started[:3]:
        copy.wait()
    two = Level(w2)
    two.build(F2, 0.25**2, 1, 13, (True, False), 12)
    shift = jnp.remainder(4 - 16 * ix, 128)
    for j in range(6):
        T2[0, j] = pltpu.roll(q3[1 + start // 2 + j], shift, 1)
    T2[1] = matmul(T2[0].reshape(48, 128), spread_pairs(128, 128, 0, 0, 24)).reshape(6, 8, 128)
    zero2 = jnp.zeros((16, 128), F32)
    for ref in (qa2, qb2):
        ref[0] = zero2
        ref[13] = zero2
    for j in range(6):
        rows = T2[1, j]
        T2y[j, pl.ds(0, 8, 2), :] = rows
        T2y[j, pl.ds(1, 8, 2), :] = rows
        plane = T2y[j]
        for k in (0, 1):
            p = 1 + 2 * j + k
            qa2[p] = d2[p] + jnp.where(F2[p] > 0.0, plane, 0.0)
    two.sweep(qa2, f2, qb2, 1, 13, 12)
    two.sweep(qb2, f2, qa2, 1, 13, 12)

    one = Level(w1)
    shift = jnp.remainder(4 - 4 * iy, 16)
    for j in range(8):
        at = jnp.clip(4 * iz - 2 + j, 0, 31) - start
        U1[j] = pltpu.roll(qa2[1 + at], shift, 0)
    U1[...] = matmul(rows_of(U1, 8), spread_pairs(128, 128, 0, 112, 48)).reshape(8, 16, 128)
    for j in range(8):
        part = U1[j, 0:12, :]
        T1[j, pl.ds(0, 12, 2), :] = part
        T1[j, pl.ds(1, 12, 2), :] = part
        plane = T1[j]
        for k in (0, 1):
            p = 4 + 2 * j + k
            qa1[p] = qb1[p] + jnp.where(one.inv[p] > 0.0, plane, 0.0)
    one.sweep(qa1, f1, qc1, 5, 19, 7)
    one.sweep(qc1, f1, qa1, 6, 18, 6)

    zero_level = Level(w0)
    T0[...] = matmul(qa1[6:18].reshape(288, 128), spread_pairs(128, 256, 0, 0, 128)).reshape(12, 24, 256)

    def refine(j):
        for half in (0, 1):
            part = T0[j, 4:20, 128 * half : 128 * half + 128]
            U0[half, j, pl.ds(0, 16, 2), :] = part
            U0[half, j, pl.ds(1, 16, 2), :] = part
        plane = jnp.concatenate([U0[0, j], U0[1, j]], axis=1)
        for k in (0, 1):
            p = 4 + 2 * j + k
            qa0[p] = D0[p] + jnp.where(zero_level.inv[p] > 0.0, plane, 0.0)

    for copy in started[3:9]:
        copy.wait()
    planes(0, 12, refine, 4)
    for copy in started[9:15]:
        copy.wait()
    zero_level.sweep(qa0, S, qb0, 6, 26)
    zero_level.sweep(qb0, S, qa0, 7, 25)

    def finish(p):
        c, rest = zero_level.residual(qa0, S, p)
        kept_p[p - 8] = c[8:24, 0:128]
        kept_r[p - 8] = rest[8:24, 0:128]

    for copy in started[15:]:
        copy.wait()
    started = []
    for k in (0, 8):
        planes(8 + k, 16 + k, finish, 8)
        at = slice(k, k + 8)
        pairs = ((kept_p.at[at], pressure.at[at]), (kept_r.at[at], residual.at[at]))
        started += copies(pairs, out_sems.at[k // 4 : k // 4 + 2])
    for copy in started:
        copy.wait()


def call(kernel, name, ins, outs, scratch=(), aliases=()):
    anywhere = pl.BlockSpec(memory_space=pl.ANY)
    spec = {"v": pl.BlockSpec(memory_space=pltpu.VMEM), "n": pl.BlockSpec(memory_space=pltpu.VMEM), "h": anywhere}
    kind = {"v": pltpu.VMEM, "h": pltpu.HBM, "n": jax.ShapeDtypeStruct}
    space = {"v": pltpu.VMEM, "h": pltpu.HBM}

    def run(*args):
        args = [pltpu.with_memory_space_constraint(a, space[k]) if k in space else a for a, k in zip(args, ins)]
        return pl.pallas_call(
            kernel,
            out_shape=[kind[k](shape, F32) for k, shape in outs],
            in_specs=[spec[k] for k in ins],
            out_specs=[spec[k] for k, _ in outs],
            scratch_shapes=[pltpu.VMEM(shape, F32) if isinstance(shape, tuple) else shape for shape in scratch],
            compiler_params=pltpu.CompilerParams(vmem_limit_bytes=VMEM_LIMIT),
            input_output_aliases=dict(aliases),
            name=name,
        )(*args)

    return run


def ring(axis, step):
    size = lax.axis_size(axis)
    return [(i, (i + step) % size) for i in range(size)]


def exchange(to_low, to_high, axis, reach=1):
    return lax.ppermute(to_high, axis, ring(axis, reach)), lax.ppermute(to_low, axis, ring(axis, -reach))


FINE, BIG, MID, MID2, WIDE1 = (7, 32, 32, 256), (32, 32, 256), (14, 16, 128), (34, 16, 128), (24, 24, 128)
WINDOW = (14, 16, 128)
THREE, FOUR = (18, 8, 128), (10, 8, 128)


def local(source, fraction):
    def dma(count):
        return pltpu.SemaphoreType.DMA((count,))

    own, strip = (16, 16, 128), (8, 16, 128)
    s, f, to_left, to_right = call(
        pack_x_kernel, "pack_x", "hh", [("v", own)] * 2 + [("v", strip)] * 2, [dma(8)]
    )(source, fraction)
    from_left, from_right = exchange(to_left, to_right, "gx")
    rows = (sum(ROWS), 16, 128)
    started = call(pack_own_kernel, "pack_own", "vv", [("v", rows), ("v", rows)])(s, f)
    halo, to_low, to_high = call(
        pack_y_kernel, "pack_y", "vvvv", [("v", own), ("v", rows), ("v", rows)], (), [(2, 1), (3, 2)]
    )(from_right, from_left, *started)
    y_halos = exchange(to_low, to_high, "gy")
    layers = (len(TILES), 8, 128)
    to_low, to_high = call(pack_z_kernel, "pack_z", "vvvvv", [("v", layers)] * 2, [(3, 16, 8, 128)] * 2)(
        s, f, halo, *y_halos
    )
    z_low, z_high = exchange(to_low, to_high, "gz")
    coarse = [(14, 32, 256), (14, 16, 256), (14, 2, 32, 128)]
    *inner, fine_inner = call(
        inner_kernel,
        "inner",
        "vvvvv",
        [("v", FINE), ("v", BIG), ("v", BIG), ("v", MID), ("v", MID), ("h", FINE)],
        [*coarse, (3, 16, 8, 128), (3, 16, 8, 128), dma(5)],
    )(s, f, halo, *y_halos)
    rows = (sum(ROWS_ONE), 8, 128)
    fine, own1, to_low, to_high, payload = call(
        down_kernel,
        "down",
        "v" * 7,
        [("v", FINE), ("v", BIG), ("v", BIG), ("v", MID), ("v", MID), ("h", FINE)]
        + [("v", (16, 8, 128)), ("v", rows), ("v", rows), ("h", (32, 16, 128))],
        [*coarse, (4, 16, 128)] + [MID] * 7 + [dma(10), (32, 16, 128), dma(1)],
        [(2 + i, i) for i in range(5)],
    )(z_low, z_high, *inner)[5:]
    y_low, y_high = exchange(to_low, to_high, "gy")
    got = lax.all_to_all(payload, ("gy", "gz"), 0, 0)
    layers = (len(TILES_ONE), 8, 128)
    to_low, to_high, rows = call(
        spread_y_kernel,
        "spread_y",
        "vvv",
        [("v", layers)] * 2 + [("v", (48, 8, 128))],
        [(2, 8, 8, 128)] * 2,
    )(own1, y_low, y_high)
    z_low, z_high = exchange(to_low, to_high, "gz")
    one = call(wide_kernel, "wide", "vvv", [("v", WIDE1)] * 7, [WIDE1] * 2)(rows, z_low, z_high)
    payload, *kept = call(
        middle_kernel,
        "middle",
        "vv",
        [("h", (8, 4, 8, 128))] + [("h", WINDOW)] * 3,
        [MID2] * 4 + [(16, 16, 128), (16, 16, 128)] + [MID2] * 5 + [dma(3), (4, 8, 128), dma(16)],
    )(got, rows)
    got = lax.all_to_all(payload, "gx", 0, 0)
    pressure, residual = call(
        up_kernel,
        "up",
        "v" * 8 + "h" * 5,
        [("h", own)] * 2,
        [WINDOW] * 3
        + [FINE]
        + [dma(18)]
        + [THREE] * 4
        + [FOUR] * 4
        + [THREE] * 5
        + [FOUR] * 5
        + [WINDOW] * 5
        + [(9, 8, 128), (4, 8, 128), (8, 8, 128), (4, 8, 128), (8, 128), (8, 128), WINDOW, WINDOW, (2, 6, 8, 128), (6, 16, 128)]
        + [WIDE1] * 2
        + [(8, 24, 128), (8, 16, 128), (12, 24, 256), (2, 12, 32, 128), BIG, BIG, own, own, dma(4)],
    )(got, *one, *kept, fine_inner, fine)
    return (pressure, residual)


def solution(mesh):
    spec = P("gz", "gy", "gx")
    return jax.shard_map(
        local, mesh=mesh, in_specs=(spec, spec), out_specs=(spec, spec), check_vma=False
    )
```
